256 devices in a mesh: gx: 8 (over z_hi, core), gy: 4 (over y), gz: 8 (over z_lo, x).
Axes of the slice: x: 4, y: 4, z: 8 (z_hi: 4, z_lo: 2; z = z_hi * 2 + z_lo), core: 2. Of those that a mesh axis runs over, the one named last changes fastest.
Arguments:
- volume: bfloat16 [4, 32, 128, 512], P(None, 'gx', 'gz', 'gy'), may hold values from -6 to 6
- first_filters: float32 [32, 108], replicated, may hold values from -0.625 to 0.625
- first_bias: float32 [32], replicated, may hold values from -3 to 3
- second_filters: float32 [64, 864], replicated, may hold values from -0.21875 to 0.21875
- second_bias: float32 [64], replicated, may hold values from -3 to 3
- cotangent: bfloat16 [64, 8, 32, 128], P(None, 'gx', 'gz', 'gy'), may hold values from -6 to 6
Outputs:
- features: bfloat16 [64, 8, 32, 128], P(None, 'gx', 'gz', 'gy')
- stepped_first: float32 [32, 108], replicated
- offset_first: float32 [32], replicated
- stepped_second: float32 [64, 864], replicated
- offset_second: float32 [64], replicated
The draws below stay inside these ranges and needn't reach their ends.
All inputs are finite; a program needn't handle non-finite values.
Results may differ from the reference program's by a relative error of at most 0.0015.
The reference program's roundings to bfloat16 on the way (of `first_half`, `pooled`, `second_error`, `pooled_error` and `first_error`) count: a program that leaves them out, or rounds other values in their place, can miss the bound.
Values may be sent and summed in bfloat16 or wider, within the bound.
A program may use at most 128 MiB of HBM per device.

```python
import jax
import jax.numpy as jnp
from jax import lax

C0 = 4
C1 = 32
C2 = 64
NW = 32
ND = 128
NH = 512


def level_of(rng, extent, split, least, high):
    def one(position, shards_of):
        draws = jax.random.uniform(jax.random.fold_in(jax.random.fold_in(rng, 6), position), (shards_of,), jnp.float32, least / len(split), high / len(split))
        return jnp.repeat(jnp.exp(draws), extent[position] // shards_of).reshape((-1,) + (1,) * (len(extent) - position - 1))

    loudness = one(*split[0])
    for cut in split[1:]:
        loudness = loudness * one(*cut)
    return loudness


def scatter_about(own_key, shape, scale, limit, cuts=(), kind=jnp.bfloat16):
    array = scale * jax.random.normal(own_key, shape, jnp.float32)
    if cuts:
        array = array * level_of(own_key, shape, cuts, -0.22, 0.18)
    return jnp.clip(array, -limit, limit).astype(kind)


def setup_inputs(seed: int = 0) -> dict:
    splits = jax.random.split(jax.random.key(seed), 7)
    return {
        "volume": scatter_about(splits[0], (C0, NW, ND, NH), 1.0, 6.0, ((1, 8), (2, 8), (3, 4))),
        "first_filters": scatter_about(splits[1], (C1, 27 * C0), (27 * C0) ** -0.5, 0.625, (), jnp.float32),
        "first_bias": scatter_about(splits[2], (C1,), 0.5, 3.0, (), jnp.float32),
        "second_filters": scatter_about(splits[3], (C2, 27 * C1), (27 * C1) ** -0.5, 0.21875, (), jnp.float32),
        "second_bias": scatter_about(splits[4], (C2,), 0.5, 3.0, (), jnp.float32),
        "cotangent": scatter_about(splits[5], (C2, NW // 4, ND // 4, NH // 4), 1.0, 6.0, ((1, 8), (2, 8), (3, 4))),
    }


negative_slope = 0.3
learn_rate = 0.001

def leaky_relu(tensor):
    return jnp.where(tensor > 0, tensor, negative_slope * tensor)

def slopes(tensor):
    return jnp.where(tensor > 0, 1.0, negative_slope).astype(tensor.dtype)

def pool_pairs(tensor):
    channels, wide_cells, deep_cells, high_cells = tensor.shape
    blocks = tensor.reshape(channels, wide_cells // 2, 2, deep_cells // 2, 2, high_cells // 2, 2)
    return lax.optimization_barrier(jnp.mean(blocks, axis=(2, 4, 6)))

def spread(tensor):
    channels, wide_cells, deep_cells, high_cells = tensor.shape
    expanded = jnp.broadcast_to(tensor[:, :, None, :, None, :, None], (channels, wide_cells, 2, deep_cells, 2, high_cells, 2))
    return expanded.reshape(channels, 2 * wide_cells, 2 * deep_cells, 2 * high_cells)

def to_kernel(filters, in_channels):
    out_channels = filters.shape[0]
    return filters.reshape(out_channels, 3, 3, 3, in_channels).transpose(0, 4, 1, 2, 3)

def from_kernel(kernel):
    out_channels = kernel.shape[0]
    return kernel.transpose(0, 2, 3, 4, 1).reshape(out_channels, -1)

def convolve(tensor, kernel):
    result = lax.conv_general_dilated(tensor[None], kernel, (1, 1, 1), 'SAME', dimension_numbers=('NCDHW', 'OIDHW', 'NCDHW'), precision=lax.Precision.HIGHEST)
    return result[0]

def reference(volume, first_filters, first_bias, second_filters, second_bias, cotangent):
    first_half = first_filters.astype(jnp.bfloat16).astype(jnp.float32)
    second_half = second_filters.astype(jnp.bfloat16).astype(jnp.float32)
    first_kernel = to_kernel(first_half, volume.shape[0])
    second_kernel = to_kernel(second_half, first_filters.shape[0])
    volume_wide = volume.astype(jnp.float32)
    first_pre = convolve(volume_wide, first_kernel) + first_bias[:, None, None, None]
    pooled = pool_pairs(leaky_relu(first_pre)).astype(jnp.bfloat16)
    pooled_wide = pooled.astype(jnp.float32)
    second_pre = convolve(pooled_wide, second_kernel) + second_bias[:, None, None, None]
    features = pool_pairs(leaky_relu(second_pre)).astype(jnp.bfloat16)
    second_error = (spread(cotangent.astype(jnp.float32)) * 0.125 * slopes(second_pre)).astype(jnp.bfloat16)
    second_wide = second_error.astype(jnp.float32)
    pullback_two = jax.vjp(convolve, pooled_wide, second_kernel)[1]
    pooled_error, second_kgrad = pullback_two(second_wide)
    pooled_error = pooled_error.astype(jnp.bfloat16)
    second_grad = from_kernel(second_kgrad)
    second_bias_grad = lax.optimization_barrier(jnp.sum(second_wide, axis=(1, 2, 3)))
    first_error = (spread(pooled_error.astype(jnp.float32)) * 0.125 * slopes(first_pre)).astype(jnp.bfloat16)
    first_wide = first_error.astype(jnp.float32)
    pullback_one = jax.vjp(lambda kernel: convolve(volume_wide, kernel), first_kernel)[1]
    first_grad = from_kernel(pullback_one(first_wide)[0])
    first_bias_grad = lax.optimization_barrier(jnp.sum(first_wide, axis=(1, 2, 3)))
    return (features, first_filters - learn_rate * first_grad, first_bias - learn_rate * first_bias_grad, second_filters - learn_rate * second_grad, second_bias - learn_rate * second_bias_grad)
```

```python
import functools

import jax
import jax.numpy as jnp
import numpy as np
from jax import lax
from jax.experimental import pallas as pl
from jax.experimental.pallas import tpu as pltpu
from jax.sharding import PartitionSpec as P

slope_below = 0.3
learn_rate = 0.001
f32 = jnp.float32
bf16 = jnp.bfloat16
MESH = pl.DeviceIdType.MESH
NN = (((1,), (0,)), ((), ()))
NT = (((1,), (1,)), ((), ()))
TN = (((0,), (0,)), ((), ()))


def mm(a, b, dims=NN):
    return lax.dot_general(a, b, dims, preferred_element_type=f32)


def tables():
    edge = np.zeros((32, 256))
    for r in range(16):
        edge[r, r * 16] = 1
        edge[16 + r, r * 16 + 15] = 1
    place = np.zeros((512, 480))
    for wp in range(6):
        for dp in range(18):
            for ch in range(4):
                w, d = wp - 1, dp - 1
                inner_w, inner_d = 0 <= w < 4, 0 <= d < 16
                if inner_w and inner_d:
                    src = (ch * 4 + w) * 16 + d
                elif inner_d:
                    src = 256 + (64 if w > 0 else 0) + ch * 16 + d
                elif inner_w:
                    src = 384 + (16 if d > 0 else 0) + ch * 4 + w
                else:
                    a, b = int(w > 0), int(d > 0)
                    src = 416 + (a * 2 + b) * 16 + ch * 4 + (0 if a else 3)
                place[(wp * 18 + dp) * 4 + ch, src] = 1
    shift1 = np.zeros((128, 384))
    for l in range(128):
        if l:
            shift1[l - 1, l] = 1
        shift1[l, 128 + l] = 1
        if l < 127:
            shift1[l + 1, 256 + l] = 1
    pick1 = np.zeros((16, 128))
    pick1[0, 0] = pick1[1, 127] = 1
    put1 = np.zeros((32, 384))
    put1[1, 0] = 1
    put1[16, 256 + 127] = 1
    shift2 = np.zeros((128, 384))
    swapped = np.zeros((128, 384))
    for l in range(128):
        for k in range(3):
            s = l % 64 + k - 1
            if 0 <= s < 64:
                s += l - l % 64
                shift2[s, k * 128 + l] = 1
                swapped[(s + 64) % 128, k * 128 + l] = 1
    pick2 = np.zeros((16, 128))
    pick2s = np.zeros((16, 128))
    for r, l in enumerate((0, 63, 64, 127)):
        pick2[r, l] = 1
        pick2s[r, (l + 64) % 128] = 1
    put2 = np.zeros((32, 384))
    put2[1, 0] = put2[3, 64] = 1
    put2[16, 256 + 63] = put2[18, 256 + 127] = 1
    even = np.zeros((256, 128))
    for half in range(2):
        for h in range(64):
            even[half * 128 + 2 * h, half * 64 + h] = 1
    twice = np.zeros((128, 256))
    for half in range(2):
        for h in range(128):
            twice[half * 64 + h // 2, half * 128 + h] = 1
    spread = np.zeros((128, 256))
    gather = np.zeros((256, 128))
    for dc in range(4):
        for hc in range(32):
            for t in range(2):
                spread[dc * 32 + hc, (dc % 2) * 128 + (dc // 2) * 64 + 2 * hc + t] = 1
            gather[(dc % 2) * 128 + (dc // 2) * 64 + 2 * hc, dc * 32 + hc] = 1
    widen = np.zeros((108, 144))
    for q in range(108):
        widen[q, (q // 12) * 16 + q % 12] = 1
    ident = np.zeros((64, 256))
    for o in range(64):
        ident[o, o] = ident[o, 128 + 64 + o] = 1
    every = dict(
        edge=edge, place=place, shift1=shift1, pick1=pick1, put1=put1, shift2=shift2, swapped=swapped,
        pick2=pick2, pick2s=pick2s, put2=put2, even=even, twice=twice, spread=spread, gather=gather,
        widen=widen, narrow=widen.T, ident=ident,
    )
    return {name: value.astype(jnp.bfloat16) for name, value in every.items()}


def row_to_column(row):
    n = row.shape[1]
    diagonal = lax.broadcasted_iota(jnp.int32, (n, n), 0) == lax.broadcasted_iota(jnp.int32, (n, n), 1)
    return jnp.sum(jnp.where(diagonal, jnp.broadcast_to(row, (n, n)), 0.0), axis=1, keepdims=True)


def column_to_row(column):
    n = column.shape[0]
    diagonal = lax.broadcasted_iota(jnp.int32, (n, n), 0) == lax.broadcasted_iota(jnp.int32, (n, n), 1)
    return jnp.sum(jnp.where(diagonal, jnp.broadcast_to(column, (n, n)), 0.0), axis=0, keepdims=True)


def kept(flag, value):
    return lax.select(flag, value, jnp.zeros_like(value))


def leaky(a):
    return jnp.where(a > 0, a, slope_below * a)


def slope(a):
    return jnp.where(a > 0, 1.0, slope_below)


def split3(a):
    high = a.astype(bf16)
    rest = a - high.astype(f32)
    mid = rest.astype(bf16)
    return high, mid, (rest - mid.astype(f32)).astype(bf16)


TABLE_NAMES = (
    "edge", "place", "shift1", "pick1", "put1", "shift2", "swapped", "pick2", "pick2s", "put2",
    "even", "twice", "spread", "gather", "widen", "narrow", "ident",
)


def kernel(sizes, *refs):
    GX, GY, GZ, NX = sizes
    ZL = GZ // NX
    ZH = GX // 2
    NZ = ZH * ZL
    vol, filt1, bias1, filt2, bias2, cot = refs[:6]
    t = dict(zip(TABLE_NAMES, refs[6:6 + len(TABLE_NAMES)]))
    refs = refs[6 + len(TABLE_NAMES):]
    feat, step1, off1, step2, off2 = refs[:5]
    (
        edges, wide_in, deep_in, corner_in, col1, col1_in, xs, pre1, summed,
        pooled, wide2, deep2, corner2, v2, col2, col2_in, ys,
        errs, wide3, deep3, corner3, v3, col3, col3_in, fs, turned, perr,
        grads, core_in, red1, x_in, red2, y_in, red3, z_in, total, send_sems, recv_sems,
    ) = refs[5:]

    gx, gy, gz = lax.axis_index("gx"), lax.axis_index("gy"), lax.axis_index("gz")
    core, zh = lax.rem(gx, 2), lax.div(gx, 2)
    xc, zl = lax.rem(gz, NX), lax.div(gz, NX)
    zc = zh * ZL + zl

    def shifted(dx, dy, dz):
        return (lax.rem(gx + (dx + GX), GX), lax.rem(gy + (dy + GY), GY), lax.rem(gz + (dz + GZ), GZ))

    sibling = (gx + 1 - 2 * core, gy, gz)

    def x_peer(r):
        p = lax.rem(xc + r, NX)
        return p, (gx, gy, zl * NX + p)

    def y_peer(r):
        p = lax.rem(gy + r, GY)
        return p, (gx, p, gz)

    def z_peer(r):
        p = lax.rem(zc + r, NZ)
        return (2 * lax.div(p, ZL) + core, gy, lax.rem(p, ZL) * NX + xc)

    ring = [(dx, dz) for dx in (-1, 0, 1) for dz in (-1, 0, 1) if (dx, dz) != (0, 0)]
    peers = [shifted(dx, 0, dz) for dx, dz in ring]
    peers += [shifted(0, -1, 0), shifted(0, 1, 0), sibling]
    peers += [x_peer(r)[1] for r in range(1, NX)]
    peers += [y_peer(r)[1] for r in range(1, GY)]
    peers += [z_peer(r) for r in range(1, NZ)]
    barrier = pltpu.get_barrier_semaphore()
    for peer in peers:
        pl.semaphore_signal(barrier, inc=1, device_id=peer, device_id_type=MESH)

    count = [0]
    started = []

    def send(src, dst, device):
        n = count[0]
        count[0] += 1
        copy = pltpu.make_async_remote_copy(
            src_ref=src, dst_ref=dst, send_sem=send_sems.at[n], recv_sem=recv_sems.at[n],
            device_id=device, device_id_type=MESH,
        )
        copy.start()
        started.append(copy)
        return copy

    def arrive(copies):
        for copy in copies:
            copy.wait_recv()

    block = vol[...].reshape(256, 128)
    edges[...] = mm(t["edge"][...], block).astype(bf16)
    first_half = filt1[...].astype(bf16)
    wide_first = mm(first_half, t["widen"][...]).astype(bf16)
    bias1_col = row_to_column(bias1[...])
    bias2_col = row_to_column(bias2[...])
    second_half = filt2[...].astype(bf16)

    pl.semaphore_wait(barrier, len(peers))

    has_left, has_right = gx > 0, gx < GX - 1
    has_front, has_back = gz > 0, gz < GZ - 1
    has_below, has_above = gy > 0, gy < GY - 1

    def send_ring(wide_src, wide_dst, deep_src, deep_dst, corner_src, corner_dst):
        copies = []
        for a in range(2):
            dx = 1 if a == 0 else -1
            copies.append(send(wide_src(a), wide_dst.at[a], shifted(dx, 0, 0)))
        for b in range(2):
            dz = 1 if b == 0 else -1
            copies.append(send(deep_src(b), deep_dst.at[b], shifted(0, 0, dz)))
        for a in range(2):
            for b in range(2):
                copies.append(
                    send(corner_src(a, b), corner_dst.at[a * 2 + b], shifted(1 if a == 0 else -1, 0, 1 if b == 0 else -1))
                )
        return copies

    def send_columns(src, dst):
        return [send(src, dst.at[0], shifted(0, 1, 0)), send(src, dst.at[1], shifted(0, -1, 0))]

    def columns_in(dst):
        return jnp.concatenate([kept(has_below, dst[0]), kept(has_above, dst[1])], axis=0)

    def edge_rows(b):
        return edges.at[pl.ds(16, 16)] if b == 0 else edges.at[pl.ds(0, 16)]

    copies = send_ring(
        lambda a: vol.at[:, 3] if a == 0 else vol.at[:, 0], wide_in,
        edge_rows, deep_in, lambda a, b: edge_rows(b), corner_in,
    )

    turn = mm(second_half, t["ident"][...], TN).astype(bf16)
    for m in range(13):
        low = turn[64 * m:64 * m + 32, :128].astype(f32)
        high = turn[64 * m + 32:64 * m + 64, 128:].astype(f32)
        turned[:, 128 * m:128 * m + 128] = (low + high).astype(bf16)
    turned[:, 1664:1792] = turn[832:864, :128]
    spread_cot = mm(cot[...], t["spread"][...]) * 0.125

    arrive(copies)
    edge_flags = (has_left, has_right)
    deep_flags = (has_front, has_back)
    pieces = [block]
    for a in range(2):
        pieces.append(kept(edge_flags[a], wide_in[a]).reshape(64, 128))
    for b in range(2):
        pieces.append(kept(deep_flags[b], deep_in[b]))
    for a in range(2):
        for b in range(2):
            pieces.append(kept(jnp.logical_and(edge_flags[a], deep_flags[b]), corner_in[a * 2 + b]))
    rows = mm(t["place"][...], jnp.concatenate(pieces, axis=0)).astype(bf16)
    col1[...] = mm(t["pick1"][...], rows, NT).astype(bf16)
    copies = send_columns(col1, col1_in)
    inner = mm(rows, t["shift1"][...])
    arrive(copies)
    full = inner + mm(columns_in(col1_in), t["put1"][...], TN)
    third = [full[:, 128 * k:128 * k + 128].reshape(64, 8, 128) for k in range(3)]
    rolled = [pltpu.roll(piece, 4, axis=1) for piece in third]
    sub = lax.broadcasted_iota(jnp.int32, (64, 8, 128), 1)
    upper = sub < 4
    ones = jnp.where(sub == 4, 1.0, 0.0)
    even_tile = jnp.concatenate(
        [jnp.where(upper, third[0], rolled[1]), jnp.where(upper, third[2], ones)], axis=1
    )
    odd_tile = jnp.concatenate(
        [jnp.where(upper, rolled[0], third[1]), jnp.where(upper, rolled[2], ones)], axis=1
    )
    xs[:, 0] = even_tile.astype(bf16)
    xs[:, 1] = odd_tile.astype(bf16)

    def cols1(w, half_d):
        def at(i, dp, parity):
            return xs[(w + i) * 9 + dp, parity]

        one = [at(i, half_d + j // 2, j % 2) for i in range(3) for j in range(3)]
        two = [at(i, half_d + (j + 1) // 2, (j + 1) % 2) for i in range(3) for j in range(3)]
        return jnp.concatenate(
            [jnp.concatenate(one, axis=0), jnp.concatenate(two, axis=0)], axis=1
        )

    def forward1(pd, carry):
        for pw in range(2):
            part = None
            for w in (2 * pw, 2 * pw + 1):
                pre = mm(wide_first, cols1(w, pd)) + bias1_col
                pre1[w, pd] = pre
                act = leaky(pre)
                act = act[:, :128] + act[:, 128:]
                part = act if part is None else part + act
            part = (part + pltpu.roll(part, 127, axis=1)) * 0.125
            summed[pw, pd] = part.astype(bf16)
        return carry

    lax.fori_loop(0, 8, forward1, 0)
    pooled_val = (
        mm(summed[:, 0:4].reshape(256, 128), t["even"][0:128])
        + mm(summed[:, 4:8].reshape(256, 128), t["even"][128:256])
    ).astype(bf16)
    pooled[...] = pooled_val.reshape(2, 4, 32, 128)

    def assemble(own, wide, deep, corner, v, n):
        left = [kept(edge_flags[a], wide[a]) for a in range(2)]
        v[0:4] = left[0]
        v[4:8] = own[0]
        v[8:12] = own[1]
        v[12:16] = left[1]
        low = lax.broadcasted_iota(jnp.int32, (n, 128), 1) < 64
        for wp in range(4):
            if wp == 0 or wp == 3:
                a = 0 if wp == 0 else 1
                near = left[a]
                far = [
                    kept(jnp.logical_and(edge_flags[a], deep_flags[b]), corner[a * 2 + b]) for b in range(2)
                ]
            else:
                near = own[wp - 1]
                far = [kept(deep_flags[b], deep[b, wp - 1]) for b in range(2)]
            v[16 + wp] = jnp.where(low, near[3].astype(f32), far[0].astype(f32)).astype(bf16)
            v[20 + wp] = jnp.where(low, far[1].astype(f32), near[0].astype(f32)).astype(bf16)

    def halo(own, wide, deep, corner, v, col, col_in, out, n, flipped, meanwhile):
        copies = send_ring(
            lambda a: own.at[1 - a], wide,
            lambda b: own.at[:, 3 if b == 0 else 0], deep,
            lambda a, b: own.at[1 - a, 3 if b == 0 else 0], corner,
        )
        result = meanwhile()
        arrive(copies)
        assemble(own, wide, deep, corner, v, n)
        main = v[0:16].reshape(16 * n, 128)
        side = v[16:24].reshape(8 * n, 128)
        col[:, 0:16 * n] = mm(t["pick2"][...], main, NT).astype(bf16)
        col[:, 16 * n:24 * n] = mm(t["pick2s"][...], side, NT).astype(bf16)
        copies = send_columns(col, col_in)
        inner = jnp.concatenate([mm(main, t["shift2"][...]), mm(side, t["swapped"][...])], axis=0)
        arrive(copies)
        full = inner + mm(columns_in(col_in), t["put2"][...], TN)
        for k in range(3):
            place = 2 - k if flipped else k
            piece = full[:, 128 * k:128 * k + 128].astype(bf16).reshape(24, n, 128)
            out[:, place * n:place * n + n, :] = piece
        return result

    def tile(wp, dp):
        if dp == 0:
            return 16 + wp
        if dp == 5:
            return 20 + wp
        return wp * 4 + dp - 1

    halo(pooled, wide2, deep2, corner2, v2, col2, col2_in, ys, 32, False, lambda: None)

    def cols2(w, dq, extra):
        taps = [ys[tile(w + i, dq + j)] for i in range(3) for j in range(3)]
        return jnp.concatenate(taps + extra, axis=0)

    feat_sum = [None, None]
    for dq in range(4):
        cols = jnp.concatenate([cols2(0, dq, []), cols2(1, dq, [])], axis=1)
        pre = mm(second_half, cols) + bias2_col
        act = leaky(pre)
        act = act[:, :128] + act[:, 128:]
        pair = dq // 2
        feat_sum[pair] = act if feat_sum[pair] is None else feat_sum[pair] + act
        cot_here = spread_cot[:, 128 * pair:128 * pair + 128]
        err = (jnp.concatenate([cot_here, cot_here], axis=1) * slope(pre)).astype(bf16)
        errs[0, dq] = err[:, :128]
        errs[1, dq] = err[:, 128:]

    def second_half_grads():
        ends = [
            ((part + pltpu.roll(part, 127, axis=1)) * 0.125).astype(bf16) for part in feat_sum
        ]
        feat[...] = (mm(ends[0], t["gather"][0:128]) + mm(ends[1], t["gather"][128:256])).astype(bf16)
        ones_rows = [jnp.ones((32, 128), bf16)]
        grad2 = None
        for dq in range(4):
            cols = jnp.concatenate([cols2(0, dq, ones_rows), cols2(1, dq, ones_rows)], axis=1)
            err = jnp.concatenate([errs[0, dq], errs[1, dq]], axis=1)
            part = mm(err, cols, NT)
            grad2 = part if grad2 is None else grad2 + part
        for l in range(7):
            grads[l * 64:l * 64 + 64] = grad2[:, 128 * l:128 * l + 128]

    halo(errs, wide3, deep3, corner3, v3, col3, col3_in, fs, 64, True, second_half_grads)

    for dq in range(4):
        def cols3(w):
            taps = [fs[tile(w + 2 - i, dq + 2 - j)] for i in range(3) for j in range(3)]
            return jnp.concatenate(taps + [jnp.zeros((64, 128), bf16)], axis=0)

        cols = jnp.concatenate([cols3(0), cols3(1)], axis=1)
        pe = mm(turned[...], cols).astype(bf16)
        both = mm(jnp.concatenate([pe[:, :128], pe[:, 128:]], axis=0), t["twice"][...]) * 0.125
        for w in range(2):
            perr[w, dq] = both[32 * w:32 * w + 32, :128]
            perr[w, dq + 4] = both[32 * w:32 * w + 32, 128:]

    def backward1(pd, acc):
        for w in range(4):
            here = perr[w // 2, pd]
            err = (jnp.concatenate([here, here], axis=1) * slope(pre1[w, pd])).astype(bf16)
            acc = acc + mm(err, cols1(w, pd), NT)
        return acc

    grad1 = lax.fori_loop(0, 8, backward1, jnp.zeros((32, 144), f32))
    grads[448:480] = grad1[:, :128]
    grads[480:512] = jnp.concatenate([grad1[:, 128:144], jnp.zeros((32, 112), f32)], axis=1)

    def part(ref, index, size):
        return ref.at[pl.ds(pl.multiple_of(index * size, size), size)]

    n1, n2, n3 = 256, 256 // NX, 256 // NX // GY
    copy = send(part(grads, 1 - core, n1), core_in, sibling)
    copy.wait_recv()
    red1[...] = part(grads, core, n1)[...] + core_in[...]
    copies = [send(part(red1, x_peer(r)[0], n2), x_in.at[r - 1], x_peer(r)[1]) for r in range(1, NX)]
    arrive(copies)
    acc = part(red1, xc, n2)[...]
    for r in range(1, NX):
        acc = acc + x_in[r - 1]
    red2[...] = acc
    copies = [send(part(red2, y_peer(r)[0], n3), y_in.at[r - 1], y_peer(r)[1]) for r in range(1, GY)]
    arrive(copies)
    acc = part(red2, gy, n3)[...]
    for r in range(1, GY):
        acc = acc + y_in[r - 1]
    red3[...] = acc
    z_in[zc] = acc
    copies = [send(red3, z_in.at[zc], z_peer(r)) for r in range(1, NZ)]
    arrive(copies)
    acc = z_in[0]
    for r in range(1, NZ):
        acc = acc + z_in[r]
    mine = part(total, (core * NX + xc) * GY + gy, n3)
    mine[...] = acc
    copies = [send(mine, mine, y_peer(r)[1]) for r in range(1, GY)]
    arrive(copies)
    mine = part(total, core * NX + xc, n2)
    copies = [send(mine, mine, x_peer(r)[1]) for r in range(1, NX)]
    arrive(copies)
    mine = part(total, core, n1)
    copy = send(mine, mine, sibling)
    copy.wait_recv()

    sums2 = jnp.concatenate([total[l * 64:l * 64 + 64] for l in range(7)], axis=1)
    step2[...] = filt2[...] - learn_rate * sums2[:, :864]
    off2[...] = bias2[...] - learn_rate * column_to_row(sums2[:, 864:865])
    sums1 = jnp.concatenate([total[448:480], total[480:512]], axis=1)[:, :144]
    narrow = sum(mm(piece, t["narrow"][...]) for piece in split3(sums1))
    step1[...] = filt1[...] - learn_rate * narrow
    off1[...] = bias1[...] - learn_rate * column_to_row(sums1[:, 12:13])

    for copy in started:
        copy.wait_send()


def shards(volume, first_filters, first_bias, second_filters, second_bias, cotangent):
    GX, GY, GZ = lax.axis_size("gx"), lax.axis_size("gy"), lax.axis_size("gz")
    NX = 4 if GZ >= 8 else 2
    NZ = (GX // 2) * (GZ // NX)
    n2, n3 = 256 // NX, 256 // NX // GY
    table = tables()
    operands = [
        volume, first_filters, first_bias.reshape(1, 32), second_filters, second_bias.reshape(1, 64),
        cotangent.reshape(64, 128),
    ] + [jnp.asarray(table[name]) for name in TABLE_NAMES]
    sems = 30 + 1 + 2 * (NX - 1) + 2 * (GY - 1) + (NZ - 1) + 1
    V = pltpu.VMEM
    out = pl.pallas_call(
        functools.partial(kernel, (GX, GY, GZ, NX)),
        out_shape=(
            jax.ShapeDtypeStruct((64, 128), bf16),
            jax.ShapeDtypeStruct((32, 108), f32),
            jax.ShapeDtypeStruct((1, 32), f32),
            jax.ShapeDtypeStruct((64, 864), f32),
            jax.ShapeDtypeStruct((1, 64), f32),
        ),
        in_specs=[pl.BlockSpec(memory_space=pltpu.VMEM)] * len(operands),
        out_specs=[pl.BlockSpec(memory_space=pltpu.VMEM)] * 5,
        scratch_shapes=[
            V((32, 128), bf16), V((2, 4, 16, 128), bf16), V((2, 16, 128), bf16), V((4, 16, 128), bf16),
            V((16, 512), bf16), V((2, 16, 512), bf16), V((64, 2, 16, 128), bf16), V((4, 8, 32, 256), f32),
            V((2, 8, 32, 128), bf16),
            V((2, 4, 32, 128), bf16), V((2, 4, 32, 128), bf16), V((2, 2, 32, 128), bf16), V((4, 32, 128), bf16),
            V((24, 32, 128), bf16), V((16, 768), bf16), V((2, 16, 768), bf16), V((24, 96, 128), bf16),
            V((2, 4, 64, 128), bf16), V((2, 4, 64, 128), bf16), V((2, 2, 64, 128), bf16), V((4, 64, 128), bf16),
            V((24, 64, 128), bf16), V((16, 1536), bf16), V((2, 16, 1536), bf16), V((24, 192, 128), bf16),
            V((32, 1792), bf16), V((2, 8, 32, 128), f32),
            V((512, 128), f32), V((256, 128), f32), V((256, 128), f32), V((NX - 1, n2, 128), f32),
            V((n2, 128), f32), V((GY - 1, n3, 128), f32), V((n3, 128), f32), V((NZ, n3, 128), f32),
            V((512, 128), f32),
            pltpu.SemaphoreType.DMA((sems,)), pltpu.SemaphoreType.DMA((sems,)),
        ],
        compiler_params=pltpu.CompilerParams(
            collective_id=0, has_side_effects=True, vmem_limit_bytes=48 * 2**20
        ),
    )(*operands)
    features, stepped_first, offset_first, stepped_second, offset_second = out
    return (
        features.reshape(64, 1, 4, 32), stepped_first, offset_first.reshape(32), stepped_second,
        offset_second.reshape(64),
    )


def solution(mesh):
    return jax.shard_map(
        shards,
        mesh=mesh,
        in_specs=(P(None, "gx", "gz", "gy"), P(), P(), P(), P(), P(None, "gx", "gz", "gy")),
        out_specs=(P(None, "gx", "gz", "gy"), P(), P(), P(), P()),
        check_vma=False,
    )
```

```python
import functools

import jax
import jax.numpy as jnp
import numpy as np
from jax import lax
from jax.experimental import pallas as pl
from jax.experimental.pallas import tpu as pltpu
from jax.sharding import PartitionSpec as P

slope_below = 0.3
learn_rate = 0.001
f32 = jnp.float32
bf16 = jnp.bfloat16
MESH = pl.DeviceIdType.MESH
NN = (((1,), (0,)), ((), ()))
NT = (((1,), (1,)), ((), ()))
TN = (((0,), (0,)), ((), ()))


def mm(a, b, dims=NN):
    return lax.dot_general(a, b, dims, preferred_element_type=f32)


def tables():
    place = np.zeros((512, 480))
    for wp in range(6):
        for dp in range(18):
            for ch in range(4):
                w, d = wp - 1, dp - 1
                inner_w, inner_d = 0 <= w < 4, 0 <= d < 16
                if inner_w and inner_d:
                    src = (ch * 4 + w) * 16 + d
                elif inner_d:
                    src = 256 + (64 if w > 0 else 0) + ch * 16 + d
                elif inner_w:
                    src = 384 + (16 if d > 0 else 0) + ch * 4 + w
                else:
                    a, b = int(w > 0), int(d > 0)
                    src = 416 + (a * 2 + b) * 16 + ch * 4 + (0 if a else 3)
                place[(wp * 18 + dp) * 4 + ch, src] = 1
    shift1 = np.zeros((128, 384))
    for l in range(128):
        if l:
            shift1[l - 1, l] = 1
        shift1[l, 128 + l] = 1
        if l < 127:
            shift1[l + 1, 256 + l] = 1
    pick1 = np.zeros((16, 128))
    pick1[0, 0] = pick1[1, 127] = 1
    put1 = np.zeros((32, 384))
    put1[1, 0] = 1
    put1[16, 256 + 127] = 1
    shift2 = np.zeros((128, 384))
    swapped = np.zeros((128, 384))
    for l in range(128):
        for k in range(3):
            s = l % 64 + k - 1
            if 0 <= s < 64:
                s += l - l % 64
                shift2[s, k * 128 + l] = 1
                swapped[(s + 64) % 128, k * 128 + l] = 1
    pick2 = np.zeros((16, 128))
    pick2s = np.zeros((16, 128))
    for r, l in enumerate((0, 63, 64, 127)):
        pick2[r, l] = 1
        pick2s[r, (l + 64) % 128] = 1
    put2 = np.zeros((32, 384))
    put2[1, 0] = put2[3, 64] = 1
    put2[16, 256 + 63] = put2[18, 256 + 127] = 1
    even = np.zeros((256, 128))
    for half in range(2):
        for h in range(64):
            even[half * 128 + 2 * h, half * 64 + h] = 1
    twice = np.zeros((128, 256))
    for half in range(2):
        for h in range(128):
            twice[half * 64 + h // 2, half * 128 + h] = 1
    spread = np.zeros((128, 256))
    collect = np.zeros((256, 128))
    for dc in range(4):
        for hc in range(32):
            for t in range(2):
                spread[dc * 32 + hc, (dc % 2) * 128 + (dc // 2) * 64 + 2 * hc + t] = 1
            collect[(dc % 2) * 128 + dc * 32 + hc, (dc // 2) * 64 + 2 * hc] = 1
    widen = np.zeros((108, 144))
    narrow = np.zeros((144, 128))
    for q in range(108):
        widen[q, (q // 12) * 16 + q % 12] = 1
        narrow[(q // 12) * 16 + q % 12, q] = 1
    narrow[12, 108] = 1
    ident = np.zeros((64, 256))
    for o in range(64):
        ident[o, o] = ident[o, 128 + 64 + o] = 1
    every = dict(
        place=place, shift1=shift1, pick1=pick1, put1=put1, shift2=shift2, swapped=swapped,
        pick2=pick2, pick2s=pick2s, put2=put2, even=even, twice=twice, spread=spread, collect=collect,
        widen=widen, narrow=narrow, ident=ident,
    )
    return every


TABLE = {}


def packed_table():
    parts, row = [], 0
    for name, value in tables().items():
        rows, lanes = value.shape
        wide = np.zeros((-(-rows // 16) * 16, 512))
        wide[:rows, :lanes] = value
        TABLE[name] = (row, rows, lanes)
        row += wide.shape[0]
        parts.append(wide)
    return np.concatenate(parts).astype(jnp.bfloat16)


PACKED = packed_table()


class Rows:
    def __init__(self, ref, name):
        self.ref = ref
        self.row, self.rows, self.lanes = TABLE[name]

    def __getitem__(self, key):
        if key is Ellipsis:
            return self.ref[self.row:self.row + self.rows, :self.lanes]
        return self.ref[self.row + key.start:self.row + key.stop, :self.lanes]


def row_to_column(row):
    n = row.shape[1]
    diagonal = lax.broadcasted_iota(jnp.int32, (n, n), 0) == lax.broadcasted_iota(jnp.int32, (n, n), 1)
    return jnp.sum(jnp.where(diagonal, jnp.broadcast_to(row, (n, n)), 0.0), axis=1, keepdims=True)


def column_to_row(column):
    n = column.shape[0]
    diagonal = lax.broadcasted_iota(jnp.int32, (n, n), 0) == lax.broadcasted_iota(jnp.int32, (n, n), 1)
    return jnp.sum(jnp.where(diagonal, jnp.broadcast_to(column, (n, n)), 0.0), axis=0, keepdims=True)


def kept(flag, value):
    return lax.select(flag, value, jnp.zeros_like(value))


def leaky(a):
    return jnp.where(a > 0, a, slope_below * a)


def slope(a):
    return jnp.where(a > 0, 1.0, slope_below)


def split3(a):
    high = a.astype(bf16)
    rest = a - high.astype(f32)
    mid = rest.astype(bf16)
    return high, mid, (rest - mid.astype(f32)).astype(bf16)


def kernel(sizes, *refs):
    GX, GY, GZ, NX = sizes
    ZL = GZ // NX
    ZH = GX // 2
    NZ = ZH * ZL
    far = refs[:7]
    refs = refs[7:]
    far_out = refs[:5]
    (
        edges, wide_in, deep_in, corner_in, col1, col1_in, xs, pre1, summed,
        pooled, wide2, deep2, corner2, v2, col2, col2_in, ys,
        errs, wide3, deep3, corner3, v3, col3, col3_in, fs, turned, perr,
        grads, core_in, red1, x_in, red2, y_in, red3, z_in, total,
        one, one_core, one_x, one_y, one_z, one_total, send_sems, recv_sems, vol, filt1, bias1, filt2, bias2, cot, packed, in_sems,
        feat, step1, off1, step2, off2, out_sems,
    ) = refs[5:]
    near = (vol, filt1, bias1, filt2, bias2, cot, packed)
    fetches = [pltpu.make_async_copy(a, b, in_sems.at[n]) for n, (a, b) in enumerate(zip(far, near))]
    for fetch in fetches:
        fetch.start()
    t = {name: Rows(packed, name) for name in TABLE}

    gx, gy, gz = lax.axis_index("gx"), lax.axis_index("gy"), lax.axis_index("gz")
    core, zh = lax.rem(gx, 2), lax.div(gx, 2)
    xc, zl = lax.rem(gz, NX), lax.div(gz, NX)
    zc = zh * ZL + zl

    def shifted(dx, dy, dz):
        return (lax.rem(gx + (dx + GX), GX), lax.rem(gy + (dy + GY), GY), lax.rem(gz + (dz + GZ), GZ))

    sibling = (gx + 1 - 2 * core, gy, gz)

    def x_peer(r):
        p = lax.rem(xc + r, NX)
        return p, (gx, gy, zl * NX + p)

    def y_peer(r):
        p = lax.rem(gy + r, GY)
        return p, (gx, p, gz)

    def z_peer(r):
        p = lax.rem(zc + r, NZ)
        return (2 * lax.div(p, ZL) + core, gy, lax.rem(p, ZL) * NX + xc)

    ring = [(dx, dz) for dx in (-1, 0, 1) for dz in (-1, 0, 1) if (dx, dz) != (0, 0)]
    peers = [shifted(dx, 0, dz) for dx, dz in ring]
    peers += [shifted(0, -1, 0), shifted(0, 1, 0), sibling]
    peers += [x_peer(r)[1] for r in range(1, NX)]
    peers += [y_peer(r)[1] for r in range(1, GY)]
    peers += [z_peer(r) for r in range(1, NZ)]
    barrier = pltpu.get_barrier_semaphore()
    for peer in peers:
        pl.semaphore_signal(barrier, inc=1, device_id=peer, device_id_type=MESH)

    count = [0]
    started = []

    def send(src, dst, device):
        n = count[0]
        count[0] += 1
        copy = pltpu.make_async_remote_copy(
            src_ref=src, dst_ref=dst, send_sem=send_sems.at[n], recv_sem=recv_sems.at[n],
            device_id=device, device_id_type=MESH,
        )
        copy.start()
        started.append(copy)
        return copy

    def put_out(n):
        copy = pltpu.make_async_copy((feat, step1, off1, step2, off2)[n], far_out[n], out_sems.at[n])
        copy.start()
        return copy

    def arrive(copies):
        for copy in copies:
            copy.wait_recv()

    row = lax.broadcasted_iota(jnp.int32, (32, 256), 0)
    column = lax.broadcasted_iota(jnp.int32, (32, 256), 1)
    wanted = jnp.where(row < 16, row * 16, row * 16 - 241)
    edge = jnp.where(column == wanted, 1.0, 0.0).astype(bf16)
    fetches[0].wait()
    block = vol[...].reshape(256, 128)
    edges[...] = mm(edge, block).astype(bf16)
    pl.semaphore_wait(barrier, len(peers))

    has_left, has_right = gx > 0, gx < GX - 1
    has_front, has_back = gz > 0, gz < GZ - 1
    has_below, has_above = gy > 0, gy < GY - 1

    def send_ring(wide_src, wide_dst, deep_src, deep_dst, corner_src, corner_dst):
        copies = []
        for a in range(2):
            dx = 1 if a == 0 else -1
            copies.append(send(wide_src(a), wide_dst.at[a], shifted(dx, 0, 0)))
        for b in range(2):
            dz = 1 if b == 0 else -1
            copies.append(send(deep_src(b), deep_dst.at[b], shifted(0, 0, dz)))
        for a in range(2):
            for b in range(2):
                copies.append(
                    send(corner_src(a, b), corner_dst.at[a * 2 + b], shifted(1 if a == 0 else -1, 0, 1 if b == 0 else -1))
                )
        return copies

    def send_columns(src, dst):
        return [send(src, dst.at[0], shifted(0, 1, 0)), send(src, dst.at[1], shifted(0, -1, 0))]

    def columns_in(dst):
        return jnp.concatenate([kept(has_below, dst[0]), kept(has_above, dst[1])], axis=0)

    def edge_rows(b):
        return edges.at[pl.ds(16, 16)] if b == 0 else edges.at[pl.ds(0, 16)]

    copies = send_ring(
        lambda a: vol.at[:, 3] if a == 0 else vol.at[:, 0], wide_in,
        edge_rows, deep_in, lambda a, b: edge_rows(b), corner_in,
    )

    for fetch in fetches[1:]:
        fetch.wait()
    first_half = filt1[...].astype(bf16)
    wide_first = mm(first_half, t["widen"][...]).astype(bf16)
    bias1_col = row_to_column(bias1[...])
    bias2_col = row_to_column(bias2[...])
    second_half = filt2[...].astype(bf16)

    turn = mm(second_half, t["ident"][...], TN).astype(bf16)
    for m in range(13):
        low = turn[64 * m:64 * m + 32, :128].astype(f32)
        high = turn[64 * m + 32:64 * m + 64, 128:].astype(f32)
        turned[:, 128 * m:128 * m + 128] = (low + high).astype(bf16)
    turned[:, 1664:1792] = turn[832:864, :128]
    spread_cot = mm(cot[...], t["spread"][...], TN) * 0.125

    arrive(copies)
    edge_flags = (has_left, has_right)
    deep_flags = (has_front, has_back)
    pieces = [block]
    for a in range(2):
        pieces.append(kept(edge_flags[a], wide_in[a]).reshape(64, 128))
    for b in range(2):
        pieces.append(kept(deep_flags[b], deep_in[b]))
    for a in range(2):
        for b in range(2):
            pieces.append(kept(jnp.logical_and(edge_flags[a], deep_flags[b]), corner_in[a * 2 + b]))
    rows = mm(t["place"][...], jnp.concatenate(pieces, axis=0)).astype(bf16)
    col1[...] = mm(t["pick1"][...], rows, NT).astype(bf16)
    copies = send_columns(col1, col1_in)
    inner = mm(rows, t["shift1"][...])
    arrive(copies)
    full = inner + mm(columns_in(col1_in), t["put1"][...], TN)
    third = [full[:, 128 * k:128 * k + 128].reshape(64, 8, 128) for k in range(3)]
    rolled = [pltpu.roll(piece, 4, axis=1) for piece in third]
    sub = lax.broadcasted_iota(jnp.int32, (64, 8, 128), 1)
    upper = sub < 4
    ones = jnp.where(sub == 4, 1.0, 0.0)
    even_tile = jnp.concatenate(
        [jnp.where(upper, third[0], rolled[1]), jnp.where(upper, third[2], ones)], axis=1
    )
    odd_tile = jnp.concatenate(
        [jnp.where(upper, rolled[0], third[1]), jnp.where(upper, rolled[2], ones)], axis=1
    )
    xs[:, 0] = even_tile.astype(bf16)
    xs[:, 1] = odd_tile.astype(bf16)

    def cols1(w, half_d):
        def at(i, dp, parity):
            return xs[(w + i) * 9 + dp, parity]

        one = [at(i, half_d + j // 2, j % 2) for i in range(3) for j in range(3)]
        two = [at(i, half_d + (j + 1) // 2, (j + 1) % 2) for i in range(3) for j in range(3)]
        return jnp.concatenate(
            [jnp.concatenate(one, axis=0), jnp.concatenate(two, axis=0)], axis=1
        )

    def forward1(pd, carry):
        for pw in range(2):
            part = None
            for w in (2 * pw, 2 * pw + 1):
                pre = mm(wide_first, cols1(w, pd)) + bias1_col
                pre1[w, pd] = pre
                act = leaky(pre)
                act = act[:, :128] + act[:, 128:]
                part = act if part is None else part + act
            part = (part + pltpu.roll(part, 127, axis=1)) * 0.125
            summed[pw, pd] = part.astype(bf16)
        return carry

    lax.fori_loop(0, 8, forward1, 0)
    pooled_val = (
        mm(summed[:, 0:4].reshape(256, 128), t["even"][0:128])
        + mm(summed[:, 4:8].reshape(256, 128), t["even"][128:256])
    ).astype(bf16)
    pooled[...] = pooled_val.reshape(2, 4, 32, 128)

    def assemble(own, wide, deep, corner, v, n):
        left = [kept(edge_flags[a], wide[a]) for a in range(2)]
        v[0:4] = left[0]
        v[4:8] = own[0]
        v[8:12] = own[1]
        v[12:16] = left[1]
        low = lax.broadcasted_iota(jnp.int32, (n, 128), 1) < 64
        for wp in range(4):
            if wp == 0 or wp == 3:
                a = 0 if wp == 0 else 1
                near = left[a]
                far = [
                    kept(jnp.logical_and(edge_flags[a], deep_flags[b]), corner[a * 2 + b]) for b in range(2)
                ]
            else:
                near = own[wp - 1]
                far = [kept(deep_flags[b], deep[b, wp - 1]) for b in range(2)]
            v[16 + wp] = jnp.where(low, near[3].astype(f32), far[0].astype(f32)).astype(bf16)
            v[20 + wp] = jnp.where(low, far[1].astype(f32), near[0].astype(f32)).astype(bf16)

    def halo(own, wide, deep, corner, v, col, col_in, out, n, flipped, meanwhile, between):
        copies = send_ring(
            lambda a: own.at[1 - a], wide,
            lambda b: own.at[:, 3 if b == 0 else 0], deep,
            lambda a, b: own.at[1 - a, 3 if b == 0 else 0], corner,
        )
        result = meanwhile()
        arrive(copies)
        assemble(own, wide, deep, corner, v, n)
        main = v[0:16].reshape(16 * n, 128)
        side = v[16:24].reshape(8 * n, 128)
        col[:, 0:16 * n] = mm(t["pick2"][...], main, NT).astype(bf16)
        col[:, 16 * n:24 * n] = mm(t["pick2s"][...], side, NT).astype(bf16)
        copies = send_columns(col, col_in)
        result = between(result)
        inner = jnp.concatenate([mm(main, t["shift2"][...]), mm(side, t["swapped"][...])], axis=0)
        arrive(copies)
        full = inner + mm(columns_in(col_in), t["put2"][...], TN)
        for k in range(3):
            place = 2 - k if flipped else k
            piece = full[:, 128 * k:128 * k + 128].astype(bf16).reshape(24, n, 128)
            out[:, place * n:place * n + n, :] = piece
        return result

    def tile(wp, dp):
        if dp == 0:
            return 16 + wp
        if dp == 5:
            return 20 + wp
        return wp * 4 + dp - 1

    halo(pooled, wide2, deep2, corner2, v2, col2, col2_in, ys, 32, False, lambda: None, lambda a: a)

    def cols2(w, dq, extra):
        taps = [ys[tile(w + i, dq + j)] for i in range(3) for j in range(3)]
        return jnp.concatenate(taps + extra, axis=0)

    feat_sum = [None, None]
    for dq in range(4):
        cols = jnp.concatenate([cols2(0, dq, []), cols2(1, dq, [])], axis=1)
        pre = mm(second_half, cols) + bias2_col
        act = leaky(pre)
        act = act[:, :128] + act[:, 128:]
        pair = dq // 2
        feat_sum[pair] = act if feat_sum[pair] is None else feat_sum[pair] + act
        cot_here = spread_cot[:, 128 * pair:128 * pair + 128]
        err = (jnp.concatenate([cot_here, cot_here], axis=1) * slope(pre)).astype(bf16)
        errs[0, dq] = err[:, :128]
        errs[1, dq] = err[:, 128:]

    def second_half_grads():
        ends = [
            ((both + pltpu.roll(both, 127, axis=1)) * 0.125).astype(bf16) for both in feat_sum
        ]
        feat[...] = (mm(t["collect"][0:128], ends[0], NT) + mm(t["collect"][128:256], ends[1], NT)).astype(bf16)
        ones_rows = [jnp.ones((32, 128), bf16)]
        grad2 = None
        for dq in range(4):
            cols = jnp.concatenate([cols2(0, dq, ones_rows), cols2(1, dq, ones_rows)], axis=1)
            err = jnp.concatenate([errs[0, dq], errs[1, dq]], axis=1)
            piece = mm(err, cols, NT)
            grad2 = piece if grad2 is None else grad2 + piece
        for l in range(7):
            grads[l * 64:l * 64 + 64] = grad2[:, 128 * l:128 * l + 128]
        grads[448:512] = jnp.zeros((64, 128), f32)
        return put_out(0), send(part(grads, 1 - core, n1), core_in, sibling)

    def part(ref, index, size):
        return ref.at[pl.ds(pl.multiple_of(index * size, size), size)]

    n1, n2, n3 = 256, 256 // NX, 256 // NX // GY

    def sum_core(copy):
        copy.wait_recv()
        red1[...] = part(grads, core, n1)[...] + core_in[...]
        return [send(part(red1, x_peer(r)[0], n2), x_in.at[r - 1], x_peer(r)[1]) for r in range(1, NX)]

    def sum_x(copies):
        arrive(copies)
        acc = part(red1, xc, n2)[...]
        for r in range(1, NX):
            acc = acc + x_in[r - 1]
        red2[...] = acc
        return [send(part(red2, y_peer(r)[0], n3), y_in.at[r - 1], y_peer(r)[1]) for r in range(1, GY)]

    def sum_y(copies):
        arrive(copies)
        acc = part(red2, gy, n3)[...]
        for r in range(1, GY):
            acc = acc + y_in[r - 1]
        red3[...] = acc
        z_in[zc] = acc
        return [send(red3, z_in.at[zc], z_peer(r)) for r in range(1, NZ)]

    def sum_z(copies):
        arrive(copies)
        acc = z_in[0]
        for r in range(1, NZ):
            acc = acc + z_in[r]
        mine = part(total, (core * NX + xc) * GY + gy, n3)
        mine[...] = acc
        return [send(mine, mine, y_peer(r)[1]) for r in range(1, GY)]

    def gather_x(copies):
        arrive(copies)
        mine = part(total, core * NX + xc, n2)
        return [send(mine, mine, x_peer(r)[1]) for r in range(1, NX)]

    def gather_core(copies):
        arrive(copies)
        mine = part(total, core, n1)
        return send(mine, mine, sibling)

    def everyone(value, slots, index, devices):
        slots[index] = value
        return [send(slots.at[index], slots.at[index], device) for device in devices]

    def summed_slots(copies, slots):
        arrive(copies)
        acc = slots[0]
        for n in range(1, slots.shape[0]):
            acc = acc + slots[n]
        return acc

    feat_out, copies2 = halo(
        errs, wide3, deep3, corner3, v3, col3, col3_in, fs, 64, True, second_half_grads,
        lambda a: (a[0], sum_core(a[1])),
    )

    for dq in range(4):
        def cols3(w):
            taps = [fs[tile(w + 2 - i, dq + 2 - j)] for i in range(3) for j in range(3)]
            return jnp.concatenate(taps + [jnp.zeros((64, 128), bf16)], axis=0)

        cols = jnp.concatenate([cols3(0), cols3(1)], axis=1)
        pe = mm(turned[...], cols).astype(bf16)
        both = mm(jnp.concatenate([pe[:, :128], pe[:, 128:]], axis=0), t["twice"][...]) * 0.125
        for w in range(2):
            perr[w, dq] = both[32 * w:32 * w + 32, :128]
            perr[w, dq + 4] = both[32 * w:32 * w + 32, 128:]

    copies2 = sum_x(copies2)

    def backward1(pd, acc):
        for w in range(4):
            here = perr[w // 2, pd]
            err = (jnp.concatenate([here, here], axis=1) * slope(pre1[w, pd])).astype(bf16)
            acc = acc + mm(err, cols1(w, pd), NT)
        return acc

    grad1 = lax.fori_loop(0, 8, backward1, jnp.zeros((32, 144), f32))
    one[...] = sum(mm(piece, t["narrow"][...]) for piece in split3(grad1))
    copies1 = send(part(one, 1 - core, 16), one_core, sibling)
    copies2 = sum_y(copies2)
    copies1.wait_recv()
    copies1 = everyone(part(one, core, 16)[...] + one_core[...], one_x, xc, [x_peer(r)[1] for r in range(1, NX)])
    copies2 = sum_z(copies2)
    copies1 = everyone(summed_slots(copies1, one_x), one_y, gy, [y_peer(r)[1] for r in range(1, GY)])
    copies2 = gather_x(copies2)
    copies1 = everyone(summed_slots(copies1, one_y), one_z, zc, [z_peer(r) for r in range(1, NZ)])
    copy2 = gather_core(copies2)
    mine = part(one_total, core, 16)
    mine[...] = summed_slots(copies1, one_z)
    copy1 = send(mine, mine, sibling)

    copy2.wait_recv()
    sums2 = jnp.concatenate([total[l * 64:l * 64 + 64] for l in range(7)], axis=1)
    step2[...] = filt2[...] - learn_rate * sums2[:, :864]
    off2[...] = bias2[...] - learn_rate * column_to_row(sums2[:, 864:865])
    outs = [put_out(3), put_out(4)]
    copy1.wait_recv()
    sums1 = one_total[...]
    step1[...] = filt1[...] - learn_rate * sums1[:, :108]
    off1[...] = bias1[...] - learn_rate * column_to_row(sums1[:, 108:109])
    outs += [put_out(1), put_out(2)]

    for copy in started:
        copy.wait_send()
    feat_out.wait()
    for out in outs:
        out.wait()


def hand_on(*refs):
    sems = refs[10]
    copies = [pltpu.make_async_copy(refs[n], refs[5 + n], sems.at[n]) for n in range(5)]
    for copy in copies:
        copy.start()
    for copy in copies:
        copy.wait()


def shards(volume, first_filters, first_bias, second_filters, second_bias, cotangent):
    GX, GY, GZ = lax.axis_size("gx"), lax.axis_size("gy"), lax.axis_size("gz")
    NX = 4 if GZ >= 8 else 2
    NZ = (GX // 2) * (GZ // NX)
    n2, n3 = 256 // NX, 256 // NX // GY
    operands = [
        volume, first_filters, first_bias.reshape(1, 32), second_filters, second_bias.reshape(1, 64),
        cotangent.transpose(1, 2, 3, 0).reshape(128, 64), jnp.asarray(PACKED),
    ]
    sems = 30 + 4 + 3 * (NX - 1) + 3 * (GY - 1) + 2 * (NZ - 1)
    V = pltpu.VMEM
    results = (
        jax.ShapeDtypeStruct((128, 64), bf16),
        jax.ShapeDtypeStruct((32, 108), f32),
        jax.ShapeDtypeStruct((1, 32), f32),
        jax.ShapeDtypeStruct((64, 864), f32),
        jax.ShapeDtypeStruct((1, 64), f32),
    )
    out = pl.pallas_call(
        functools.partial(kernel, (GX, GY, GZ, NX)),
        out_shape=results,
        in_specs=[pl.BlockSpec(memory_space=pltpu.HBM)] * len(operands),
        out_specs=[pl.BlockSpec(memory_space=pltpu.HBM)] * 5,
        scratch_shapes=[
            V((32, 128), bf16), V((2, 4, 16, 128), bf16), V((2, 16, 128), bf16), V((4, 16, 128), bf16),
            V((16, 512), bf16), V((2, 16, 512), bf16), V((64, 2, 16, 128), bf16), V((4, 8, 32, 256), f32),
            V((2, 8, 32, 128), bf16),
            V((2, 4, 32, 128), bf16), V((2, 4, 32, 128), bf16), V((2, 2, 32, 128), bf16), V((4, 32, 128), bf16),
            V((24, 32, 128), bf16), V((16, 768), bf16), V((2, 16, 768), bf16), V((24, 96, 128), bf16),
            V((2, 4, 64, 128), bf16), V((2, 4, 64, 128), bf16), V((2, 2, 64, 128), bf16), V((4, 64, 128), bf16),
            V((24, 64, 128), bf16), V((16, 1536), bf16), V((2, 16, 1536), bf16), V((24, 192, 128), bf16),
            V((32, 1792), bf16), V((2, 8, 32, 128), f32),
            V((512, 128), f32), V((256, 128), f32), V((256, 128), f32), V((NX - 1, n2, 128), f32),
            V((n2, 128), f32), V((GY - 1, n3, 128), f32), V((n3, 128), f32), V((NZ, n3, 128), f32),
            V((512, 128), f32),
            V((32, 128), f32), V((16, 128), f32), V((NX, 16, 128), f32), V((GY, 16, 128), f32),
            V((NZ, 16, 128), f32), V((32, 128), f32),
            pltpu.SemaphoreType.DMA((sems,)), pltpu.SemaphoreType.DMA((sems,)),
        ] + [V(a.shape, a.dtype) for a in operands] + [
            pltpu.SemaphoreType.DMA((len(operands),)),
        ] + [V(a.shape, a.dtype) for a in results] + [
            pltpu.SemaphoreType.DMA((5,)),
        ],
        compiler_params=pltpu.CompilerParams(
            collective_id=0, has_side_effects=True, vmem_limit_bytes=62 * 2**20
        ),
    )(*operands)
    out = pl.pallas_call(
        hand_on,
        out_shape=results,
        in_specs=[pl.BlockSpec(memory_space=pltpu.HBM)] * 5,
        out_specs=[pl.BlockSpec(memory_space=pltpu.HBM)] * 5,
        scratch_shapes=[pltpu.SemaphoreType.DMA((5,))],
        compiler_params=pltpu.CompilerParams(vmem_limit_bytes=62 * 2**20),
    )(*out)
    features, stepped_first, offset_first, stepped_second, offset_second = out
    return (
        features.reshape(1, 4, 32, 64).transpose(3, 0, 1, 2), stepped_first, offset_first.reshape(32), stepped_second,
        offset_second.reshape(64),
    )


def solution(mesh):
    return jax.shard_map(
        shards,
        mesh=mesh,
        in_specs=(P(None, "gx", "gz", "gy"), P(), P(), P(), P(), P(None, "gx", "gz", "gy")),
        out_specs=(P(None, "gx", "gz", "gy"), P(), P(), P(), P()),
        check_vma=False,
    )
```

```python
import functools

import jax
import jax.numpy as jnp
import numpy as np
from jax import lax
from jax.experimental import pallas as pl
from jax.experimental.pallas import tpu as pltpu
from jax.sharding import PartitionSpec as P

slope_below = 0.3
learn_rate = 0.001
f32 = jnp.float32
bf16 = jnp.bfloat16
MESH = pl.DeviceIdType.MESH
NN = (((1,), (0,)), ((), ()))
NT = (((1,), (1,)), ((), ()))
TN = (((0,), (0,)), ((), ()))


def mm(a, b, dims=NN):
    return lax.dot_general(a, b, dims, preferred_element_type=f32)


def tables():
    place = np.zeros((512, 480))
    for wp in range(6):
        for dp in range(18):
            for ch in range(4):
                w, d = wp - 1, dp - 1
                inner_w, inner_d = 0 <= w < 4, 0 <= d < 16
                if inner_w and inner_d:
                    src = (ch * 4 + w) * 16 + d
                elif inner_d:
                    src = 256 + (64 if w > 0 else 0) + ch * 16 + d
                elif inner_w:
                    src = 384 + (16 if d > 0 else 0) + ch * 4 + w
                else:
                    a, b = int(w > 0), int(d > 0)
                    src = 416 + (a * 2 + b) * 16 + ch * 4 + (0 if a else 3)
                place[(wp * 18 + dp) * 4 + ch, src] = 1
    shift1 = np.zeros((128, 384))
    for l in range(128):
        if l:
            shift1[l - 1, l] = 1
        shift1[l, 128 + l] = 1
        if l < 127:
            shift1[l + 1, 256 + l] = 1
    order1 = np.zeros((1152, 128))
    for wp in range(6):
        for dp in range(18):
            a, b = (wp > 0) + (wp > 4), (dp > 0) + (dp > 16)
            w, d = (3, wp - 1, 0)[a], (15, dp - 1, 0)[b]
            order1[(a * 3 + b) * 128 + w * 16 + d, wp * 18 + dp] = 1
    four = np.zeros((128, 512))
    for q in range(512):
        four[q // 4, q] = 1
    put1 = np.zeros((32, 256))
    for ch in range(4):
        put1[ch * 2 + 1, 0] = put1[16 + ch * 2, 255] = 1
    shift2 = np.zeros((128, 384))
    swapped = np.zeros((128, 384))
    for l in range(128):
        for k in range(3):
            s = l % 64 + k - 1
            if 0 <= s < 64:
                s += l - l % 64
                shift2[s, k * 128 + l] = 1
                swapped[(s + 64) % 128, k * 128 + l] = 1
    ends = (0, 63, 64, 127)
    pick2 = np.zeros((16, 512))
    for dq in range(4):
        for n, l in enumerate(ends):
            pick2[dq * 4 + n, dq * 128 + l] = 1
    put2 = np.zeros((96, 1536))
    for dp in range(6):
        if dp == 0:
            near = ((0, 3, 1), (1, 3, 0))
        elif dp == 5:
            near = ((1, 0, 1), (2, 0, 0))
        else:
            near = ((1, dp - 1, 0), (1, dp - 1, 1))
        for half, (dz, dq, there) in enumerate(near):
            put2[dz * 16 + dq * 4 + 2 * there + 1, dp * 256 + 64 * half] = 1
            put2[48 + dz * 16 + dq * 4 + 2 * there, dp * 256 + 128 + 64 * half + 63] = 1
    even = np.zeros((256, 128))
    for half in range(2):
        for h in range(64):
            even[half * 128 + 2 * h, half * 64 + h] = 1
    twice = np.zeros((128, 256))
    for half in range(2):
        for h in range(128):
            twice[half * 64 + h // 2, half * 128 + h] = 1
    spread = np.zeros((128, 256))
    collect = np.zeros((256, 128))
    for dc in range(4):
        for hc in range(32):
            for t in range(2):
                spread[dc * 32 + hc, (dc % 2) * 128 + (dc // 2) * 64 + 2 * hc + t] = 1
            collect[(dc % 2) * 128 + dc * 32 + hc, (dc // 2) * 64 + 2 * hc] = 1
    widen = np.zeros((108, 144))
    narrow = np.zeros((144, 128))
    for q in range(108):
        widen[q, (q // 12) * 16 + q % 12] = 1
        narrow[(q // 12) * 16 + q % 12, q] = 1
    narrow[12, 108] = 1
    ident = np.zeros((64, 256))
    for o in range(64):
        ident[o, o] = ident[o, 128 + 64 + o] = 1
    every = dict(
        place=place, shift1=shift1, order1=order1, four=four, put1=put1, shift2=shift2, swapped=swapped,
        pick2=pick2, put2=put2, even=even, twice=twice, spread=spread, collect=collect,
        widen=widen, narrow=narrow, ident=ident,
    )
    return every


TABLE = {}


def packed_table():
    parts, row = [], 0
    for name, value in tables().items():
        rows, lanes = value.shape
        wide = np.zeros((-(-rows // 16) * 16, -(-lanes // 512) * 512))
        wide[:rows, :lanes] = value
        wide = np.concatenate(np.split(wide, wide.shape[1] // 512, axis=1))
        TABLE[name] = (row, rows, lanes)
        row += wide.shape[0]
        parts.append(wide)
    return np.concatenate(parts).astype(jnp.bfloat16)


PACKED = packed_table()


class Rows:
    def __init__(self, ref, name):
        self.ref = ref
        self.row, self.rows, self.lanes = TABLE[name]

    def __getitem__(self, key):
        if self.lanes > 512:
            step = -(-self.rows // 16) * 16
            return jnp.concatenate(
                [self.ref[self.row + n * step:self.row + n * step + self.rows, :] for n in range(self.lanes // 512)],
                axis=1,
            )
        if key is Ellipsis:
            return self.ref[self.row:self.row + self.rows, :self.lanes]
        return self.ref[self.row + key.start:self.row + key.stop, :self.lanes]


def row_to_column(row):
    n = row.shape[1]
    diagonal = lax.broadcasted_iota(jnp.int32, (n, n), 0) == lax.broadcasted_iota(jnp.int32, (n, n), 1)
    return jnp.sum(jnp.where(diagonal, jnp.broadcast_to(row, (n, n)), 0.0), axis=1, keepdims=True)


def column_to_row(column):
    n = column.shape[0]
    diagonal = lax.broadcasted_iota(jnp.int32, (n, n), 0) == lax.broadcasted_iota(jnp.int32, (n, n), 1)
    return jnp.sum(jnp.where(diagonal, jnp.broadcast_to(column, (n, n)), 0.0), axis=0, keepdims=True)


def kept(flag, value):
    return lax.select(flag, value, jnp.zeros_like(value))


def leaky(a):
    return jnp.where(a > 0, a, slope_below * a)


def slope(a):
    return jnp.where(a > 0, 1.0, slope_below)


def split3(a):
    high = a.astype(bf16)
    rest = a - high.astype(f32)
    mid = rest.astype(bf16)
    return high, mid, (rest - mid.astype(f32)).astype(bf16)


def kernel(sizes, *refs):
    GX, GY, GZ, NX = sizes
    ZL = GZ // NX
    ZH = GX // 2
    NZ = ZH * ZL
    far = refs[:7]
    refs = refs[7:]
    far_out = refs[:5]
    (
        edges, wide_in, deep_in, corner_in, col1, col1_in, xs, pre1, summed,
        pooled, wide2, deep2, corner2, v2, col2, col2_in, ys,
        errs, wide3, deep3, corner3, v3, col3, col3_in, fs, turned, perr,
        grads, core_in, red1, x_in, red2, y_in, red3, z_in, total,
        one, one_core, one_x, one_y, one_z, one_total, send_sems, recv_sems, vol, filt1, bias1, filt2, bias2, cot, packed, in_sems,
        feat, step1, off1, step2, off2, out_sems,
    ) = refs[5:]
    near = (vol, filt1, bias1, filt2, bias2, cot, packed)
    fetches = [pltpu.make_async_copy(a, b, in_sems.at[n]) for n, (a, b) in enumerate(zip(far, near))]
    for fetch in fetches:
        fetch.start()
    t = {name: Rows(packed, name) for name in TABLE}

    gx, gy, gz = lax.axis_index("gx"), lax.axis_index("gy"), lax.axis_index("gz")
    core, zh = lax.rem(gx, 2), lax.div(gx, 2)
    xc, zl = lax.rem(gz, NX), lax.div(gz, NX)
    zc = zh * ZL + zl

    def shifted(dx, dy, dz):
        return (lax.rem(gx + (dx + GX), GX), lax.rem(gy + (dy + GY), GY), lax.rem(gz + (dz + GZ), GZ))

    sibling = (gx + 1 - 2 * core, gy, gz)

    def x_peer(r):
        p = lax.rem(xc + r, NX)
        return p, (gx, gy, zl * NX + p)

    def y_peer(r):
        p = lax.rem(gy + r, GY)
        return p, (gx, p, gz)

    def z_peer(r):
        p = lax.rem(zc + r, NZ)
        return (2 * lax.div(p, ZL) + core, gy, lax.rem(p, ZL) * NX + xc)

    square = [(dx, dz) for dx in (-1, 0, 1) for dz in (-1, 0, 1)]
    peers = [shifted(dx, 0, dz) for dx, dz in square if (dx, dz) != (0, 0)]
    peers += [shifted(dx, dy, dz) for dx, dz in square for dy in (-1, 1)]
    peers += [x_peer(r)[1] for r in range(1, NX)]
    peers += [y_peer(r)[1] for r in range(1, GY)]
    peers += [z_peer(r) for r in range(1, NZ)]
    barrier = pltpu.get_barrier_semaphore()
    for peer in peers:
        pl.semaphore_signal(barrier, inc=1, device_id=peer, device_id_type=MESH)

    count = [0]
    started = []

    def send(src, dst, device):
        n = count[0]
        count[0] += 1
        copy = pltpu.make_async_remote_copy(
            src_ref=src, dst_ref=dst, send_sem=send_sems.at[n], recv_sem=recv_sems.at[n],
            device_id=device, device_id_type=MESH,
        )
        copy.start()
        started.append(copy)
        return copy

    def put_out(n):
        copy = pltpu.make_async_copy((feat, step1, off1, step2, off2)[n], far_out[n], out_sems.at[n])
        copy.start()
        return copy

    def arrive(copies):
        for copy in copies:
            copy.wait_recv()

    row = lax.broadcasted_iota(jnp.int32, (32, 256), 0)
    column = lax.broadcasted_iota(jnp.int32, (32, 256), 1)
    wanted = jnp.where(row < 16, row * 16, row * 16 - 241)
    edge = jnp.where(column == wanted, 1.0, 0.0).astype(bf16)
    fetches[0].wait()
    block = vol[...].reshape(256, 128)
    edges[...] = mm(edge, block).astype(bf16)
    pl.semaphore_wait(barrier, len(peers))

    has_left, has_right = gx > 0, gx < GX - 1
    has_front, has_back = gz > 0, gz < GZ - 1
    has_below, has_above = gy > 0, gy < GY - 1

    def send_ring(wide_src, wide_dst, deep_src, deep_dst, corner_src, corner_dst):
        copies = []
        for a in range(2):
            dx = 1 if a == 0 else -1
            copies.append(send(wide_src(a), wide_dst.at[a], shifted(dx, 0, 0)))
        for b in range(2):
            dz = 1 if b == 0 else -1
            copies.append(send(deep_src(b), deep_dst.at[b], shifted(0, 0, dz)))
        for a in range(2):
            for b in range(2):
                copies.append(
                    send(corner_src(a, b), corner_dst.at[a * 2 + b], shifted(1 if a == 0 else -1, 0, 1 if b == 0 else -1))
                )
        return copies

    def send_columns(src, dst):
        copies = []
        for dx, dz in square:
            for side in range(2):
                dy = 1 if side == 0 else -1
                copies.append(send(src, dst.at[side, 1 - dx, 1 - dz], shifted(dx, dy, dz)))
        return copies

    def columns_in(dst, dx):
        rows = []
        for side in range(2):
            for dz in (-1, 0, 1):
                flag = (has_below, has_above)[side]
                if dx:
                    flag = jnp.logical_and(flag, edge_flags[(dx + 1) // 2])
                if dz:
                    flag = jnp.logical_and(flag, deep_flags[(dz + 1) // 2])
                rows.append(kept(flag, dst[side, dx + 1, dz + 1]))
        return rows

    edge_flags = (has_left, has_right)
    deep_flags = (has_front, has_back)

    def edge_rows(b):
        return edges.at[pl.ds(16, 16)] if b == 0 else edges.at[pl.ds(0, 16)]

    copies = send_ring(
        lambda a: vol.at[:, 3] if a == 0 else vol.at[:, 0], wide_in,
        edge_rows, deep_in, lambda a, b: edge_rows(b), corner_in,
    )

    row = lax.broadcasted_iota(jnp.int32, (16, 512), 0)
    column = lax.broadcasted_iota(jnp.int32, (16, 512), 1)
    wanted = jnp.where(row < 8, lax.div(row, 2) * 128 + lax.rem(row, 2) * 127, -1)
    pick1 = jnp.where(column == wanted, 1.0, 0.0).astype(bf16)
    ends = sum(
        mm(pick1[:, 128 * ch:128 * ch + 128], vol[ch].reshape(64, 128), NT) for ch in range(4)
    )
    col1[...] = jnp.concatenate([ends, jnp.zeros((16, 64), f32)], axis=1).astype(bf16)
    copies_c = send_columns(col1, col1_in)
    for fetch in fetches[1:]:
        fetch.wait()
    first_half = filt1[...].astype(bf16)
    wide_first = mm(first_half, t["widen"][...]).astype(bf16)
    bias1_col = row_to_column(bias1[...])
    bias2_col = row_to_column(bias2[...])
    second_half = filt2[...].astype(bf16)

    turn = mm(second_half, t["ident"][...], TN).astype(bf16)
    for m in range(13):
        low = turn[64 * m:64 * m + 32, :128].astype(f32)
        high = turn[64 * m + 32:64 * m + 64, 128:].astype(f32)
        turned[:, 128 * m:128 * m + 128] = (low + high).astype(bf16)
    turned[:, 1664:1792] = turn[832:864, :128]
    spread_cot = mm(cot[...], t["spread"][...], TN) * 0.125

    arrive(copies)
    pieces = [block]
    for a in range(2):
        pieces.append(kept(edge_flags[a], wide_in[a]).reshape(64, 128))
    for b in range(2):
        pieces.append(kept(deep_flags[b], deep_in[b]))
    for a in range(2):
        for b in range(2):
            pieces.append(kept(jnp.logical_and(edge_flags[a], deep_flags[b]), corner_in[a * 2 + b]))
    rows = mm(t["place"][...], jnp.concatenate(pieces, axis=0)).astype(bf16)
    inner = mm(rows, t["shift1"][...])
    arrive(copies_c)
    columns = [columns_in(col1_in, dx) for dx in (-1, 0, 1)]
    sides = [
        jnp.concatenate([columns[a][side * 3 + b] for a in range(3) for b in range(3)], axis=1)
        for side in range(2)
    ]
    ordered = mm(jnp.concatenate(sides, axis=0), t["order1"][...]).astype(bf16)
    ordered = mm(ordered, t["four"][...])
    row = lax.broadcasted_iota(jnp.int32, (32, 512), 0)
    column = lax.broadcasted_iota(jnp.int32, (32, 512), 1)
    same = lax.rem(lax.div(row, 2), 8) == lax.rem(column, 4)
    ordered = jnp.where(same, ordered, 0.0).astype(bf16)
    ends = mm(ordered, t["put1"][...], TN)
    full = [inner[:, :128] + ends[:, :128], inner[:, 128:256], inner[:, 256:] + ends[:, 128:]]
    third = [piece.reshape(64, 8, 128) for piece in full]
    rolled = [pltpu.roll(piece, 4, axis=1) for piece in third]
    sub = lax.broadcasted_iota(jnp.int32, (64, 8, 128), 1)
    upper = sub < 4
    ones = jnp.where(sub == 4, 1.0, 0.0)
    even_tile = jnp.concatenate(
        [jnp.where(upper, third[0], rolled[1]), jnp.where(upper, third[2], ones)], axis=1
    )
    odd_tile = jnp.concatenate(
        [jnp.where(upper, rolled[0], third[1]), jnp.where(upper, rolled[2], ones)], axis=1
    )
    xs[:, 0] = even_tile.astype(bf16)
    xs[:, 1] = odd_tile.astype(bf16)

    def cols1(w, half_d):
        def at(i, dp, parity):
            return xs[(w + i) * 9 + dp, parity]

        one = [at(i, half_d + j // 2, j % 2) for i in range(3) for j in range(3)]
        two = [at(i, half_d + (j + 1) // 2, (j + 1) % 2) for i in range(3) for j in range(3)]
        return jnp.concatenate(
            [jnp.concatenate(one, axis=0), jnp.concatenate(two, axis=0)], axis=1
        )

    def forward1(pd, carry):
        for pw in range(2):
            part = None
            for w in (2 * pw, 2 * pw + 1):
                pre = mm(wide_first, cols1(w, pd)) + bias1_col
                pre1[w, pd] = pre
                act = leaky(pre)
                act = act[:, :128] + act[:, 128:]
                part = act if part is None else part + act
            part = (part + pltpu.roll(part, 127, axis=1)) * 0.125
            summed[pw, pd] = part.astype(bf16)
        return carry

    lax.fori_loop(0, 8, forward1, 0)
    pooled_val = (
        mm(summed[:, 0:4].reshape(256, 128), t["even"][0:128])
        + mm(summed[:, 4:8].reshape(256, 128), t["even"][128:256])
    ).astype(bf16)
    pooled[...] = pooled_val.reshape(2, 4, 32, 128)

    def assemble(own, wide, deep, corner, v, n):
        left = [kept(edge_flags[a], wide[a]) for a in range(2)]
        v[0:4] = left[0]
        v[4:8] = own[0]
        v[8:12] = own[1]
        v[12:16] = left[1]
        low = lax.broadcasted_iota(jnp.int32, (n, 128), 1) < 64
        for wp in range(4):
            if wp == 0 or wp == 3:
                a = 0 if wp == 0 else 1
                near = left[a]
                far = [
                    kept(jnp.logical_and(edge_flags[a], deep_flags[b]), corner[a * 2 + b]) for b in range(2)
                ]
            else:
                near = own[wp - 1]
                far = [kept(deep_flags[b], deep[b, wp - 1]) for b in range(2)]
            v[16 + wp] = jnp.where(low, near[3].astype(f32), far[0].astype(f32)).astype(bf16)
            v[20 + wp] = jnp.where(low, far[1].astype(f32), near[0].astype(f32)).astype(bf16)

    def halo(own, wide, deep, corner, v, col, col_in, out, n, flipped, meanwhile, between):
        copies = send_ring(
            lambda a: own.at[1 - a], wide,
            lambda b: own.at[:, 3 if b == 0 else 0], deep,
            lambda a, b: own.at[1 - a, 3 if b == 0 else 0], corner,
        )
        pick = t["pick2"][...]
        ends = sum(
            mm(pick[:, 128 * dq:128 * dq + 128], own[:, dq].reshape(2 * n, 128), NT) for dq in range(4)
        )
        if n < 64:
            ends = jnp.concatenate([ends, jnp.zeros((16, 128 - 2 * n), f32)], axis=1)
        col[...] = ends.astype(bf16)
        copies_c = send_columns(col, col_in)
        result = meanwhile()
        arrive(copies)
        assemble(own, wide, deep, corner, v, n)
        main = v[0:16].reshape(16 * n, 128)
        side = v[16:24].reshape(8 * n, 128)
        inner = jnp.concatenate([mm(main, t["shift2"][...]), mm(side, t["swapped"][...])], axis=0)
        result = between(result)
        arrive(copies_c)
        put = t["put2"][...]
        edge = [mm(jnp.concatenate(columns_in(col_in, dx), axis=0), put, TN) for dx in (-1, 0, 1)]
        for wp in range(4):
            far, w = ((0, 1), (1, 0), (1, 1), (2, 0))[wp]
            for dp in range(6):
                number = tile(wp, dp)
                for k in range(3):
                    piece = inner[number * n:number * n + n, 128 * k:128 * k + 128]
                    if k != 1:
                        lane = dp * 256 + 64 * k
                        piece = piece + edge[far][w * n:w * n + n, lane:lane + 128]
                    place = 2 - k if flipped else k
                    out[number, place * n:place * n + n, :] = piece.astype(bf16)
        return result

    def tile(wp, dp):
        if dp == 0:
            return 16 + wp
        if dp == 5:
            return 20 + wp
        return wp * 4 + dp - 1

    halo(pooled, wide2, deep2, corner2, v2, col2, col2_in, ys, 32, False, lambda: None, lambda a: a)

    def cols2(w, dq, extra):
        taps = [ys[tile(w + i, dq + j)] for i in range(3) for j in range(3)]
        return jnp.concatenate(taps + extra, axis=0)

    feat_sum = [None, None]
    for dq in range(4):
        cols = jnp.concatenate([cols2(0, dq, []), cols2(1, dq, [])], axis=1)
        pre = mm(second_half, cols) + bias2_col
        act = leaky(pre)
        act = act[:, :128] + act[:, 128:]
        pair = dq // 2
        feat_sum[pair] = act if feat_sum[pair] is None else feat_sum[pair] + act
        cot_here = spread_cot[:, 128 * pair:128 * pair + 128]
        err = (jnp.concatenate([cot_here, cot_here], axis=1) * slope(pre)).astype(bf16)
        errs[0, dq] = err[:, :128]
        errs[1, dq] = err[:, 128:]

    def second_half_grads():
        ends = [
            ((both + pltpu.roll(both, 127, axis=1)) * 0.125).astype(bf16) for both in feat_sum
        ]
        feat[...] = (mm(t["collect"][0:128], ends[0], NT) + mm(t["collect"][128:256], ends[1], NT)).astype(bf16)
        ones_rows = [jnp.ones((32, 128), bf16)]
        grad2 = None
        for dq in range(4):
            cols = jnp.concatenate([cols2(0, dq, ones_rows), cols2(1, dq, ones_rows)], axis=1)
            err = jnp.concatenate([errs[0, dq], errs[1, dq]], axis=1)
            piece = mm(err, cols, NT)
            grad2 = piece if grad2 is None else grad2 + piece
        for l in range(7):
            grads[l * 64:l * 64 + 64] = grad2[:, 128 * l:128 * l + 128]
        grads[448:512] = jnp.zeros((64, 128), f32)
        return put_out(0), send(part(grads, 1 - core, n1), core_in, sibling)

    def part(ref, index, size):
        return ref.at[pl.ds(pl.multiple_of(index * size, size), size)]

    n1, n2, n3 = 256, 256 // NX, 256 // NX // GY

    def sum_core(copy):
        copy.wait_recv()
        red1[...] = part(grads, core, n1)[...] + core_in[...]
        return [send(part(red1, x_peer(r)[0], n2), x_in.at[r - 1], x_peer(r)[1]) for r in range(1, NX)]

    def sum_x(copies):
        arrive(copies)
        acc = part(red1, xc, n2)[...]
        for r in range(1, NX):
            acc = acc + x_in[r - 1]
        red2[...] = acc
        return [send(part(red2, y_peer(r)[0], n3), y_in.at[r - 1], y_peer(r)[1]) for r in range(1, GY)]

    def sum_y(copies):
        arrive(copies)
        acc = part(red2, gy, n3)[...]
        for r in range(1, GY):
            acc = acc + y_in[r - 1]
        red3[...] = acc
        z_in[zc] = acc
        return [send(red3, z_in.at[zc], z_peer(r)) for r in range(1, NZ)]

    def sum_z(copies):
        arrive(copies)
        acc = z_in[0]
        for r in range(1, NZ):
            acc = acc + z_in[r]
        mine = part(total, (core * NX + xc) * GY + gy, n3)
        mine[...] = acc
        return [send(mine, mine, y_peer(r)[1]) for r in range(1, GY)]

    def gather_x(copies):
        arrive(copies)
        mine = part(total, core * NX + xc, n2)
        return [send(mine, mine, x_peer(r)[1]) for r in range(1, NX)]

    def gather_core(copies):
        arrive(copies)
        mine = part(total, core, n1)
        return send(mine, mine, sibling)

    def everyone(value, slots, index, devices):
        slots[index] = value
        return [send(slots.at[index], slots.at[index], device) for device in devices]

    def summed_slots(copies, slots):
        arrive(copies)
        acc = slots[0]
        for n in range(1, slots.shape[0]):
            acc = acc + slots[n]
        return acc

    feat_out, copies2 = halo(
        errs, wide3, deep3, corner3, v3, col3, col3_in, fs, 64, True, second_half_grads,
        lambda a: (a[0], sum_core(a[1])),
    )

    for dq in range(4):
        def cols3(w):
            taps = [fs[tile(w + 2 - i, dq + 2 - j)] for i in range(3) for j in range(3)]
            return jnp.concatenate(taps + [jnp.zeros((64, 128), bf16)], axis=0)

        cols = jnp.concatenate([cols3(0), cols3(1)], axis=1)
        pe = mm(turned[...], cols).astype(bf16)
        both = mm(jnp.concatenate([pe[:, :128], pe[:, 128:]], axis=0), t["twice"][...]) * 0.125
        for w in range(2):
            perr[w, dq] = both[32 * w:32 * w + 32, :128]
            perr[w, dq + 4] = both[32 * w:32 * w + 32, 128:]

    copies2 = sum_x(copies2)

    def backward1(pd, acc):
        for w in range(4):
            here = perr[w // 2, pd]
            err = (jnp.concatenate([here, here], axis=1) * slope(pre1[w, pd])).astype(bf16)
            acc = acc + mm(err, cols1(w, pd), NT)
        return acc

    grad1 = lax.fori_loop(0, 8, backward1, jnp.zeros((32, 144), f32))
    one[...] = sum(mm(piece, t["narrow"][...]) for piece in split3(grad1))
    copies1 = send(part(one, 1 - core, 16), one_core, sibling)
    copies2 = sum_y(copies2)
    copies1.wait_recv()
    copies1 = everyone(part(one, core, 16)[...] + one_core[...], one_x, xc, [x_peer(r)[1] for r in range(1, NX)])
    copies2 = sum_z(copies2)
    copies1 = everyone(summed_slots(copies1, one_x), one_y, gy, [y_peer(r)[1] for r in range(1, GY)])
    copies2 = gather_x(copies2)
    copies1 = everyone(summed_slots(copies1, one_y), one_z, zc, [z_peer(r) for r in range(1, NZ)])
    copy2 = gather_core(copies2)
    mine = part(one_total, core, 16)
    mine[...] = summed_slots(copies1, one_z)
    copy1 = send(mine, mine, sibling)

    copy2.wait_recv()
    sums2 = jnp.concatenate([total[l * 64:l * 64 + 64] for l in range(7)], axis=1)
    step2[...] = filt2[...] - learn_rate * sums2[:, :864]
    off2[...] = bias2[...] - learn_rate * column_to_row(sums2[:, 864:865])
    outs = [put_out(3), put_out(4)]
    copy1.wait_recv()
    sums1 = one_total[...]
    step1[...] = filt1[...] - learn_rate * sums1[:, :108]
    off1[...] = bias1[...] - learn_rate * column_to_row(sums1[:, 108:109])
    outs += [put_out(1), put_out(2)]

    for copy in started:
        copy.wait_send()
    feat_out.wait()
    for out in outs:
        out.wait()


def hand_on(*refs):
    ins, outs, spots, in_sems, out_sems = refs[:5], refs[5:10], refs[10:15], refs[15], refs[16]
    reads = [pltpu.make_async_copy(ins[n], spots[n], in_sems.at[n]) for n in range(5)]
    writes = [pltpu.make_async_copy(spots[n], outs[n], out_sems.at[n]) for n in range(5)]
    for copy in reads:
        copy.start()
    for n in (3, 0, 1, 2, 4):
        reads[n].wait()
        writes[n].start()
    for copy in writes:
        copy.wait()


def shards(volume, first_filters, first_bias, second_filters, second_bias, cotangent):
    GX, GY, GZ = lax.axis_size("gx"), lax.axis_size("gy"), lax.axis_size("gz")
    NX = 4 if GZ >= 8 else 2
    NZ = (GX // 2) * (GZ // NX)
    n2, n3 = 256 // NX, 256 // NX // GY
    operands = [
        volume, first_filters, first_bias.reshape(1, 32), second_filters, second_bias.reshape(1, 64),
        cotangent.transpose(1, 2, 3, 0).reshape(128, 64), jnp.asarray(PACKED),
    ]
    sems = 78 + 4 + 3 * (NX - 1) + 3 * (GY - 1) + 2 * (NZ - 1)
    V = pltpu.VMEM
    results = (
        jax.ShapeDtypeStruct((128, 64), bf16),
        jax.ShapeDtypeStruct((32, 108), f32),
        jax.ShapeDtypeStruct((1, 32), f32),
        jax.ShapeDtypeStruct((64, 864), f32),
        jax.ShapeDtypeStruct((1, 64), f32),
    )
    out = pl.pallas_call(
        functools.partial(kernel, (GX, GY, GZ, NX)),
        out_shape=results,
        in_specs=[pl.BlockSpec(memory_space=pltpu.HBM)] * len(operands),
        out_specs=[pl.BlockSpec(memory_space=pltpu.HBM)] * 5,
        scratch_shapes=[
            V((32, 128), bf16), V((2, 4, 16, 128), bf16), V((2, 16, 128), bf16), V((4, 16, 128), bf16),
            V((16, 128), bf16), V((2, 3, 3, 16, 128), bf16), V((64, 2, 16, 128), bf16), V((4, 8, 32, 256), f32),
            V((2, 8, 32, 128), bf16),
            V((2, 4, 32, 128), bf16), V((2, 4, 32, 128), bf16), V((2, 2, 32, 128), bf16), V((4, 32, 128), bf16),
            V((24, 32, 128), bf16), V((16, 128), bf16), V((2, 3, 3, 16, 128), bf16), V((24, 96, 128), bf16),
            V((2, 4, 64, 128), bf16), V((2, 4, 64, 128), bf16), V((2, 2, 64, 128), bf16), V((4, 64, 128), bf16),
            V((24, 64, 128), bf16), V((16, 128), bf16), V((2, 3, 3, 16, 128), bf16), V((24, 192, 128), bf16),
            V((32, 1792), bf16), V((2, 8, 32, 128), f32),
            V((512, 128), f32), V((256, 128), f32), V((256, 128), f32), V((NX - 1, n2, 128), f32),
            V((n2, 128), f32), V((GY - 1, n3, 128), f32), V((n3, 128), f32), V((NZ, n3, 128), f32),
            V((512, 128), f32),
            V((32, 128), f32), V((16, 128), f32), V((NX, 16, 128), f32), V((GY, 16, 128), f32),
            V((NZ, 16, 128), f32), V((32, 128), f32),
            pltpu.SemaphoreType.DMA((sems,)), pltpu.SemaphoreType.DMA((sems,)),
        ] + [V(a.shape, a.dtype) for a in operands] + [
            pltpu.SemaphoreType.DMA((len(operands),)),
        ] + [V(a.shape, a.dtype) for a in results] + [
            pltpu.SemaphoreType.DMA((5,)),
        ],
        compiler_params=pltpu.CompilerParams(
            collective_id=0, has_side_effects=True, vmem_limit_bytes=62 * 2**20
        ),
    )(*operands)
    out = pl.pallas_call(
        hand_on,
        out_shape=results,
        in_specs=[pl.BlockSpec(memory_space=pltpu.HBM)] * 5,
        out_specs=[pl.BlockSpec(memory_space=pltpu.HBM)] * 5,
        scratch_shapes=[V(a.shape, a.dtype) for a in results]
        + [pltpu.SemaphoreType.DMA((5,)), pltpu.SemaphoreType.DMA((5,))],
        compiler_params=pltpu.CompilerParams(vmem_limit_bytes=62 * 2**20),
    )(*out)
    features, stepped_first, offset_first, stepped_second, offset_second = out
    return (
        features.reshape(1, 4, 32, 64).transpose(3, 0, 1, 2), stepped_first, offset_first.reshape(32), stepped_second,
        offset_second.reshape(64),
    )


def solution(mesh):
    return jax.shard_map(
        shards,
        mesh=mesh,
        in_specs=(P(None, "gx", "gz", "gy"), P(), P(), P(), P(), P(None, "gx", "gz", "gy")),
        out_specs=(P(None, "gx", "gz", "gy"), P(), P(), P(), P()),
        check_vma=False,
    )
```

```python
import functools

import jax
import jax.numpy as jnp
import numpy as np
from jax import lax
from jax.experimental import pallas as pl
from jax.experimental.pallas import tpu as pltpu
from jax.sharding import PartitionSpec as P

slope_below = 0.3
learn_rate = 0.001
f32 = jnp.float32
bf16 = jnp.bfloat16
MESH = pl.DeviceIdType.MESH
NN = (((1,), (0,)), ((), ()))
NT = (((1,), (1,)), ((), ()))
TN = (((0,), (0,)), ((), ()))


def mm(a, b, dims=NN):
    return lax.dot_general(a, b, dims, preferred_element_type=f32)


def tables():
    place = np.zeros((512, 480))
    for wp in range(6):
        for dp in range(18):
            for ch in range(4):
                w, d = wp - 1, dp - 1
                inner_w, inner_d = 0 <= w < 4, 0 <= d < 16
                if inner_w and inner_d:
                    src = (ch * 4 + w) * 16 + d
                elif inner_d:
                    src = 256 + (64 if w > 0 else 0) + ch * 16 + d
                elif inner_w:
                    src = 384 + (16 if d > 0 else 0) + ch * 4 + w
                else:
                    a, b = int(w > 0), int(d > 0)
                    src = 416 + (a * 2 + b) * 16 + ch * 4 + (0 if a else 3)
                place[(wp * 18 + dp) * 4 + ch, src] = 1
    shift1 = np.zeros((128, 384))
    for l in range(128):
        if l:
            shift1[l - 1, l] = 1
        shift1[l, 128 + l] = 1
        if l < 127:
            shift1[l + 1, 256 + l] = 1
    order1 = np.zeros((1152, 128))
    for wp in range(6):
        for dp in range(18):
            a, b = (wp > 0) + (wp > 4), (dp > 0) + (dp > 16)
            w, d = (3, wp - 1, 0)[a], (15, dp - 1, 0)[b]
            order1[(a * 3 + b) * 128 + w * 16 + d, wp * 18 + dp] = 1
    four = np.zeros((128, 512))
    for q in range(512):
        four[q // 4, q] = 1
    put1 = np.zeros((32, 256))
    for ch in range(4):
        put1[ch * 2 + 1, 0] = put1[16 + ch * 2, 255] = 1
    shift2 = np.zeros((128, 384))
    swapped = np.zeros((128, 384))
    for l in range(128):
        for k in range(3):
            s = l % 64 + k - 1
            if 0 <= s < 64:
                s += l - l % 64
                shift2[s, k * 128 + l] = 1
                swapped[(s + 64) % 128, k * 128 + l] = 1
    ends = (0, 63, 64, 127)
    pick2 = np.zeros((16, 512))
    for dq in range(4):
        for n, l in enumerate(ends):
            pick2[dq * 4 + n, dq * 128 + l] = 1
    put2 = np.zeros((96, 1536))
    for dp in range(6):
        if dp == 0:
            near = ((0, 3, 1), (1, 3, 0))
        elif dp == 5:
            near = ((1, 0, 1), (2, 0, 0))
        else:
            near = ((1, dp - 1, 0), (1, dp - 1, 1))
        for half, (dz, dq, there) in enumerate(near):
            put2[dz * 16 + dq * 4 + 2 * there + 1, dp * 256 + 64 * half] = 1
            put2[48 + dz * 16 + dq * 4 + 2 * there, dp * 256 + 128 + 64 * half + 63] = 1
    even = np.zeros((256, 128))
    for half in range(2):
        for h in range(64):
            even[half * 128 + 2 * h, half * 64 + h] = 1
    twice = np.zeros((128, 256))
    for half in range(2):
        for h in range(128):
            twice[half * 64 + h // 2, half * 128 + h] = 1
    spread = np.zeros((128, 256))
    collect = np.zeros((256, 128))
    for dc in range(4):
        for hc in range(32):
            for t in range(2):
                spread[dc * 32 + hc, (dc % 2) * 128 + (dc // 2) * 64 + 2 * hc + t] = 1
            collect[(dc % 2) * 128 + dc * 32 + hc, (dc // 2) * 64 + 2 * hc] = 1
    widen = np.zeros((108, 144))
    narrow = np.zeros((144, 128))
    for q in range(108):
        widen[q, (q // 12) * 16 + q % 12] = 1
        narrow[(q // 12) * 16 + q % 12, q] = 1
    narrow[12, 108] = 1
    ident = np.zeros((64, 256))
    for o in range(64):
        ident[o, o] = ident[o, 128 + 64 + o] = 1
    every = dict(
        place=place, shift1=shift1, order1=order1, four=four, put1=put1, shift2=shift2, swapped=swapped,
        pick2=pick2, put2=put2, even=even, twice=twice, spread=spread, collect=collect,
        widen=widen, narrow=narrow, ident=ident,
    )
    return every


TABLE = {}


def packed_table():
    parts, row = [], 0
    for name, value in tables().items():
        rows, lanes = value.shape
        wide = np.zeros((-(-rows // 16) * 16, -(-lanes // 512) * 512))
        wide[:rows, :lanes] = value
        wide = np.concatenate(np.split(wide, wide.shape[1] // 512, axis=1))
        TABLE[name] = (row, rows, lanes)
        row += wide.shape[0]
        parts.append(wide)
    return np.concatenate(parts).astype(jnp.bfloat16)


PACKED = packed_table()


class Rows:
    def __init__(self, ref, name):
        self.ref = ref
        self.row, self.rows, self.lanes = TABLE[name]

    def __getitem__(self, key):
        if self.lanes > 512:
            step = -(-self.rows // 16) * 16
            return jnp.concatenate(
                [self.ref[self.row + n * step:self.row + n * step + self.rows, :] for n in range(self.lanes // 512)],
                axis=1,
            )
        if key is Ellipsis:
            return self.ref[self.row:self.row + self.rows, :self.lanes]
        return self.ref[self.row + key.start:self.row + key.stop, :self.lanes]


def row_to_column(row):
    n = row.shape[1]
    diagonal = lax.broadcasted_iota(jnp.int32, (n, n), 0) == lax.broadcasted_iota(jnp.int32, (n, n), 1)
    return jnp.sum(jnp.where(diagonal, jnp.broadcast_to(row, (n, n)), 0.0), axis=1, keepdims=True)


def column_to_row(column):
    n = column.shape[0]
    diagonal = lax.broadcasted_iota(jnp.int32, (n, n), 0) == lax.broadcasted_iota(jnp.int32, (n, n), 1)
    return jnp.sum(jnp.where(diagonal, jnp.broadcast_to(column, (n, n)), 0.0), axis=0, keepdims=True)


def kept(flag, value):
    return lax.select(flag, value, jnp.zeros_like(value))


def leaky(a):
    return jnp.where(a > 0, a, slope_below * a)


def slope(a):
    return jnp.where(a > 0, 1.0, slope_below)


def split3(a):
    high = a.astype(bf16)
    rest = a - high.astype(f32)
    mid = rest.astype(bf16)
    return high, mid, (rest - mid.astype(f32)).astype(bf16)


def kernel(sizes, *refs):
    GX, GY, GZ, NX = sizes
    ZL = GZ // NX
    ZH = GX // 2
    NZ = ZH * ZL
    far = refs[:7]
    refs = refs[7:]
    far_out = refs[:5]
    (
        edges, wide_in, deep_in, corner_in, col1, col1_in, xs, pre1, summed,
        pooled, wide2, deep2, corner2, v2, col2, col2_in, ys,
        errs, wide3, deep3, corner3, v3, col3, col3_in, fs, turned, perr,
        grads, core_in, red1, x_in, red2, y_in, red3, z_in, total,
        one, one_core, one_x, one_y, one_z, one_total, send_sems, recv_sems, vol, filt1, bias1, filt2, bias2, cot, packed, in_sems,
        feat, step1, off1, step2, off2, out_sems,
    ) = refs[5:]
    near = (vol, filt1, bias1, filt2, bias2, cot, packed)
    fetches = [pltpu.make_async_copy(a, b, in_sems.at[n]) for n, (a, b) in enumerate(zip(far, near))]
    for fetch in fetches:
        fetch.start()
    t = {name: Rows(packed, name) for name in TABLE}

    gx, gy, gz = lax.axis_index("gx"), lax.axis_index("gy"), lax.axis_index("gz")
    core, zh = lax.rem(gx, 2), lax.div(gx, 2)
    xc, zl = lax.rem(gz, NX), lax.div(gz, NX)
    zc = zh * ZL + zl

    def shifted(dx, dy, dz):
        return (lax.rem(gx + (dx + GX), GX), lax.rem(gy + (dy + GY), GY), lax.rem(gz + (dz + GZ), GZ))

    sibling = (gx + 1 - 2 * core, gy, gz)

    def x_peer(r):
        p = lax.rem(xc + r, NX)
        return p, (gx, gy, zl * NX + p)

    def y_peer(r):
        p = lax.rem(gy + r, GY)
        return p, (gx, p, gz)

    def z_peer(r):
        p = lax.rem(zc + r, NZ)
        return (2 * lax.div(p, ZL) + core, gy, lax.rem(p, ZL) * NX + xc)

    square = [(dx, dz) for dx in (-1, 0, 1) for dz in (-1, 0, 1)]
    peers = [shifted(dx, 0, dz) for dx, dz in square if (dx, dz) != (0, 0)]
    peers += [shifted(dx, dy, dz) for dx, dz in square for dy in (-1, 1)]
    peers += [x_peer(r)[1] for r in range(1, NX)]
    peers += [y_peer(r)[1] for r in range(1, GY)]
    peers += [z_peer(r) for r in range(1, NZ)]
    barrier = pltpu.get_barrier_semaphore()
    for peer in peers:
        pl.semaphore_signal(barrier, inc=1, device_id=peer, device_id_type=MESH)

    count = [0]
    started = []

    def send(src, dst, device):
        n = count[0]
        count[0] += 1
        copy = pltpu.make_async_remote_copy(
            src_ref=src, dst_ref=dst, send_sem=send_sems.at[n], recv_sem=recv_sems.at[n],
            device_id=device, device_id_type=MESH,
        )
        copy.start()
        started.append(copy)
        return copy

    def put_out(n):
        copy = pltpu.make_async_copy((feat, step1, off1, step2, off2)[n], far_out[n], out_sems.at[n])
        copy.start()
        return copy

    def arrive(copies):
        for copy in copies:
            copy.wait_recv()

    row = lax.broadcasted_iota(jnp.int32, (32, 256), 0)
    column = lax.broadcasted_iota(jnp.int32, (32, 256), 1)
    wanted = jnp.where(row < 16, row * 16, row * 16 - 241)
    edge = jnp.where(column == wanted, 1.0, 0.0).astype(bf16)
    fetches[0].wait()
    block = vol[...].reshape(256, 128)
    edges[...] = mm(edge, block).astype(bf16)
    pl.semaphore_wait(barrier, len(peers))

    has_left, has_right = gx > 0, gx < GX - 1
    has_front, has_back = gz > 0, gz < GZ - 1
    has_below, has_above = gy > 0, gy < GY - 1

    def send_ring(wide_src, wide_dst, deep_src, deep_dst, corner_src, corner_dst):
        copies = []
        for a in range(2):
            dx = 1 if a == 0 else -1
            copies.append(send(wide_src(a), wide_dst.at[a], shifted(dx, 0, 0)))
        for b in range(2):
            dz = 1 if b == 0 else -1
            copies.append(send(deep_src(b), deep_dst.at[b], shifted(0, 0, dz)))
        for a in range(2):
            for b in range(2):
                copies.append(
                    send(corner_src(a, b), corner_dst.at[a * 2 + b], shifted(1 if a == 0 else -1, 0, 1 if b == 0 else -1))
                )
        return copies

    def send_columns(src, dst):
        copies = []
        for dx, dz in square:
            for side in range(2):
                dy = 1 if side == 0 else -1
                copies.append(send(src, dst.at[side, 1 - dx, 1 - dz], shifted(dx, dy, dz)))
        return copies

    def columns_in(dst, dx):
        rows = []
        for side in range(2):
            for dz in (-1, 0, 1):
                flag = (has_below, has_above)[side]
                if dx:
                    flag = jnp.logical_and(flag, edge_flags[(dx + 1) // 2])
                if dz:
                    flag = jnp.logical_and(flag, deep_flags[(dz + 1) // 2])
                rows.append(kept(flag, dst[side, dx + 1, dz + 1]))
        return rows

    edge_flags = (has_left, has_right)
    deep_flags = (has_front, has_back)

    def edge_rows(b):
        return edges.at[pl.ds(16, 16)] if b == 0 else edges.at[pl.ds(0, 16)]

    copies = send_ring(
        lambda a: vol.at[:, 3] if a == 0 else vol.at[:, 0], wide_in,
        edge_rows, deep_in, lambda a, b: edge_rows(b), corner_in,
    )

    row = lax.broadcasted_iota(jnp.int32, (16, 512), 0)
    column = lax.broadcasted_iota(jnp.int32, (16, 512), 1)
    wanted = jnp.where(row < 8, lax.div(row, 2) * 128 + lax.rem(row, 2) * 127, -1)
    pick1 = jnp.where(column == wanted, 1.0, 0.0).astype(bf16)
    ends = sum(
        mm(pick1[:, 128 * ch:128 * ch + 128], vol[ch].reshape(64, 128), NT) for ch in range(4)
    )
    col1[...] = jnp.concatenate([ends, jnp.zeros((16, 64), f32)], axis=1).astype(bf16)
    copies_c = send_columns(col1, col1_in)
    for fetch in fetches[1:]:
        fetch.wait()
    first_half = filt1[...].astype(bf16)
    wide_first = mm(first_half, t["widen"][...]).astype(bf16)
    bias1_col = row_to_column(bias1[...])
    bias2_col = row_to_column(bias2[...])
    second_half = filt2[...].astype(bf16)

    turn = mm(second_half, t["ident"][...], TN).astype(bf16)
    for m in range(13):
        low = turn[64 * m:64 * m + 32, :128].astype(f32)
        high = turn[64 * m + 32:64 * m + 64, 128:].astype(f32)
        turned[:, 128 * m:128 * m + 128] = (low + high).astype(bf16)
    turned[:, 1664:1792] = turn[832:864, :128]
    spread_cot = mm(cot[...], t["spread"][...], TN) * 0.125

    arrive(copies)
    pieces = [block]
    for a in range(2):
        pieces.append(kept(edge_flags[a], wide_in[a]).reshape(64, 128))
    for b in range(2):
        pieces.append(kept(deep_flags[b], deep_in[b]))
    for a in range(2):
        for b in range(2):
            pieces.append(kept(jnp.logical_and(edge_flags[a], deep_flags[b]), corner_in[a * 2 + b]))
    rows = mm(t["place"][...], jnp.concatenate(pieces, axis=0)).astype(bf16)
    inner = mm(rows, t["shift1"][...])
    arrive(copies_c)
    columns = [columns_in(col1_in, dx) for dx in (-1, 0, 1)]
    sides = [
        jnp.concatenate([columns[a][side * 3 + b] for a in range(3) for b in range(3)], axis=1)
        for side in range(2)
    ]
    ordered = mm(jnp.concatenate(sides, axis=0), t["order1"][...]).astype(bf16)
    ordered = mm(ordered, t["four"][...])
    row = lax.broadcasted_iota(jnp.int32, (32, 512), 0)
    column = lax.broadcasted_iota(jnp.int32, (32, 512), 1)
    same = lax.rem(lax.div(row, 2), 8) == lax.rem(column, 4)
    ordered = jnp.where(same, ordered, 0.0).astype(bf16)
    ends = mm(ordered, t["put1"][...], TN)
    full = [inner[:, :128] + ends[:, :128], inner[:, 128:256], inner[:, 256:] + ends[:, 128:]]
    third = [piece.reshape(64, 8, 128) for piece in full]
    rolled = [pltpu.roll(piece, 4, axis=1) for piece in third]
    sub = lax.broadcasted_iota(jnp.int32, (64, 8, 128), 1)
    upper = sub < 4
    ones = jnp.where(sub == 4, 1.0, 0.0)
    even_tile = jnp.concatenate(
        [jnp.where(upper, third[0], rolled[1]), jnp.where(upper, third[2], ones)], axis=1
    )
    odd_tile = jnp.concatenate(
        [jnp.where(upper, rolled[0], third[1]), jnp.where(upper, rolled[2], ones)], axis=1
    )
    xs[:, 0] = even_tile.astype(bf16)
    xs[:, 1] = odd_tile.astype(bf16)

    def cols1(w, half_d):
        def at(i, dp, parity):
            return xs[(w + i) * 9 + dp, parity]

        one = [at(i, half_d + j // 2, j % 2) for i in range(3) for j in range(3)]
        two = [at(i, half_d + (j + 1) // 2, (j + 1) % 2) for i in range(3) for j in range(3)]
        return jnp.concatenate(
            [jnp.concatenate(one, axis=0), jnp.concatenate(two, axis=0)], axis=1
        )

    def forward1(pd, carry):
        for pw in range(2):
            part = None
            for w in (2 * pw, 2 * pw + 1):
                pre = mm(wide_first, cols1(w, pd)) + bias1_col
                pre1[w, pd] = pre
                act = leaky(pre)
                act = act[:, :128] + act[:, 128:]
                part = act if part is None else part + act
            part = (part + pltpu.roll(part, 127, axis=1)) * 0.125
            summed[pw, pd] = part.astype(bf16)
        return carry

    lax.fori_loop(0, 8, forward1, 0)
    pooled_val = (
        mm(summed[:, 0:4].reshape(256, 128), t["even"][0:128])
        + mm(summed[:, 4:8].reshape(256, 128), t["even"][128:256])
    ).astype(bf16)
    pooled[...] = pooled_val.reshape(2, 4, 32, 128)

    def assemble(own, wide, deep, corner, v, n):
        left = [kept(edge_flags[a], wide[a]) for a in range(2)]
        v[0:4] = left[0]
        v[4:8] = own[0]
        v[8:12] = own[1]
        v[12:16] = left[1]
        low = lax.broadcasted_iota(jnp.int32, (n, 128), 1) < 64
        for wp in range(4):
            if wp == 0 or wp == 3:
                a = 0 if wp == 0 else 1
                near = left[a]
                far = [
                    kept(jnp.logical_and(edge_flags[a], deep_flags[b]), corner[a * 2 + b]) for b in range(2)
                ]
            else:
                near = own[wp - 1]
                far = [kept(deep_flags[b], deep[b, wp - 1]) for b in range(2)]
            v[16 + wp] = jnp.where(low, near[3].astype(f32), far[0].astype(f32)).astype(bf16)
            v[20 + wp] = jnp.where(low, far[1].astype(f32), near[0].astype(f32)).astype(bf16)

    def halo(own, wide, deep, corner, v, col, col_in, out, n, flipped, meanwhile, between):
        copies = send_ring(
            lambda a: own.at[1 - a], wide,
            lambda b: own.at[:, 3 if b == 0 else 0], deep,
            lambda a, b: own.at[1 - a, 3 if b == 0 else 0], corner,
        )
        pick = t["pick2"][...]
        ends = sum(
            mm(pick[:, 128 * dq:128 * dq + 128], own[:, dq].reshape(2 * n, 128), NT) for dq in range(4)
        )
        if n < 64:
            ends = jnp.concatenate([ends, jnp.zeros((16, 128 - 2 * n), f32)], axis=1)
        col[...] = ends.astype(bf16)
        copies_c = send_columns(col, col_in)
        result = meanwhile()
        arrive(copies)
        assemble(own, wide, deep, corner, v, n)
        main = v[0:16].reshape(16 * n, 128)
        side = v[16:24].reshape(8 * n, 128)
        inner = jnp.concatenate([mm(main, t["shift2"][...]), mm(side, t["swapped"][...])], axis=0)
        result = between(result)
        arrive(copies_c)
        put = t["put2"][...]
        edge = [mm(jnp.concatenate(columns_in(col_in, dx), axis=0), put, TN) for dx in (-1, 0, 1)]
        for wp in range(4):
            far, w = ((0, 1), (1, 0), (1, 1), (2, 0))[wp]
            for dp in range(6):
                number = tile(wp, dp)
                for k in range(3):
                    piece = inner[number * n:number * n + n, 128 * k:128 * k + 128]
                    if k != 1:
                        lane = dp * 256 + 64 * k
                        piece = piece + edge[far][w * n:w * n + n, lane:lane + 128]
                    place = 2 - k if flipped else k
                    out[number, place * n:place * n + n, :] = piece.astype(bf16)
        return result

    def tile(wp, dp):
        if dp == 0:
            return 16 + wp
        if dp == 5:
            return 20 + wp
        return wp * 4 + dp - 1

    halo(pooled, wide2, deep2, corner2, v2, col2, col2_in, ys, 32, False, lambda: None, lambda a: a)

    def cols2(w, dq, extra):
        taps = [ys[tile(w + i, dq + j)] for i in range(3) for j in range(3)]
        return jnp.concatenate(taps + extra, axis=0)

    feat_sum = [None, None]
    for dq in range(4):
        cols = jnp.concatenate([cols2(0, dq, []), cols2(1, dq, [])], axis=1)
        pre = mm(second_half, cols) + bias2_col
        act = leaky(pre)
        act = act[:, :128] + act[:, 128:]
        pair = dq // 2
        feat_sum[pair] = act if feat_sum[pair] is None else feat_sum[pair] + act
        cot_here = spread_cot[:, 128 * pair:128 * pair + 128]
        err = (jnp.concatenate([cot_here, cot_here], axis=1) * slope(pre)).astype(bf16)
        errs[0, dq] = err[:, :128]
        errs[1, dq] = err[:, 128:]

    def second_half_grads():
        ends = [
            ((both + pltpu.roll(both, 127, axis=1)) * 0.125).astype(bf16) for both in feat_sum
        ]
        feat[...] = (mm(t["collect"][0:128], ends[0], NT) + mm(t["collect"][128:256], ends[1], NT)).astype(bf16)
        ones_rows = [jnp.ones((32, 128), bf16)]
        grad2 = None
        for dq in range(4):
            cols = jnp.concatenate([cols2(0, dq, ones_rows), cols2(1, dq, ones_rows)], axis=1)
            err = jnp.concatenate([errs[0, dq], errs[1, dq]], axis=1)
            piece = mm(err, cols, NT)
            grad2 = piece if grad2 is None else grad2 + piece
        for l in range(7):
            grads[l * 64:l * 64 + 64] = grad2[:, 128 * l:128 * l + 128]
        grads[448:512] = jnp.zeros((64, 128), f32)
        return put_out(0), sum_core(send(part(grads, 1 - core, n1), core_in, sibling))

    def part(ref, index, size):
        return ref.at[pl.ds(pl.multiple_of(index * size, size), size)]

    n1, n2, n3 = 256, 256 // NX, 256 // NX // GY

    def sum_core(copy):
        copy.wait_recv()
        red1[...] = part(grads, core, n1)[...] + core_in[...]
        return [send(part(red1, x_peer(r)[0], n2), x_in.at[r - 1], x_peer(r)[1]) for r in range(1, NX)]

    def sum_x(copies):
        arrive(copies)
        acc = part(red1, xc, n2)[...]
        for r in range(1, NX):
            acc = acc + x_in[r - 1]
        red2[...] = acc
        return [send(part(red2, y_peer(r)[0], n3), y_in.at[r - 1], y_peer(r)[1]) for r in range(1, GY)]

    def sum_y(copies):
        arrive(copies)
        acc = part(red2, gy, n3)[...]
        for r in range(1, GY):
            acc = acc + y_in[r - 1]
        red3[...] = acc
        z_in[zc] = acc
        return [send(red3, z_in.at[zc], z_peer(r)) for r in range(1, NZ)]

    def sum_z(copies):
        arrive(copies)
        acc = z_in[0]
        for r in range(1, NZ):
            acc = acc + z_in[r]
        mine = part(total, (core * NX + xc) * GY + gy, n3)
        mine[...] = acc
        return [send(mine, mine, y_peer(r)[1]) for r in range(1, GY)]

    def gather_x(copies):
        arrive(copies)
        mine = part(total, core * NX + xc, n2)
        return [send(mine, mine, x_peer(r)[1]) for r in range(1, NX)]

    def gather_core(copies):
        arrive(copies)
        mine = part(total, core, n1)
        return send(mine, mine, sibling)

    def everyone(value, slots, index, devices):
        slots[index] = value
        return [send(slots.at[index], slots.at[index], device) for device in devices]

    def summed_slots(copies, slots):
        arrive(copies)
        acc = slots[0]
        for n in range(1, slots.shape[0]):
            acc = acc + slots[n]
        return acc

    feat_out, copies2 = halo(
        errs, wide3, deep3, corner3, v3, col3, col3_in, fs, 64, True, second_half_grads,
        lambda a: (a[0], sum_x(a[1])),
    )

    for dq in range(4):
        def cols3(w):
            taps = [fs[tile(w + 2 - i, dq + 2 - j)] for i in range(3) for j in range(3)]
            return jnp.concatenate(taps + [jnp.zeros((64, 128), bf16)], axis=0)

        cols = jnp.concatenate([cols3(0), cols3(1)], axis=1)
        pe = mm(turned[...], cols).astype(bf16)
        both = mm(jnp.concatenate([pe[:, :128], pe[:, 128:]], axis=0), t["twice"][...]) * 0.125
        for w in range(2):
            perr[w, dq] = both[32 * w:32 * w + 32, :128]
            perr[w, dq + 4] = both[32 * w:32 * w + 32, 128:]

    copies2 = sum_y(copies2)

    def backward1(pd, acc):
        for w in range(4):
            here = perr[w // 2, pd]
            err = (jnp.concatenate([here, here], axis=1) * slope(pre1[w, pd])).astype(bf16)
            acc = acc + mm(err, cols1(w, pd), NT)
        return acc

    grad1 = lax.fori_loop(0, 8, backward1, jnp.zeros((32, 144), f32))
    one[...] = sum(mm(piece, t["narrow"][...]) for piece in split3(grad1))
    copies1 = send(part(one, 1 - core, 16), one_core, sibling)
    copies1.wait_recv()
    copies1 = everyone(part(one, core, 16)[...] + one_core[...], one_x, xc, [x_peer(r)[1] for r in range(1, NX)])
    copies2 = sum_z(copies2)
    copies1 = everyone(summed_slots(copies1, one_x), one_y, gy, [y_peer(r)[1] for r in range(1, GY)])
    copies2 = gather_x(copies2)
    copies1 = everyone(summed_slots(copies1, one_y), one_z, zc, [z_peer(r) for r in range(1, NZ)])
    copy2 = gather_core(copies2)
    copy2.wait_recv()
    sums2 = jnp.concatenate([total[l * 64:l * 64 + 64] for l in range(7)], axis=1)
    step2[...] = filt2[...] - learn_rate * sums2[:, :864]
    off2[...] = bias2[...] - learn_rate * column_to_row(sums2[:, 864:865])
    outs = [put_out(3), put_out(4)]
    mine = part(one_total, core, 16)
    mine[...] = summed_slots(copies1, one_z)
    copy1 = send(mine, mine, sibling)
    copy1.wait_recv()
    sums1 = one_total[...]
    step1[...] = filt1[...] - learn_rate * sums1[:, :108]
    off1[...] = bias1[...] - learn_rate * column_to_row(sums1[:, 108:109])
    outs += [put_out(1), put_out(2)]

    for copy in started:
        copy.wait_send()
    feat_out.wait()
    for out in outs:
        out.wait()


def hand_on(*refs):
    ins, outs, spots, in_sems, out_sems = refs[:5], refs[5:10], refs[10:15], refs[15], refs[16]
    reads = [pltpu.make_async_copy(ins[n], spots[n], in_sems.at[n]) for n in range(5)]
    writes = [pltpu.make_async_copy(spots[n], outs[n], out_sems.at[n]) for n in range(5)]
    for copy in reads:
        copy.start()
    for n in (3, 0, 1, 2, 4):
        reads[n].wait()
        writes[n].start()
    for copy in writes:
        copy.wait()


def shards(volume, first_filters, first_bias, second_filters, second_bias, cotangent):
    GX, GY, GZ = lax.axis_size("gx"), lax.axis_size("gy"), lax.axis_size("gz")
    NX = 4 if GZ >= 8 else 2
    NZ = (GX // 2) * (GZ // NX)
    n2, n3 = 256 // NX, 256 // NX // GY
    operands = [
        volume, first_filters, first_bias.reshape(1, 32), second_filters, second_bias.reshape(1, 64),
        cotangent.transpose(1, 2, 3, 0).reshape(128, 64), jnp.asarray(PACKED),
    ]
    sems = 78 + 4 + 3 * (NX - 1) + 3 * (GY - 1) + 2 * (NZ - 1)
    V = pltpu.VMEM
    results = (
        jax.ShapeDtypeStruct((128, 64), bf16),
        jax.ShapeDtypeStruct((32, 108), f32),
        jax.ShapeDtypeStruct((1, 32), f32),
        jax.ShapeDtypeStruct((64, 864), f32),
        jax.ShapeDtypeStruct((1, 64), f32),
    )
    out = pl.pallas_call(
        functools.partial(kernel, (GX, GY, GZ, NX)),
        out_shape=results,
        in_specs=[pl.BlockSpec(memory_space=pltpu.HBM)] * len(operands),
        out_specs=[pl.BlockSpec(memory_space=pltpu.HBM)] * 5,
        scratch_shapes=[
            V((32, 128), bf16), V((2, 4, 16, 128), bf16), V((2, 16, 128), bf16), V((4, 16, 128), bf16),
            V((16, 128), bf16), V((2, 3, 3, 16, 128), bf16), V((64, 2, 16, 128), bf16), V((4, 8, 32, 256), f32),
            V((2, 8, 32, 128), bf16),
            V((2, 4, 32, 128), bf16), V((2, 4, 32, 128), bf16), V((2, 2, 32, 128), bf16), V((4, 32, 128), bf16),
            V((24, 32, 128), bf16), V((16, 128), bf16), V((2, 3, 3, 16, 128), bf16), V((24, 96, 128), bf16),
            V((2, 4, 64, 128), bf16), V((2, 4, 64, 128), bf16), V((2, 2, 64, 128), bf16), V((4, 64, 128), bf16),
            V((24, 64, 128), bf16), V((16, 128), bf16), V((2, 3, 3, 16, 128), bf16), V((24, 192, 128), bf16),
            V((32, 1792), bf16), V((2, 8, 32, 128), f32),
            V((512, 128), f32), V((256, 128), f32), V((256, 128), f32), V((NX - 1, n2, 128), f32),
            V((n2, 128), f32), V((GY - 1, n3, 128), f32), V((n3, 128), f32), V((NZ, n3, 128), f32),
            V((512, 128), f32),
            V((32, 128), f32), V((16, 128), f32), V((NX, 16, 128), f32), V((GY, 16, 128), f32),
            V((NZ, 16, 128), f32), V((32, 128), f32),
            pltpu.SemaphoreType.DMA((sems,)), pltpu.SemaphoreType.DMA((sems,)),
        ] + [V(a.shape, a.dtype) for a in operands] + [
            pltpu.SemaphoreType.DMA((len(operands),)),
        ] + [V(a.shape, a.dtype) for a in results] + [
            pltpu.SemaphoreType.DMA((5,)),
        ],
        compiler_params=pltpu.CompilerParams(
            collective_id=0, has_side_effects=True, vmem_limit_bytes=62 * 2**20
        ),
    )(*operands)
    out = pl.pallas_call(
        hand_on,
        out_shape=results,
        in_specs=[pl.BlockSpec(memory_space=pltpu.HBM)] * 5,
        out_specs=[pl.BlockSpec(memory_space=pltpu.HBM)] * 5,
        scratch_shapes=[V(a.shape, a.dtype) for a in results]
        + [pltpu.SemaphoreType.DMA((5,)), pltpu.SemaphoreType.DMA((5,))],
        compiler_params=pltpu.CompilerParams(vmem_limit_bytes=62 * 2**20),
    )(*out)
    features, stepped_first, offset_first, stepped_second, offset_second = out
    return (
        features.reshape(1, 4, 32, 64).transpose(3, 0, 1, 2), stepped_first, offset_first.reshape(32), stepped_second,
        offset_second.reshape(64),
    )


def solution(mesh):
    return jax.shard_map(
        shards,
        mesh=mesh,
        in_specs=(P(None, "gx", "gz", "gy"), P(), P(), P(), P(), P(None, "gx", "gz", "gy")),
        out_specs=(P(None, "gx", "gz", "gy"), P(), P(), P(), P()),
        check_vma=False,
    )
```

```python
import functools

import jax
import jax.numpy as jnp
import numpy as np
from jax import lax
from jax.experimental import pallas as pl
from jax.experimental.pallas import tpu as pltpu
from jax.sharding import PartitionSpec as P

slope_below = 0.3
learn_rate = 0.001
f32 = jnp.float32
bf16 = jnp.bfloat16
MESH = pl.DeviceIdType.MESH
NN = (((1,), (0,)), ((), ()))
NT = (((1,), (1,)), ((), ()))
TN = (((0,), (0,)), ((), ()))


def mm(a, b, dims=NN):
    return lax.dot_general(a, b, dims, preferred_element_type=f32)


def tables():
    place = np.zeros((512, 480))
    for wp in range(6):
        for dp in range(18):
            for ch in range(4):
                w, d = wp - 1, dp - 1
                inner_w, inner_d = 0 <= w < 4, 0 <= d < 16
                if inner_w and inner_d:
                    src = (ch * 4 + w) * 16 + d
                elif inner_d:
                    src = 256 + (64 if w > 0 else 0) + ch * 16 + d
                elif inner_w:
                    src = 384 + (16 if d > 0 else 0) + ch * 4 + w
                else:
                    a, b = int(w > 0), int(d > 0)
                    src = 416 + (a * 2 + b) * 16 + ch * 4 + (0 if a else 3)
                place[(wp * 18 + dp) * 4 + ch, src] = 1
    shift1 = np.zeros((128, 384))
    for l in range(128):
        if l:
            shift1[l - 1, l] = 1
        shift1[l, 128 + l] = 1
        if l < 127:
            shift1[l + 1, 256 + l] = 1
    order1 = np.zeros((1152, 128))
    for wp in range(6):
        for dp in range(18):
            a, b = (wp > 0) + (wp > 4), (dp > 0) + (dp > 16)
            w, d = (3, wp - 1, 0)[a], (15, dp - 1, 0)[b]
            order1[(a * 3 + b) * 128 + w * 16 + d, wp * 18 + dp] = 1
    four = np.zeros((128, 512))
    for q in range(512):
        four[q // 4, q] = 1
    put1 = np.zeros((32, 256))
    for ch in range(4):
        put1[ch * 2 + 1, 0] = put1[16 + ch * 2, 255] = 1
    shift2 = np.zeros((128, 384))
    swapped = np.zeros((128, 384))
    for l in range(128):
        for k in range(3):
            s = l % 64 + k - 1
            if 0 <= s < 64:
                s += l - l % 64
                shift2[s, k * 128 + l] = 1
                swapped[(s + 64) % 128, k * 128 + l] = 1
    ends = (0, 63, 64, 127)
    pick2 = np.zeros((16, 512))
    for dq in range(4):
        for n, l in enumerate(ends):
            pick2[dq * 4 + n, dq * 128 + l] = 1
    put2 = np.zeros((96, 2048))
    for dq in range(-2, 6):
        for half in range(2):
            d = dq + 4 * half
            dz = (d >= 0) + (d > 7)
            there, row = (d % 8) // 4, (d % 4) * 4
            put2[dz * 16 + row + 2 * there + 1, (dq + 2) * 256 + 64 * half] = 1
            put2[48 + dz * 16 + row + 2 * there, (dq + 2) * 256 + 128 + 64 * half + 63] = 1
    pick3 = np.zeros((32, 768))
    put3 = np.zeros((64, 1536))
    for dq in range(6):
        for n, l in enumerate(ends):
            pick3[dq * 4 + n, dq * 128 + l] = 1
        for half in range(2):
            put3[dq * 4 + 2 * half + 1, dq * 256 + 64 * half] = 1
            put3[32 + dq * 4 + 2 * half, dq * 256 + 128 + 64 * half + 63] = 1
    even = np.zeros((256, 128))
    for half in range(2):
        for h in range(64):
            even[half * 128 + 2 * h, half * 64 + h] = 1
    twice = np.zeros((128, 256))
    for half in range(2):
        for h in range(128):
            twice[half * 64 + h // 2, half * 128 + h] = 1
    spread = np.zeros((192, 512))
    for dc in range(-1, 5):
        for hc in range(32):
            row = (128 if dc < 0 else 160 if dc > 3 else dc * 32) + hc
            for t in range(2):
                for half in range(2):
                    kind = {0: 0, 1: 1, -1: 2, 2: 3}.get(dc - 2 * half)
                    if kind is not None:
                        spread[row, kind * 128 + half * 64 + 2 * hc + t] = 1
    collect = np.zeros((256, 128))
    for dc in range(4):
        for hc in range(32):
            collect[(dc % 2) * 128 + dc * 32 + hc, (dc // 2) * 64 + 2 * hc] = 1
    widen = np.zeros((108, 144))
    narrow = np.zeros((144, 128))
    for q in range(108):
        widen[q, (q // 12) * 16 + q % 12] = 1
        narrow[(q // 12) * 16 + q % 12, q] = 1
    narrow[12, 108] = 1
    ident = np.zeros((64, 256))
    for o in range(64):
        ident[o, o] = ident[o, 128 + 64 + o] = 1
    every = dict(
        place=place, shift1=shift1, order1=order1, four=four, put1=put1, shift2=shift2, swapped=swapped,
        pick2=pick2, put2=put2, pick3=pick3, put3=put3, even=even, twice=twice, spread=spread, collect=collect,
        widen=widen, narrow=narrow, ident=ident,
    )
    return every


TABLE = {}


def packed_table():
    parts, row = [], 0
    for name, value in tables().items():
        rows, lanes = value.shape
        if name == "order1":
            value = np.concatenate(np.split(value, 4), axis=1)
            rows //= 4
        wide = np.zeros((-(-rows // 16) * 16, -(-lanes // 512) * 512))
        wide[:rows, :value.shape[1]] = value
        wide = np.concatenate(np.split(wide, wide.shape[1] // 512, axis=1))
        TABLE[name] = (row, rows, lanes)
        row += wide.shape[0]
        parts.append(wide)
    return np.concatenate(parts).astype(jnp.bfloat16)


PACKED = packed_table()


class Rows:
    def __init__(self, ref, name):
        self.ref = ref
        self.row, self.rows, self.lanes = TABLE[name]

    def folded(self):
        return jnp.concatenate(
            [self.ref[self.row:self.row + self.rows, 128 * n:128 * n + 128] for n in range(4)], axis=0
        )

    def __getitem__(self, key):
        if self.lanes > 512:
            step = -(-self.rows // 16) * 16
            return jnp.concatenate(
                [self.ref[self.row + n * step:self.row + n * step + self.rows, :] for n in range(-(-self.lanes // 512))],
                axis=1,
            )
        if key is Ellipsis:
            return self.ref[self.row:self.row + self.rows, :self.lanes]
        return self.ref[self.row + key.start:self.row + key.stop, :self.lanes]


def row_to_column(row):
    n = row.shape[1]
    diagonal = lax.broadcasted_iota(jnp.int32, (n, n), 0) == lax.broadcasted_iota(jnp.int32, (n, n), 1)
    return jnp.sum(jnp.where(diagonal, jnp.broadcast_to(row, (n, n)), 0.0), axis=1, keepdims=True)


def column_to_row(column):
    n = column.shape[0]
    diagonal = lax.broadcasted_iota(jnp.int32, (n, n), 0) == lax.broadcasted_iota(jnp.int32, (n, n), 1)
    return jnp.sum(jnp.where(diagonal, jnp.broadcast_to(column, (n, n)), 0.0), axis=0, keepdims=True)


def kept(flag, value):
    return lax.select(flag, value, jnp.zeros_like(value))


def leaky(a):
    return jnp.where(a > 0, a, slope_below * a)


def slope(a):
    return jnp.where(a > 0, 1.0, slope_below)


def split3(a):
    high = a.astype(bf16)
    rest = a - high.astype(f32)
    mid = rest.astype(bf16)
    return high, mid, (rest - mid.astype(f32)).astype(bf16)


def kernel(sizes, *refs):
    GX, GY, GZ, NX = sizes
    ZL = GZ // NX
    ZH = GX // 2
    NZ = ZH * ZL
    far = refs[:7]
    refs = refs[7:]
    far_out = refs[:5]
    (
        edges, wide_in, deep_in, corner_in, col1, col1_in, xs, pre1, summed,
        wide_t, deep_t, corner_t, pooled, packs, wide2, deep2, corner2, v2, col2, col2_in, ys,
        errs, col3, col3_in, fs, turned, perr,
        grads, core_in, red1, x_in, red2, y_in, red3, z_in, total,
        one, one_core, one_x, one_y, one_z, one_total, send_sems, recv_sems, vol, filt1, bias1, filt2, bias2, cot, packed, in_sems,
        feat, step1, off1, step2, off2, out_sems,
    ) = refs[5:]
    near = (vol, filt1, bias1, filt2, bias2, cot, packed)
    fetches = [pltpu.make_async_copy(a, b, in_sems.at[n]) for n, (a, b) in enumerate(zip(far, near))]
    for fetch in fetches:
        fetch.start()
    t = {name: Rows(packed, name) for name in TABLE}

    gx, gy, gz = lax.axis_index("gx"), lax.axis_index("gy"), lax.axis_index("gz")
    core, zh = lax.rem(gx, 2), lax.div(gx, 2)
    xc, zl = lax.rem(gz, NX), lax.div(gz, NX)
    zc = zh * ZL + zl

    def shifted(dx, dy, dz):
        return (lax.rem(gx + (dx + GX), GX), lax.rem(gy + (dy + GY), GY), lax.rem(gz + (dz + GZ), GZ))

    sibling = (gx + 1 - 2 * core, gy, gz)

    def x_peer(r):
        p = lax.rem(xc + r, NX)
        return p, (gx, gy, zl * NX + p)

    def y_peer(r):
        p = lax.rem(gy + r, GY)
        return p, (gx, p, gz)

    def z_peer(r):
        p = lax.rem(zc + r, NZ)
        return (2 * lax.div(p, ZL) + core, gy, lax.rem(p, ZL) * NX + xc)

    square = [(dx, dz) for dx in (-1, 0, 1) for dz in (-1, 0, 1)]
    peers = [shifted(dx, 0, dz) for dx, dz in square if (dx, dz) != (0, 0)]
    peers += [shifted(dx, dy, dz) for dx, dz in square for dy in (-1, 1)]
    peers += [x_peer(r)[1] for r in range(1, NX)]
    peers += [y_peer(r)[1] for r in range(1, GY)]
    peers += [z_peer(r) for r in range(1, NZ)]
    barrier = pltpu.get_barrier_semaphore()
    for peer in peers:
        pl.semaphore_signal(barrier, inc=1, device_id=peer, device_id_type=MESH)

    count = [0]
    started = []

    def send(src, dst, device):
        n = count[0]
        count[0] += 1
        copy = pltpu.make_async_remote_copy(
            src_ref=src, dst_ref=dst, send_sem=send_sems.at[n], recv_sem=recv_sems.at[n],
            device_id=device, device_id_type=MESH,
        )
        copy.start()
        started.append(copy)
        return copy

    def put_out(n):
        copy = pltpu.make_async_copy((feat, step1, off1, step2, off2)[n], far_out[n], out_sems.at[n])
        copy.start()
        return copy

    def arrive(copies):
        for copy in copies:
            copy.wait_recv()

    row = lax.broadcasted_iota(jnp.int32, (32, 256), 0)
    column = lax.broadcasted_iota(jnp.int32, (32, 256), 1)
    wanted = jnp.where(row < 16, row * 16, row * 16 - 241)
    edge = jnp.where(column == wanted, 1.0, 0.0).astype(bf16)
    fetches[0].wait()
    block = vol[...].reshape(256, 128)
    edges[...] = mm(edge, block).astype(bf16)
    pl.semaphore_wait(barrier, len(peers))

    has_left, has_right = gx > 0, gx < GX - 1
    has_front, has_back = gz > 0, gz < GZ - 1
    has_below, has_above = gy > 0, gy < GY - 1

    def send_ring(wide_src, wide_dst, deep_src, deep_dst, corner_src, corner_dst):
        copies = []
        for a in range(2):
            dx = 1 if a == 0 else -1
            copies.append(send(wide_src(a), wide_dst.at[a], shifted(dx, 0, 0)))
        for b in range(2):
            dz = 1 if b == 0 else -1
            copies.append(send(deep_src(b), deep_dst.at[b], shifted(0, 0, dz)))
        for a in range(2):
            for b in range(2):
                copies.append(
                    send(corner_src(a, b), corner_dst.at[a * 2 + b], shifted(1 if a == 0 else -1, 0, 1 if b == 0 else -1))
                )
        return copies

    def send_columns(src, dst):
        copies = []
        for dx, dz in square:
            for side in range(2):
                dy = 1 if side == 0 else -1
                copies.append(send(src, dst.at[side, 1 - dx, 1 - dz], shifted(dx, dy, dz)))
        return copies

    def columns_in(dst, dx):
        rows = []
        for side in range(2):
            for dz in (-1, 0, 1):
                flag = (has_below, has_above)[side]
                if dx:
                    flag = jnp.logical_and(flag, edge_flags[(dx + 1) // 2])
                if dz:
                    flag = jnp.logical_and(flag, deep_flags[(dz + 1) // 2])
                rows.append(kept(flag, dst[side, dx + 1, dz + 1]))
        return rows

    edge_flags = (has_left, has_right)
    deep_flags = (has_front, has_back)

    def edge_rows(b):
        return edges.at[pl.ds(16, 16)] if b == 0 else edges.at[pl.ds(0, 16)]

    copies = send_ring(
        lambda a: vol.at[:, 3] if a == 0 else vol.at[:, 0], wide_in,
        edge_rows, deep_in, lambda a, b: edge_rows(b), corner_in,
    )

    row = lax.broadcasted_iota(jnp.int32, (16, 512), 0)
    column = lax.broadcasted_iota(jnp.int32, (16, 512), 1)
    wanted = jnp.where(row < 8, lax.div(row, 2) * 128 + lax.rem(row, 2) * 127, -1)
    pick1 = jnp.where(column == wanted, 1.0, 0.0).astype(bf16)
    ends = sum(
        mm(pick1[:, 128 * ch:128 * ch + 128], vol[ch].reshape(64, 128), NT) for ch in range(4)
    )
    col1[...] = jnp.concatenate([ends, jnp.zeros((16, 64), f32)], axis=1).astype(bf16)
    copies_c = send_columns(col1, col1_in)
    for fetch in fetches[1:]:
        fetch.wait()
    first_half = filt1[...].astype(bf16)
    wide_first = mm(first_half, t["widen"][...]).astype(bf16)
    bias1_col = row_to_column(bias1[...])
    bias2_col = row_to_column(bias2[...])
    second_half = filt2[...].astype(bf16)

    copies_t = send_ring(
        lambda a: cot, wide_t, lambda b: cot.at[96:128] if b == 0 else cot.at[0:32], deep_t,
        lambda a, b: cot.at[96:128] if b == 0 else cot.at[0:32], corner_t,
    )

    turn = mm(second_half, t["ident"][...], TN).astype(bf16)
    for m in range(13):
        low = turn[64 * m:64 * m + 32, :128].astype(f32)
        high = turn[64 * m + 32:64 * m + 64, 128:].astype(f32)
        turned[:, 128 * m:128 * m + 128] = (low + high).astype(bf16)
    turned[:, 1664:1792] = turn[832:864, :128]

    arrive(copies)
    pieces = [block]
    for a in range(2):
        pieces.append(kept(edge_flags[a], wide_in[a]).reshape(64, 128))
    for b in range(2):
        pieces.append(kept(deep_flags[b], deep_in[b]))
    for a in range(2):
        for b in range(2):
            pieces.append(kept(jnp.logical_and(edge_flags[a], deep_flags[b]), corner_in[a * 2 + b]))
    rows = mm(t["place"][...], jnp.concatenate(pieces, axis=0)).astype(bf16)
    inner = mm(rows, t["shift1"][...])
    arrive(copies_c)
    columns = [columns_in(col1_in, dx) for dx in (-1, 0, 1)]
    sides = [
        jnp.concatenate([columns[a][side * 3 + b] for a in range(3) for b in range(3)], axis=1)
        for side in range(2)
    ]
    ordered = mm(jnp.concatenate(sides, axis=0), t["order1"].folded()).astype(bf16)
    ordered = mm(ordered, t["four"][...])
    row = lax.broadcasted_iota(jnp.int32, (32, 512), 0)
    column = lax.broadcasted_iota(jnp.int32, (32, 512), 1)
    same = lax.rem(lax.div(row, 2), 8) == lax.rem(column, 4)
    ordered = jnp.where(same, ordered, 0.0).astype(bf16)
    ends = mm(ordered, t["put1"][...], TN)
    full = [inner[:, :128] + ends[:, :128], inner[:, 128:256], inner[:, 256:] + ends[:, 128:]]
    third = [piece.reshape(64, 8, 128) for piece in full]
    rolled = [pltpu.roll(piece, 4, axis=1) for piece in third]
    sub = lax.broadcasted_iota(jnp.int32, (64, 8, 128), 1)
    upper = sub < 4
    ones = jnp.where(sub == 4, 1.0, 0.0)
    even_tile = jnp.concatenate(
        [jnp.where(upper, third[0], rolled[1]), jnp.where(upper, third[2], ones)], axis=1
    )
    odd_tile = jnp.concatenate(
        [jnp.where(upper, rolled[0], third[1]), jnp.where(upper, rolled[2], ones)], axis=1
    )
    xs[:, 0] = even_tile.astype(bf16)
    xs[:, 1] = odd_tile.astype(bf16)

    def cols1(w, half_d):
        def at(i, dp, parity):
            return xs[(w + i) * 9 + dp, parity]

        one = [at(i, half_d + j // 2, j % 2) for i in range(3) for j in range(3)]
        two = [at(i, half_d + (j + 1) // 2, (j + 1) % 2) for i in range(3) for j in range(3)]
        return jnp.concatenate(
            [jnp.concatenate(one, axis=0), jnp.concatenate(two, axis=0)], axis=1
        )

    def forward1(pd, carry):
        for pw in range(2):
            part = None
            for w in (2 * pw, 2 * pw + 1):
                pre = mm(wide_first, cols1(w, pd)) + bias1_col
                pre1[w, pd] = pre
                act = leaky(pre)
                act = act[:, :128] + act[:, 128:]
                part = act if part is None else part + act
            part = (part + pltpu.roll(part, 127, axis=1)) * 0.125
            summed[pw, pd] = part.astype(bf16)
        return carry

    lax.fori_loop(0, 8, forward1, 0)
    pooled_val = (
        mm(summed[:, 0:4].reshape(256, 128), t["even"][0:128])
        + mm(summed[:, 4:8].reshape(256, 128), t["even"][128:256])
    ).astype(bf16)
    pooled[...] = pooled_val.reshape(2, 4, 32, 128)

    def turned_half(a):
        return pltpu.roll(a.astype(f32), 64, axis=1)

    low = lax.broadcasted_iota(jnp.int32, (32, 128), 1) < 64

    def halves(a, b):
        return jnp.where(low, a.astype(f32), b.astype(f32)).astype(bf16)

    for w in range(2):
        packs[0, w] = halves(turned_half(pooled[w, 2]), pooled[w, 3])
        packs[1, w] = halves(pooled[w, 0], turned_half(pooled[w, 1]))
    copies = send_ring(
        lambda a: pooled, wide2, lambda b: packs.at[b], deep2, lambda a, b: packs.at[b], corner2
    )
    pick = t["pick2"][...]
    ends = sum(
        mm(pick[:, 128 * dq:128 * dq + 128], pooled[:, dq].reshape(64, 128), NT) for dq in range(4)
    )
    col2[...] = jnp.concatenate([ends, jnp.zeros((16, 64), f32)], axis=1).astype(bf16)
    copies_c = send_columns(col2, col2_in)

    arrive(copies_t)
    spread_cot = []
    for dx in (-1, 0, 1):
        a = max(dx, 0)
        beside = edge_flags[a]
        if dx:
            rows = [kept(beside, wide_t[a])]
            rows += [kept(jnp.logical_and(beside, deep_flags[b]), corner_t[a * 2 + b]) for b in range(2)]
        else:
            rows = [cot[...]] + [kept(deep_flags[b], deep_t[b]) for b in range(2)]
        spread_cot.append(mm(jnp.concatenate(rows, axis=0), t["spread"][...], TN) * 0.125)

    arrive(copies)
    for wp in range(6):
        a, w = wp // 4, wp % 2
        if wp in (2, 3):
            near = [pooled[w, dq] for dq in range(4)]
            front, back = (kept(deep_flags[b], deep2[b, w]) for b in range(2))
        else:
            near = [kept(edge_flags[a], wide2[a, w, dq]) for dq in range(4)]
            front, back = (
                kept(jnp.logical_and(edge_flags[a], deep_flags[b]), corner2[a * 2 + b, w]) for b in range(2)
            )
        for dq in range(4):
            v2[wp * 6 + dq] = near[dq]
        v2[wp * 6 + 4] = halves(front, turned_half(near[2]))
        v2[wp * 6 + 5] = halves(turned_half(near[1]), back)
        v2[36 + wp] = halves(near[3], front)
        v2[42 + wp] = halves(back, near[0])
    inner = jnp.concatenate(
        [mm(v2[0:36].reshape(1152, 128), t["shift2"][...]), mm(v2[36:48].reshape(384, 128), t["swapped"][...])],
        axis=0,
    )
    arrive(copies_c)
    put = t["put2"][...]
    edge = [mm(jnp.concatenate(columns_in(col2_in, dx), axis=0), put, TN) for dx in (-1, 0, 1)]
    for wp in range(6):
        for dp in range(8):
            number = {0: wp * 6 + 4, 1: 36 + wp, 6: 42 + wp, 7: wp * 6 + 5}.get(dp, wp * 6 + dp - 2)
            for k in range(3):
                piece = inner[number * 32:number * 32 + 32, 128 * k:128 * k + 128]
                if k != 1:
                    lane = dp * 256 + 64 * k
                    piece = piece + edge[wp // 2][(wp % 2) * 32:(wp % 2) * 32 + 32, lane:lane + 128]
                ys[wp * 8 + dp, k * 32:k * 32 + 32, :] = piece.astype(bf16)

    def cols2(w, dq, extra):
        taps = [ys[(w + i) * 8 + dq + j] for i in range(3) for j in range(3)]
        return jnp.concatenate(taps + extra, axis=0)

    feat_sum = [None, None]
    for dq in range(6):
        kind = {0: 2, 5: 3}.get(dq, (dq - 1) // 2)
        for pair in ((1, 2), (0, 3)):
            cols = jnp.concatenate([cols2(w, dq, []) for w in pair], axis=1)
            pre = mm(second_half, cols) + bias2_col
            if pair == (1, 2) and 0 < dq < 5:
                act = leaky(pre)
                act = act[:, :128] + act[:, 128:]
                feat_sum[kind] = act if feat_sum[kind] is None else feat_sum[kind] + act
            for n, w in enumerate(pair):
                here = spread_cot[(w + 1) // 2][:, 128 * kind:128 * kind + 128]
                errs[w, dq] = (here * slope(pre[:, 128 * n:128 * n + 128])).astype(bf16)

    pick = t["pick3"][...]
    col3[...] = sum(
        mm(pick[:, 128 * dq:128 * dq + 128], errs[:, dq].reshape(256, 128), NT) for dq in range(6)
    ).astype(bf16)
    copies = [send(col3, col3_in.at[0], shifted(0, 1, 0)), send(col3, col3_in.at[1], shifted(0, -1, 0))]

    def second_half_grads():
        ends = [
            ((both + pltpu.roll(both, 127, axis=1)) * 0.125).astype(bf16) for both in feat_sum
        ]
        feat[...] = (mm(t["collect"][0:128], ends[0], NT) + mm(t["collect"][128:256], ends[1], NT)).astype(bf16)
        ones_rows = [jnp.ones((32, 128), bf16)]
        grad2 = None
        for dq in range(4):
            cols = jnp.concatenate([cols2(w, dq + 1, ones_rows) for w in (1, 2)], axis=1)
            err = jnp.concatenate([errs[w, dq + 1] for w in (1, 2)], axis=1)
            piece = mm(err, cols, NT)
            grad2 = piece if grad2 is None else grad2 + piece
        for l in range(7):
            grads[l * 64:l * 64 + 64] = grad2[:, 128 * l:128 * l + 128]
        grads[448:512] = jnp.zeros((64, 128), f32)
        return put_out(0), sum_core(send(part(grads, 1 - core, n1), core_in, sibling))

    def part(ref, index, size):
        return ref.at[pl.ds(pl.multiple_of(index * size, size), size)]

    n1, n2, n3 = 256, 256 // NX, 256 // NX // GY

    def sum_core(copy):
        copy.wait_recv()
        red1[...] = part(grads, core, n1)[...] + core_in[...]
        return [send(part(red1, x_peer(r)[0], n2), x_in.at[r - 1], x_peer(r)[1]) for r in range(1, NX)]

    def sum_x(copies):
        arrive(copies)
        acc = part(red1, xc, n2)[...]
        for r in range(1, NX):
            acc = acc + x_in[r - 1]
        red2[...] = acc
        return [send(part(red2, y_peer(r)[0], n3), y_in.at[r - 1], y_peer(r)[1]) for r in range(1, GY)]

    def sum_y(copies):
        arrive(copies)
        acc = part(red2, gy, n3)[...]
        for r in range(1, GY):
            acc = acc + y_in[r - 1]
        red3[...] = acc
        z_in[zc] = acc
        return [send(red3, z_in.at[zc], z_peer(r)) for r in range(1, NZ)]

    def sum_z(copies):
        arrive(copies)
        acc = z_in[0]
        for r in range(1, NZ):
            acc = acc + z_in[r]
        mine = part(total, (core * NX + xc) * GY + gy, n3)
        mine[...] = acc
        return [send(mine, mine, y_peer(r)[1]) for r in range(1, GY)]

    def gather_x(copies):
        arrive(copies)
        mine = part(total, core * NX + xc, n2)
        return [send(mine, mine, x_peer(r)[1]) for r in range(1, NX)]

    def gather_core(copies):
        arrive(copies)
        mine = part(total, core, n1)
        return send(mine, mine, sibling)

    def everyone(value, slots, index, devices):
        slots[index] = value
        return [send(slots.at[index], slots.at[index], device) for device in devices]

    def summed_slots(copies, slots):
        arrive(copies)
        acc = slots[0]
        for n in range(1, slots.shape[0]):
            acc = acc + slots[n]
        return acc

    feat_out, copies2 = second_half_grads()
    inner = mm(errs[...].reshape(1536, 128), t["shift2"][...])
    arrive(copies)
    rows = [kept(has_below, col3_in[0]), kept(has_above, col3_in[1])]
    edge = mm(jnp.concatenate(rows, axis=0), t["put3"][...], TN)
    for wp in range(4):
        for dp in range(6):
            number = wp * 6 + dp
            for k in range(3):
                piece = inner[number * 64:number * 64 + 64, 128 * k:128 * k + 128]
                if k != 1:
                    lane = dp * 256 + 64 * k
                    piece = piece + edge[wp * 64:wp * 64 + 64, lane:lane + 128]
                fs[number, (2 - k) * 64:(2 - k) * 64 + 64, :] = piece.astype(bf16)
    copies2 = sum_x(copies2)

    for dq in range(4):
        def cols3(w):
            taps = [fs[(w + 2 - i) * 6 + dq + 2 - j] for i in range(3) for j in range(3)]
            return jnp.concatenate(taps + [jnp.zeros((64, 128), bf16)], axis=0)

        cols = jnp.concatenate([cols3(0), cols3(1)], axis=1)
        pe = mm(turned[...], cols).astype(bf16)
        both = mm(jnp.concatenate([pe[:, :128], pe[:, 128:]], axis=0), t["twice"][...]) * 0.125
        for w in range(2):
            perr[w, dq] = both[32 * w:32 * w + 32, :128]
            perr[w, dq + 4] = both[32 * w:32 * w + 32, 128:]

    copies2 = sum_y(copies2)

    def backward1(pd, acc):
        for w in range(4):
            here = perr[w // 2, pd]
            err = (jnp.concatenate([here, here], axis=1) * slope(pre1[w, pd])).astype(bf16)
            acc = acc + mm(err, cols1(w, pd), NT)
        return acc

    grad1 = lax.fori_loop(0, 8, backward1, jnp.zeros((32, 144), f32))
    one[...] = sum(mm(piece, t["narrow"][...]) for piece in split3(grad1))
    copies1 = send(part(one, 1 - core, 16), one_core, sibling)
    copies1.wait_recv()
    copies1 = everyone(part(one, core, 16)[...] + one_core[...], one_x, xc, [x_peer(r)[1] for r in range(1, NX)])
    copies2 = sum_z(copies2)
    copies1 = everyone(summed_slots(copies1, one_x), one_y, gy, [y_peer(r)[1] for r in range(1, GY)])
    copies2 = gather_x(copies2)
    copies1 = everyone(summed_slots(copies1, one_y), one_z, zc, [z_peer(r) for r in range(1, NZ)])
    copy2 = gather_core(copies2)
    copy2.wait_recv()
    sums2 = jnp.concatenate([total[l * 64:l * 64 + 64] for l in range(7)], axis=1)
    step2[...] = filt2[...] - learn_rate * sums2[:, :864]
    off2[...] = bias2[...] - learn_rate * column_to_row(sums2[:, 864:865])
    outs = [put_out(3), put_out(4)]
    mine = part(one_total, core, 16)
    mine[...] = summed_slots(copies1, one_z)
    copy1 = send(mine, mine, sibling)
    copy1.wait_recv()
    sums1 = one_total[...]
    step1[...] = filt1[...] - learn_rate * sums1[:, :108]
    off1[...] = bias1[...] - learn_rate * column_to_row(sums1[:, 108:109])
    outs += [put_out(1), put_out(2)]

    for copy in started:
        copy.wait_send()
    feat_out.wait()
    for out in outs:
        out.wait()


def hand_on(*refs):
    ins, outs, spots, in_sems, out_sems = refs[:5], refs[5:10], refs[10:15], refs[15], refs[16]
    reads = [pltpu.make_async_copy(ins[n], spots[n], in_sems.at[n]) for n in range(5)]
    writes = [pltpu.make_async_copy(spots[n], outs[n], out_sems.at[n]) for n in range(5)]
    for copy in reads:
        copy.start()
    for n in (3, 0, 1, 2, 4):
        reads[n].wait()
        writes[n].start()
    for copy in writes:
        copy.wait()


def shards(volume, first_filters, first_bias, second_filters, second_bias, cotangent):
    GX, GY, GZ = lax.axis_size("gx"), lax.axis_size("gy"), lax.axis_size("gz")
    NX = 4 if GZ >= 8 else 2
    NZ = (GX // 2) * (GZ // NX)
    n2, n3 = 256 // NX, 256 // NX // GY
    operands = [
        volume, first_filters, first_bias.reshape(1, 32), second_filters, second_bias.reshape(1, 64),
        cotangent.transpose(1, 2, 3, 0).reshape(128, 64), jnp.asarray(PACKED),
    ]
    sems = 62 + 4 + 3 * (NX - 1) + 3 * (GY - 1) + 2 * (NZ - 1)
    V = pltpu.VMEM
    results = (
        jax.ShapeDtypeStruct((128, 64), bf16),
        jax.ShapeDtypeStruct((32, 108), f32),
        jax.ShapeDtypeStruct((1, 32), f32),
        jax.ShapeDtypeStruct((64, 864), f32),
        jax.ShapeDtypeStruct((1, 64), f32),
    )
    out = pl.pallas_call(
        functools.partial(kernel, (GX, GY, GZ, NX)),
        out_shape=results,
        in_specs=[pl.BlockSpec(memory_space=pltpu.HBM)] * len(operands),
        out_specs=[pl.BlockSpec(memory_space=pltpu.HBM)] * 5,
        scratch_shapes=[
            V((32, 128), bf16), V((2, 4, 16, 128), bf16), V((2, 16, 128), bf16), V((4, 16, 128), bf16),
            V((16, 128), bf16), V((2, 3, 3, 16, 128), bf16), V((64, 2, 16, 128), bf16), V((4, 8, 32, 256), f32),
            V((2, 8, 32, 128), bf16),
            V((2, 128, 64), bf16), V((2, 32, 64), bf16), V((4, 32, 64), bf16),
            V((2, 4, 32, 128), bf16), V((2, 2, 32, 128), bf16), V((2, 2, 4, 32, 128), bf16),
            V((2, 2, 32, 128), bf16), V((4, 2, 32, 128), bf16), V((48, 32, 128), bf16),
            V((16, 128), bf16), V((2, 3, 3, 16, 128), bf16), V((48, 96, 128), bf16),
            V((4, 6, 64, 128), bf16), V((32, 256), bf16), V((2, 32, 256), bf16), V((24, 192, 128), bf16),
            V((32, 1792), bf16), V((2, 8, 32, 128), f32),
            V((512, 128), f32), V((256, 128), f32), V((256, 128), f32), V((NX - 1, n2, 128), f32),
            V((n2, 128), f32), V((GY - 1, n3, 128), f32), V((n3, 128), f32), V((NZ, n3, 128), f32),
            V((512, 128), f32),
            V((32, 128), f32), V((16, 128), f32), V((NX, 16, 128), f32), V((GY, 16, 128), f32),
            V((NZ, 16, 128), f32), V((32, 128), f32),
            pltpu.SemaphoreType.DMA((sems,)), pltpu.SemaphoreType.DMA((sems,)),
        ] + [V(a.shape, a.dtype) for a in operands] + [
            pltpu.SemaphoreType.DMA((len(operands),)),
        ] + [V(a.shape, a.dtype) for a in results] + [
            pltpu.SemaphoreType.DMA((5,)),
        ],
        compiler_params=pltpu.CompilerParams(
            collective_id=0, has_side_effects=True, vmem_limit_bytes=62 * 2**20
        ),
    )(*operands)
    out = pl.pallas_call(
        hand_on,
        out_shape=results,
        in_specs=[pl.BlockSpec(memory_space=pltpu.HBM)] * 5,
        out_specs=[pl.BlockSpec(memory_space=pltpu.HBM)] * 5,
        scratch_shapes=[V(a.shape, a.dtype) for a in results]
        + [pltpu.SemaphoreType.DMA((5,)), pltpu.SemaphoreType.DMA((5,))],
        compiler_params=pltpu.CompilerParams(vmem_limit_bytes=62 * 2**20),
    )(*out)
    features, stepped_first, offset_first, stepped_second, offset_second = out
    return (
        features.reshape(1, 4, 32, 64).transpose(3, 0, 1, 2), stepped_first, offset_first.reshape(32), stepped_second,
        offset_second.reshape(64),
    )


def solution(mesh):
    return jax.shard_map(
        shards,
        mesh=mesh,
        in_specs=(P(None, "gx", "gz", "gy"), P(), P(), P(), P(), P(None, "gx", "gz", "gy")),
        out_specs=(P(None, "gx", "gz", "gy"), P(), P(), P(), P()),
        check_vma=False,
    )
```

```python
import functools

import jax
import jax.numpy as jnp
import numpy as np
from jax import lax
from jax.experimental import pallas as pl
from jax.experimental.pallas import tpu as pltpu
from jax.sharding import PartitionSpec as P

slope_below = 0.3
learn_rate = 0.001
f32 = jnp.float32
bf16 = jnp.bfloat16
MESH = pl.DeviceIdType.MESH
NN = (((1,), (0,)), ((), ()))
NT = (((1,), (1,)), ((), ()))
TN = (((0,), (0,)), ((), ()))


def mm(a, b, dims=NN):
    return lax.dot_general(a, b, dims, preferred_element_type=f32)


def tables():
    place = np.zeros((512, 480))
    for wp in range(6):
        for dp in range(18):
            for ch in range(4):
                w, d = wp - 1, dp - 1
                inner_w, inner_d = 0 <= w < 4, 0 <= d < 16
                if inner_w and inner_d:
                    src = (ch * 4 + w) * 16 + d
                elif inner_d:
                    src = 256 + (64 if w > 0 else 0) + ch * 16 + d
                elif inner_w:
                    src = 384 + (16 if d > 0 else 0) + ch * 4 + w
                else:
                    a, b = int(w > 0), int(d > 0)
                    src = 416 + (a * 2 + b) * 16 + ch * 4 + (0 if a else 3)
                place[(wp * 18 + dp) * 4 + ch, src] = 1
    shift1 = np.zeros((128, 384))
    for l in range(128):
        if l:
            shift1[l - 1, l] = 1
        shift1[l, 128 + l] = 1
        if l < 127:
            shift1[l + 1, 256 + l] = 1
    order1 = np.zeros((1152, 128))
    for wp in range(6):
        for dp in range(18):
            a, b = (wp > 0) + (wp > 4), (dp > 0) + (dp > 16)
            w, d = (3, wp - 1, 0)[a], (15, dp - 1, 0)[b]
            order1[(a * 3 + b) * 128 + w * 16 + d, wp * 18 + dp] = 1
    four = np.zeros((128, 512))
    for q in range(512):
        four[q // 4, q] = 1
    put1 = np.zeros((32, 256))
    for ch in range(4):
        put1[ch * 2 + 1, 0] = put1[16 + ch * 2, 255] = 1
    shift2 = np.zeros((128, 384))
    swapped = np.zeros((128, 384))
    for l in range(128):
        for k in range(3):
            s = l % 64 + k - 1
            if 0 <= s < 64:
                s += l - l % 64
                shift2[s, k * 128 + l] = 1
                swapped[(s + 64) % 128, k * 128 + l] = 1
    ends = (0, 63, 64, 127)
    pick2 = np.zeros((16, 512))
    for dq in range(4):
        for n, l in enumerate(ends):
            pick2[dq * 4 + n, dq * 128 + l] = 1
    put2 = np.zeros((96, 2048))
    for dq in range(-2, 6):
        for half in range(2):
            d = dq + 4 * half
            dz = (d >= 0) + (d > 7)
            there, row = (d % 8) // 4, (d % 4) * 4
            put2[dz * 16 + row + 2 * there + 1, (dq + 2) * 256 + 64 * half] = 1
            put2[48 + dz * 16 + row + 2 * there, (dq + 2) * 256 + 128 + 64 * half + 63] = 1
    pick3 = np.zeros((32, 768))
    put3 = np.zeros((64, 1536))
    for dq in range(6):
        for n, l in enumerate(ends):
            pick3[dq * 4 + n, dq * 128 + l] = 1
        for half in range(2):
            put3[dq * 4 + 2 * half + 1, dq * 256 + 64 * half] = 1
            put3[32 + dq * 4 + 2 * half, dq * 256 + 128 + 64 * half + 63] = 1
    even = np.zeros((256, 128))
    for half in range(2):
        for h in range(64):
            even[half * 128 + 2 * h, half * 64 + h] = 1
    twice = np.zeros((128, 256))
    for half in range(2):
        for h in range(128):
            twice[half * 64 + h // 2, half * 128 + h] = 1
    spread = np.zeros((192, 512))
    for dc in range(-1, 5):
        for hc in range(32):
            row = (128 if dc < 0 else 160 if dc > 3 else dc * 32) + hc
            for t in range(2):
                for half in range(2):
                    kind = {0: 0, 1: 1, -1: 2, 2: 3}.get(dc - 2 * half)
                    if kind is not None:
                        spread[row, kind * 128 + half * 64 + 2 * hc + t] = 1
    collect = np.zeros((256, 128))
    for dc in range(4):
        for hc in range(32):
            collect[(dc % 2) * 128 + dc * 32 + hc, (dc // 2) * 64 + 2 * hc] = 1
    widen = np.zeros((108, 144))
    narrow = np.zeros((144, 128))
    for q in range(108):
        widen[q, (q // 12) * 16 + q % 12] = 1
        narrow[(q // 12) * 16 + q % 12, q] = 1
    narrow[12, 108] = 1
    ident = np.zeros((64, 256))
    for o in range(64):
        ident[o, o] = ident[o, 128 + 64 + o] = 1
    every = dict(
        place=place, shift1=shift1, order1=order1, four=four, put1=put1, shift2=shift2, swapped=swapped,
        pick2=pick2, put2=put2, pick3=pick3, put3=put3, even=even, twice=twice, spread=spread, collect=collect,
        widen=widen, narrow=narrow, ident=ident,
    )
    return every


TABLE = {}


def packed_table():
    parts, row = [], 0
    for name, value in tables().items():
        rows, lanes = value.shape
        if name == "order1":
            value = np.concatenate(np.split(value, 4), axis=1)
            rows //= 4
        wide = np.zeros((-(-rows // 16) * 16, -(-lanes // 512) * 512))
        wide[:rows, :value.shape[1]] = value
        wide = np.concatenate(np.split(wide, wide.shape[1] // 512, axis=1))
        TABLE[name] = (row, rows, lanes)
        row += wide.shape[0]
        parts.append(wide)
    return np.concatenate(parts).astype(jnp.bfloat16)


PACKED = packed_table()


class Rows:
    def __init__(self, ref, name):
        self.ref = ref
        self.row, self.rows, self.lanes = TABLE[name]

    def folded(self):
        return jnp.concatenate(
            [self.ref[self.row:self.row + self.rows, 128 * n:128 * n + 128] for n in range(4)], axis=0
        )

    def __getitem__(self, key):
        if self.lanes > 512:
            step = -(-self.rows // 16) * 16
            return jnp.concatenate(
                [self.ref[self.row + n * step:self.row + n * step + self.rows, :] for n in range(-(-self.lanes // 512))],
                axis=1,
            )
        if key is Ellipsis:
            return self.ref[self.row:self.row + self.rows, :self.lanes]
        return self.ref[self.row + key.start:self.row + key.stop, :self.lanes]


def row_to_column(row):
    n = row.shape[1]
    diagonal = lax.broadcasted_iota(jnp.int32, (n, n), 0) == lax.broadcasted_iota(jnp.int32, (n, n), 1)
    return jnp.sum(jnp.where(diagonal, jnp.broadcast_to(row, (n, n)), 0.0), axis=1, keepdims=True)


def column_to_row(column):
    n = column.shape[0]
    diagonal = lax.broadcasted_iota(jnp.int32, (n, n), 0) == lax.broadcasted_iota(jnp.int32, (n, n), 1)
    return jnp.sum(jnp.where(diagonal, jnp.broadcast_to(column, (n, n)), 0.0), axis=0, keepdims=True)


def kept(flag, value):
    return lax.select(flag, value, jnp.zeros_like(value))


def leaky(a):
    return jnp.where(a > 0, a, slope_below * a)


def slope(a):
    return jnp.where(a > 0, 1.0, slope_below)


def split3(a):
    high = a.astype(bf16)
    rest = a - high.astype(f32)
    mid = rest.astype(bf16)
    return high, mid, (rest - mid.astype(f32)).astype(bf16)


def kernel(sizes, *refs):
    GX, GY, GZ, NX = sizes
    ZL = GZ // NX
    ZH = GX // 2
    NZ = ZH * ZL
    far = refs[:7]
    refs = refs[7:]
    far_out = refs[:5]
    (
        edges, wide_in, deep_in, corner_in, col1, col1_in, xs, pre1, summed,
        wide_t, deep_t, corner_t, pooled, packs, wide2, deep2, corner2, v2, col2, col2_in, ys,
        errs, col3, col3_in, fs, turned, perr,
        grads, core_in, red1, plane_in, z_in, total,
        one, one_core, one_plane, one_z, one_total, send_sems, recv_sems, vol, filt1, bias1, filt2, bias2, cot, packed, in_sems,
        feat, step1, off1, step2, off2, out_sems,
    ) = refs[5:]
    near = (vol, filt1, bias1, filt2, bias2, cot, packed)
    fetches = [pltpu.make_async_copy(a, b, in_sems.at[n]) for n, (a, b) in enumerate(zip(far, near))]
    for fetch in fetches:
        fetch.start()
    t = {name: Rows(packed, name) for name in TABLE}

    gx, gy, gz = lax.axis_index("gx"), lax.axis_index("gy"), lax.axis_index("gz")
    core, zh = lax.rem(gx, 2), lax.div(gx, 2)
    xc, zl = lax.rem(gz, NX), lax.div(gz, NX)
    zc = zh * ZL + zl

    def shifted(dx, dy, dz):
        return (lax.rem(gx + (dx + GX), GX), lax.rem(gy + (dy + GY), GY), lax.rem(gz + (dz + GZ), GZ))

    sibling = (gx + 1 - 2 * core, gy, gz)

    plane = xc * GY + gy
    NP = NX * GY

    def plane_peer(r):
        p = lax.rem(plane + r, NP)
        return p, (gx, lax.rem(p, GY), zl * NX + lax.div(p, GY))

    def z_peer(r):
        p = lax.rem(zc + r, NZ)
        return (2 * lax.div(p, ZL) + core, gy, lax.rem(p, ZL) * NX + xc)

    square = [(dx, dz) for dx in (-1, 0, 1) for dz in (-1, 0, 1)]
    peers = [shifted(dx, 0, dz) for dx, dz in square if (dx, dz) != (0, 0)]
    peers += [shifted(dx, dy, dz) for dx, dz in square for dy in (-1, 1)]
    peers += [plane_peer(r)[1] for r in range(1, NP)]
    peers += [z_peer(r) for r in range(1, NZ)]
    barrier = pltpu.get_barrier_semaphore()
    for peer in peers:
        pl.semaphore_signal(barrier, inc=1, device_id=peer, device_id_type=MESH)

    count = [0]
    started = []

    def send(src, dst, device):
        n = count[0]
        count[0] += 1
        copy = pltpu.make_async_remote_copy(
            src_ref=src, dst_ref=dst, send_sem=send_sems.at[n], recv_sem=recv_sems.at[n],
            device_id=device, device_id_type=MESH,
        )
        copy.start()
        started.append(copy)
        return copy

    def put_out(n):
        copy = pltpu.make_async_copy((feat, step1, off1, step2, off2)[n], far_out[n], out_sems.at[n])
        copy.start()
        return copy

    def arrive(copies):
        for copy in copies:
            copy.wait_recv()

    row = lax.broadcasted_iota(jnp.int32, (32, 256), 0)
    column = lax.broadcasted_iota(jnp.int32, (32, 256), 1)
    wanted = jnp.where(row < 16, row * 16, row * 16 - 241)
    edge = jnp.where(column == wanted, 1.0, 0.0).astype(bf16)
    fetches[0].wait()
    block = vol[...].reshape(256, 128)
    edges[...] = mm(edge, block).astype(bf16)
    pl.semaphore_wait(barrier, len(peers))

    has_left, has_right = gx > 0, gx < GX - 1
    has_front, has_back = gz > 0, gz < GZ - 1
    has_below, has_above = gy > 0, gy < GY - 1

    def send_ring(wide_src, wide_dst, deep_src, deep_dst, corner_src, corner_dst):
        copies = []
        for a in range(2):
            dx = 1 if a == 0 else -1
            copies.append(send(wide_src(a), wide_dst.at[a], shifted(dx, 0, 0)))
        for b in range(2):
            dz = 1 if b == 0 else -1
            copies.append(send(deep_src(b), deep_dst.at[b], shifted(0, 0, dz)))
        for a in range(2):
            for b in range(2):
                copies.append(
                    send(corner_src(a, b), corner_dst.at[a * 2 + b], shifted(1 if a == 0 else -1, 0, 1 if b == 0 else -1))
                )
        return copies

    def send_columns(src, dst):
        copies = []
        for dx, dz in square:
            for side in range(2):
                dy = 1 if side == 0 else -1
                copies.append(send(src, dst.at[side, 1 - dx, 1 - dz], shifted(dx, dy, dz)))
        return copies

    def columns_in(dst, dx):
        rows = []
        for side in range(2):
            for dz in (-1, 0, 1):
                flag = (has_below, has_above)[side]
                if dx:
                    flag = jnp.logical_and(flag, edge_flags[(dx + 1) // 2])
                if dz:
                    flag = jnp.logical_and(flag, deep_flags[(dz + 1) // 2])
                rows.append(kept(flag, dst[side, dx + 1, dz + 1]))
        return rows

    edge_flags = (has_left, has_right)
    deep_flags = (has_front, has_back)

    def edge_rows(b):
        return edges.at[pl.ds(16, 16)] if b == 0 else edges.at[pl.ds(0, 16)]

    copies = send_ring(
        lambda a: vol.at[:, 3] if a == 0 else vol.at[:, 0], wide_in,
        edge_rows, deep_in, lambda a, b: edge_rows(b), corner_in,
    )

    row = lax.broadcasted_iota(jnp.int32, (16, 512), 0)
    column = lax.broadcasted_iota(jnp.int32, (16, 512), 1)
    wanted = jnp.where(row < 8, lax.div(row, 2) * 128 + lax.rem(row, 2) * 127, -1)
    pick1 = jnp.where(column == wanted, 1.0, 0.0).astype(bf16)
    ends = sum(
        mm(pick1[:, 128 * ch:128 * ch + 128], vol[ch].reshape(64, 128), NT) for ch in range(4)
    )
    col1[...] = jnp.concatenate([ends, jnp.zeros((16, 64), f32)], axis=1).astype(bf16)
    copies_c = send_columns(col1, col1_in)
    for fetch in fetches[1:]:
        fetch.wait()
    first_half = filt1[...].astype(bf16)
    wide_first = mm(first_half, t["widen"][...]).astype(bf16)
    bias1_col = row_to_column(bias1[...])
    bias2_col = row_to_column(bias2[...])
    second_half = filt2[...].astype(bf16)

    copies_t = send_ring(
        lambda a: cot, wide_t, lambda b: cot.at[96:128] if b == 0 else cot.at[0:32], deep_t,
        lambda a, b: cot.at[96:128] if b == 0 else cot.at[0:32], corner_t,
    )

    turn = mm(second_half, t["ident"][...], TN).astype(bf16)
    for m in range(13):
        low = turn[64 * m:64 * m + 32, :128].astype(f32)
        high = turn[64 * m + 32:64 * m + 64, 128:].astype(f32)
        turned[:, 128 * m:128 * m + 128] = (low + high).astype(bf16)
    turned[:, 1664:1792] = turn[832:864, :128]

    arrive(copies)
    pieces = [block]
    for a in range(2):
        pieces.append(kept(edge_flags[a], wide_in[a]).reshape(64, 128))
    for b in range(2):
        pieces.append(kept(deep_flags[b], deep_in[b]))
    for a in range(2):
        for b in range(2):
            pieces.append(kept(jnp.logical_and(edge_flags[a], deep_flags[b]), corner_in[a * 2 + b]))
    rows = mm(t["place"][...], jnp.concatenate(pieces, axis=0)).astype(bf16)
    inner = mm(rows, t["shift1"][...])
    arrive(copies_c)
    columns = [columns_in(col1_in, dx) for dx in (-1, 0, 1)]
    sides = [
        jnp.concatenate([columns[a][side * 3 + b] for a in range(3) for b in range(3)], axis=1)
        for side in range(2)
    ]
    ordered = mm(jnp.concatenate(sides, axis=0), t["order1"].folded()).astype(bf16)
    ordered = mm(ordered, t["four"][...])
    row = lax.broadcasted_iota(jnp.int32, (32, 512), 0)
    column = lax.broadcasted_iota(jnp.int32, (32, 512), 1)
    same = lax.rem(lax.div(row, 2), 8) == lax.rem(column, 4)
    ordered = jnp.where(same, ordered, 0.0).astype(bf16)
    ends = mm(ordered, t["put1"][...], TN)
    full = [inner[:, :128] + ends[:, :128], inner[:, 128:256], inner[:, 256:] + ends[:, 128:]]
    third = [piece.reshape(64, 8, 128) for piece in full]
    rolled = [pltpu.roll(piece, 4, axis=1) for piece in third]
    sub = lax.broadcasted_iota(jnp.int32, (64, 8, 128), 1)
    upper = sub < 4
    ones = jnp.where(sub == 4, 1.0, 0.0)
    even_tile = jnp.concatenate(
        [jnp.where(upper, third[0], rolled[1]), jnp.where(upper, third[2], ones)], axis=1
    )
    odd_tile = jnp.concatenate(
        [jnp.where(upper, rolled[0], third[1]), jnp.where(upper, rolled[2], ones)], axis=1
    )
    xs[:, 0] = even_tile.astype(bf16)
    xs[:, 1] = odd_tile.astype(bf16)

    def cols1(w, half_d):
        def at(i, dp, parity):
            return xs[(w + i) * 9 + dp, parity]

        one = [at(i, half_d + j // 2, j % 2) for i in range(3) for j in range(3)]
        two = [at(i, half_d + (j + 1) // 2, (j + 1) % 2) for i in range(3) for j in range(3)]
        return jnp.concatenate(
            [jnp.concatenate(one, axis=0), jnp.concatenate(two, axis=0)], axis=1
        )

    def forward1(pd, carry):
        for pw in range(2):
            part = None
            for w in (2 * pw, 2 * pw + 1):
                pre = mm(wide_first, cols1(w, pd)) + bias1_col
                pre1[w, pd] = pre
                act = leaky(pre)
                act = act[:, :128] + act[:, 128:]
                part = act if part is None else part + act
            part = (part + pltpu.roll(part, 127, axis=1)) * 0.125
            summed[pw, pd] = part.astype(bf16)
        return carry

    lax.fori_loop(0, 8, forward1, 0)
    pooled_val = (
        mm(summed[:, 0:4].reshape(256, 128), t["even"][0:128])
        + mm(summed[:, 4:8].reshape(256, 128), t["even"][128:256])
    ).astype(bf16)
    pooled[...] = pooled_val.reshape(2, 4, 32, 128)

    def turned_half(a):
        return pltpu.roll(a.astype(f32), 64, axis=1)

    low = lax.broadcasted_iota(jnp.int32, (32, 128), 1) < 64

    def halves(a, b):
        return jnp.where(low, a.astype(f32), b.astype(f32)).astype(bf16)

    for w in range(2):
        packs[0, w] = halves(turned_half(pooled[w, 2]), pooled[w, 3])
        packs[1, w] = halves(pooled[w, 0], turned_half(pooled[w, 1]))
    copies = send_ring(
        lambda a: pooled, wide2, lambda b: packs.at[b], deep2, lambda a, b: packs.at[b], corner2
    )
    pick = t["pick2"][...]
    ends = sum(
        mm(pick[:, 128 * dq:128 * dq + 128], pooled[:, dq].reshape(64, 128), NT) for dq in range(4)
    )
    col2[...] = jnp.concatenate([ends, jnp.zeros((16, 64), f32)], axis=1).astype(bf16)
    copies_c = send_columns(col2, col2_in)

    arrive(copies_t)
    spread_cot = []
    for dx in (-1, 0, 1):
        a = max(dx, 0)
        beside = edge_flags[a]
        if dx:
            rows = [kept(beside, wide_t[a])]
            rows += [kept(jnp.logical_and(beside, deep_flags[b]), corner_t[a * 2 + b]) for b in range(2)]
        else:
            rows = [cot[...]] + [kept(deep_flags[b], deep_t[b]) for b in range(2)]
        spread_cot.append(mm(jnp.concatenate(rows, axis=0), t["spread"][...], TN) * 0.125)

    arrive(copies)
    for wp in range(6):
        a, w = wp // 4, wp % 2
        if wp in (2, 3):
            near = [pooled[w, dq] for dq in range(4)]
            front, back = (kept(deep_flags[b], deep2[b, w]) for b in range(2))
        else:
            near = [kept(edge_flags[a], wide2[a, w, dq]) for dq in range(4)]
            front, back = (
                kept(jnp.logical_and(edge_flags[a], deep_flags[b]), corner2[a * 2 + b, w]) for b in range(2)
            )
        for dq in range(4):
            v2[wp * 6 + dq] = near[dq]
        v2[wp * 6 + 4] = halves(front, turned_half(near[2]))
        v2[wp * 6 + 5] = halves(turned_half(near[1]), back)
        v2[36 + wp] = halves(near[3], front)
        v2[42 + wp] = halves(back, near[0])
    inner = jnp.concatenate(
        [mm(v2[0:36].reshape(1152, 128), t["shift2"][...]), mm(v2[36:48].reshape(384, 128), t["swapped"][...])],
        axis=0,
    )
    arrive(copies_c)
    put = t["put2"][...]
    edge = [mm(jnp.concatenate(columns_in(col2_in, dx), axis=0), put, TN) for dx in (-1, 0, 1)]
    for wp in range(6):
        for dp in range(8):
            number = {0: wp * 6 + 4, 1: 36 + wp, 6: 42 + wp, 7: wp * 6 + 5}.get(dp, wp * 6 + dp - 2)
            for k in range(3):
                piece = inner[number * 32:number * 32 + 32, 128 * k:128 * k + 128]
                if k != 1:
                    lane = dp * 256 + 64 * k
                    piece = piece + edge[wp // 2][(wp % 2) * 32:(wp % 2) * 32 + 32, lane:lane + 128]
                ys[wp * 8 + dp, k * 32:k * 32 + 32, :] = piece.astype(bf16)

    def cols2(w, dq, extra):
        taps = [ys[(w + i) * 8 + dq + j] for i in range(3) for j in range(3)]
        return jnp.concatenate(taps + extra, axis=0)

    feat_sum = [None, None]
    for dq in range(6):
        kind = {0: 2, 5: 3}.get(dq, (dq - 1) // 2)
        for pair in ((1, 2), (0, 3)):
            cols = jnp.concatenate([cols2(w, dq, []) for w in pair], axis=1)
            pre = mm(second_half, cols) + bias2_col
            if pair == (1, 2) and 0 < dq < 5:
                act = leaky(pre)
                act = act[:, :128] + act[:, 128:]
                feat_sum[kind] = act if feat_sum[kind] is None else feat_sum[kind] + act
            for n, w in enumerate(pair):
                here = spread_cot[(w + 1) // 2][:, 128 * kind:128 * kind + 128]
                errs[w, dq] = (here * slope(pre[:, 128 * n:128 * n + 128])).astype(bf16)

    pick = t["pick3"][...]
    col3[...] = sum(
        mm(pick[:, 128 * dq:128 * dq + 128], errs[:, dq].reshape(256, 128), NT) for dq in range(6)
    ).astype(bf16)
    copies = [send(col3, col3_in.at[0], shifted(0, 1, 0)), send(col3, col3_in.at[1], shifted(0, -1, 0))]

    def second_half_grads():
        ends = [
            ((both + pltpu.roll(both, 127, axis=1)) * 0.125).astype(bf16) for both in feat_sum
        ]
        feat[...] = (mm(t["collect"][0:128], ends[0], NT) + mm(t["collect"][128:256], ends[1], NT)).astype(bf16)
        ones_rows = [jnp.ones((32, 128), bf16)]
        grad2 = None
        for dq in range(4):
            cols = jnp.concatenate([cols2(w, dq + 1, ones_rows) for w in (1, 2)], axis=1)
            err = jnp.concatenate([errs[w, dq + 1] for w in (1, 2)], axis=1)
            piece = mm(err, cols, NT)
            grad2 = piece if grad2 is None else grad2 + piece
        for l in range(7):
            grads[l * 64:l * 64 + 64] = grad2[:, 128 * l:128 * l + 128]
        grads[448:512] = jnp.zeros((64, 128), f32)
        return put_out(0), sum_core(send(part(grads, 1 - core, n1), core_in, sibling))

    def part(ref, index, size):
        return ref.at[pl.ds(pl.multiple_of(index * size, size), size)]

    n1, n3 = 256, 256 // NP

    def sum_core(copy):
        copy.wait_recv()
        red1[...] = part(grads, core, n1)[...] + core_in[...]
        return [send(part(red1, plane_peer(r)[0], n3), plane_in.at[r - 1], plane_peer(r)[1]) for r in range(1, NP)]

    def sum_plane(copies):
        arrive(copies)
        acc = part(red1, plane, n3)[...]
        for r in range(1, NP):
            acc = acc + plane_in[r - 1]
        z_in[zc] = acc
        return [send(z_in.at[zc], z_in.at[zc], z_peer(r)) for r in range(1, NZ)]

    def sum_z(copies):
        arrive(copies)
        acc = z_in[0]
        for r in range(1, NZ):
            acc = acc + z_in[r]
        mine = part(total, core * NP + plane, n3)
        mine[...] = acc
        return [send(mine, mine, plane_peer(r)[1]) for r in range(1, NP)]

    def gather_core(copies):
        arrive(copies)
        mine = part(total, core, n1)
        return send(mine, mine, sibling)

    def everyone(value, slots, index, devices):
        slots[index] = value
        return [send(slots.at[index], slots.at[index], device) for device in devices]

    def summed_slots(copies, slots):
        arrive(copies)
        acc = slots[0]
        for n in range(1, slots.shape[0]):
            acc = acc + slots[n]
        return acc

    feat_out, copies2 = second_half_grads()
    inner = mm(errs[...].reshape(1536, 128), t["shift2"][...])
    arrive(copies)
    rows = [kept(has_below, col3_in[0]), kept(has_above, col3_in[1])]
    edge = mm(jnp.concatenate(rows, axis=0), t["put3"][...], TN)
    for wp in range(4):
        for dp in range(6):
            number = wp * 6 + dp
            for k in range(3):
                piece = inner[number * 64:number * 64 + 64, 128 * k:128 * k + 128]
                if k != 1:
                    lane = dp * 256 + 64 * k
                    piece = piece + edge[wp * 64:wp * 64 + 64, lane:lane + 128]
                fs[number, (2 - k) * 64:(2 - k) * 64 + 64, :] = piece.astype(bf16)

    for dq in range(4):
        def cols3(w):
            taps = [fs[(w + 2 - i) * 6 + dq + 2 - j] for i in range(3) for j in range(3)]
            return jnp.concatenate(taps + [jnp.zeros((64, 128), bf16)], axis=0)

        cols = jnp.concatenate([cols3(0), cols3(1)], axis=1)
        pe = mm(turned[...], cols).astype(bf16)
        both = mm(jnp.concatenate([pe[:, :128], pe[:, 128:]], axis=0), t["twice"][...]) * 0.125
        for w in range(2):
            perr[w, dq] = both[32 * w:32 * w + 32, :128]
            perr[w, dq + 4] = both[32 * w:32 * w + 32, 128:]

    def backward1(pd, acc):
        for w in range(4):
            here = perr[w // 2, pd]
            err = (jnp.concatenate([here, here], axis=1) * slope(pre1[w, pd])).astype(bf16)
            acc = acc + mm(err, cols1(w, pd), NT)
        return acc

    grad1 = lax.fori_loop(0, 8, backward1, jnp.zeros((32, 144), f32))
    one[...] = sum(mm(piece, t["narrow"][...]) for piece in split3(grad1))
    copies1 = send(part(one, 1 - core, 16), one_core, sibling)
    copies2 = sum_plane(copies2)
    copies1.wait_recv()
    copies1 = everyone(
        part(one, core, 16)[...] + one_core[...], one_plane, plane, [plane_peer(r)[1] for r in range(1, NP)]
    )
    copies2 = sum_z(copies2)
    copies1 = everyone(summed_slots(copies1, one_plane), one_z, zc, [z_peer(r) for r in range(1, NZ)])
    copy2 = gather_core(copies2)
    mine = part(one_total, core, 16)
    mine[...] = summed_slots(copies1, one_z)
    copy1 = send(mine, mine, sibling)
    copy2.wait_recv()
    sums2 = jnp.concatenate([total[l * 64:l * 64 + 64] for l in range(7)], axis=1)
    step2[...] = filt2[...] - learn_rate * sums2[:, :864]
    off2[...] = bias2[...] - learn_rate * column_to_row(sums2[:, 864:865])
    outs = [put_out(3), put_out(4)]
    copy1.wait_recv()
    sums1 = one_total[...]
    step1[...] = filt1[...] - learn_rate * sums1[:, :108]
    off1[...] = bias1[...] - learn_rate * column_to_row(sums1[:, 108:109])
    outs += [put_out(1), put_out(2)]

    for copy in started:
        copy.wait_send()
    feat_out.wait()
    for out in outs:
        out.wait()


def hand_on(*refs):
    ins, outs, spots, in_sems, out_sems = refs[:5], refs[5:10], refs[10:15], refs[15], refs[16]
    reads = [pltpu.make_async_copy(ins[n], spots[n], in_sems.at[n]) for n in range(5)]
    writes = [pltpu.make_async_copy(spots[n], outs[n], out_sems.at[n]) for n in range(5)]
    for copy in reads:
        copy.start()
    for n in (3, 0, 1, 2, 4):
        reads[n].wait()
        writes[n].start()
    for copy in writes:
        copy.wait()


def shards(volume, first_filters, first_bias, second_filters, second_bias, cotangent):
    GX, GY, GZ = lax.axis_size("gx"), lax.axis_size("gy"), lax.axis_size("gz")
    NX = 4 if GZ >= 8 else 2
    NZ = (GX // 2) * (GZ // NX)
    NP = NX * GY
    n3 = 256 // NP
    operands = [
        volume, first_filters, first_bias.reshape(1, 32), second_filters, second_bias.reshape(1, 64),
        cotangent.transpose(1, 2, 3, 0).reshape(128, 64), jnp.asarray(PACKED),
    ]
    sems = 62 + 4 + 3 * (NP - 1) + 2 * (NZ - 1)
    V = pltpu.VMEM
    results = (
        jax.ShapeDtypeStruct((128, 64), bf16),
        jax.ShapeDtypeStruct((32, 108), f32),
        jax.ShapeDtypeStruct((1, 32), f32),
        jax.ShapeDtypeStruct((64, 864), f32),
        jax.ShapeDtypeStruct((1, 64), f32),
    )
    out = pl.pallas_call(
        functools.partial(kernel, (GX, GY, GZ, NX)),
        out_shape=results,
        in_specs=[pl.BlockSpec(memory_space=pltpu.HBM)] * len(operands),
        out_specs=[pl.BlockSpec(memory_space=pltpu.HBM)] * 5,
        scratch_shapes=[
            V((32, 128), bf16), V((2, 4, 16, 128), bf16), V((2, 16, 128), bf16), V((4, 16, 128), bf16),
            V((16, 128), bf16), V((2, 3, 3, 16, 128), bf16), V((64, 2, 16, 128), bf16), V((4, 8, 32, 256), f32),
            V((2, 8, 32, 128), bf16),
            V((2, 128, 64), bf16), V((2, 32, 64), bf16), V((4, 32, 64), bf16),
            V((2, 4, 32, 128), bf16), V((2, 2, 32, 128), bf16), V((2, 2, 4, 32, 128), bf16),
            V((2, 2, 32, 128), bf16), V((4, 2, 32, 128), bf16), V((48, 32, 128), bf16),
            V((16, 128), bf16), V((2, 3, 3, 16, 128), bf16), V((48, 96, 128), bf16),
            V((4, 6, 64, 128), bf16), V((32, 256), bf16), V((2, 32, 256), bf16), V((24, 192, 128), bf16),
            V((32, 1792), bf16), V((2, 8, 32, 128), f32),
            V((512, 128), f32), V((256, 128), f32), V((256, 128), f32), V((NP - 1, n3, 128), f32),
            V((NZ, n3, 128), f32),
            V((512, 128), f32),
            V((32, 128), f32), V((16, 128), f32), V((NP, 16, 128), f32),
            V((NZ, 16, 128), f32), V((32, 128), f32),
            pltpu.SemaphoreType.DMA((sems,)), pltpu.SemaphoreType.DMA((sems,)),
        ] + [V(a.shape, a.dtype) for a in operands] + [
            pltpu.SemaphoreType.DMA((len(operands),)),
        ] + [V(a.shape, a.dtype) for a in results] + [
            pltpu.SemaphoreType.DMA((5,)),
        ],
        compiler_params=pltpu.CompilerParams(
            collective_id=0, has_side_effects=True, vmem_limit_bytes=62 * 2**20
        ),
    )(*operands)
    out = pl.pallas_call(
        hand_on,
        out_shape=results,
        in_specs=[pl.BlockSpec(memory_space=pltpu.HBM)] * 5,
        out_specs=[pl.BlockSpec(memory_space=pltpu.HBM)] * 5,
        scratch_shapes=[V(a.shape, a.dtype) for a in results]
        + [pltpu.SemaphoreType.DMA((5,)), pltpu.SemaphoreType.DMA((5,))],
        compiler_params=pltpu.CompilerParams(vmem_limit_bytes=62 * 2**20),
    )(*out)
    features, stepped_first, offset_first, stepped_second, offset_second = out
    return (
        features.reshape(1, 4, 32, 64).transpose(3, 0, 1, 2), stepped_first, offset_first.reshape(32), stepped_second,
        offset_second.reshape(64),
    )


def solution(mesh):
    return jax.shard_map(
        shards,
        mesh=mesh,
        in_specs=(P(None, "gx", "gz", "gy"), P(), P(), P(), P(), P(None, "gx", "gz", "gy")),
        out_specs=(P(None, "gx", "gz", "gy"), P(), P(), P(), P()),
        check_vma=False,
    )
```

```python
import functools

import jax
import jax.numpy as jnp
import numpy as np
from jax import lax
from jax.experimental import pallas as pl
from jax.experimental.pallas import tpu as pltpu
from jax.sharding import PartitionSpec as P

slope_below = 0.3
learn_rate = 0.001
f32 = jnp.float32
bf16 = jnp.bfloat16
MESH = pl.DeviceIdType.MESH
NN = (((1,), (0,)), ((), ()))
NT = (((1,), (1,)), ((), ()))
TN = (((0,), (0,)), ((), ()))


def mm(a, b, dims=NN):
    return lax.dot_general(a, b, dims, preferred_element_type=f32)


def tables():
    place = np.zeros((512, 480))
    for wp in range(6):
        for dp in range(18):
            for ch in range(4):
                w, d = wp - 1, dp - 1
                inner_w, inner_d = 0 <= w < 4, 0 <= d < 16
                if inner_w and inner_d:
                    src = (ch * 4 + w) * 16 + d
                elif inner_d:
                    src = 256 + (64 if w > 0 else 0) + ch * 16 + d
                elif inner_w:
                    src = 384 + (16 if d > 0 else 0) + ch * 4 + w
                else:
                    a, b = int(w > 0), int(d > 0)
                    src = 416 + (a * 2 + b) * 16 + ch * 4 + (0 if a else 3)
                place[(wp * 18 + dp) * 4 + ch, src] = 1
    shift1 = np.zeros((128, 384))
    for l in range(128):
        if l:
            shift1[l - 1, l] = 1
        shift1[l, 128 + l] = 1
        if l < 127:
            shift1[l + 1, 256 + l] = 1
    order1 = np.zeros((1152, 128))
    for wp in range(6):
        for dp in range(18):
            a, b = (wp > 0) + (wp > 4), (dp > 0) + (dp > 16)
            w, d = (3, wp - 1, 0)[a], (15, dp - 1, 0)[b]
            order1[(a * 3 + b) * 128 + w * 16 + d, wp * 18 + dp] = 1
    four = np.zeros((128, 512))
    for q in range(512):
        four[q // 4, q] = 1
    put1 = np.zeros((32, 256))
    for ch in range(4):
        put1[ch * 2 + 1, 0] = put1[16 + ch * 2, 255] = 1
    shift2 = np.zeros((128, 384))
    swapped = np.zeros((128, 384))
    for l in range(128):
        for k in range(3):
            s = l % 64 + k - 1
            if 0 <= s < 64:
                s += l - l % 64
                shift2[s, k * 128 + l] = 1
                swapped[(s + 64) % 128, k * 128 + l] = 1
    ends = (0, 63, 64, 127)
    pick2 = np.zeros((16, 512))
    for dq in range(4):
        for n, l in enumerate(ends):
            pick2[dq * 4 + n, dq * 128 + l] = 1
    put2 = np.zeros((96, 2048))
    for dq in range(-2, 6):
        for half in range(2):
            d = dq + 4 * half
            dz = (d >= 0) + (d > 7)
            there, row = (d % 8) // 4, (d % 4) * 4
            put2[dz * 16 + row + 2 * there + 1, (dq + 2) * 256 + 64 * half] = 1
            put2[48 + dz * 16 + row + 2 * there, (dq + 2) * 256 + 128 + 64 * half + 63] = 1
    pick3 = np.zeros((32, 768))
    put3 = np.zeros((64, 1536))
    for dq in range(6):
        for n, l in enumerate(ends):
            pick3[dq * 4 + n, dq * 128 + l] = 1
        for half in range(2):
            put3[dq * 4 + 2 * half + 1, dq * 256 + 64 * half] = 1
            put3[32 + dq * 4 + 2 * half, dq * 256 + 128 + 64 * half + 63] = 1
    even = np.zeros((256, 128))
    for half in range(2):
        for h in range(64):
            even[half * 128 + 2 * h, half * 64 + h] = 1
    twice = np.zeros((128, 256))
    for half in range(2):
        for h in range(128):
            twice[half * 64 + h // 2, half * 128 + h] = 1
    spread = np.zeros((192, 512))
    for dc in range(-1, 5):
        for hc in range(32):
            row = (128 if dc < 0 else 160 if dc > 3 else dc * 32) + hc
            for t in range(2):
                for half in range(2):
                    kind = {0: 0, 1: 1, -1: 2, 2: 3}.get(dc - 2 * half)
                    if kind is not None:
                        spread[row, kind * 128 + half * 64 + 2 * hc + t] = 1
    collect = np.zeros((256, 128))
    for dc in range(4):
        for hc in range(32):
            collect[(dc % 2) * 128 + dc * 32 + hc, (dc // 2) * 64 + 2 * hc] = 1
    widen = np.zeros((108, 144))
    narrow = np.zeros((144, 128))
    for q in range(108):
        widen[q, (q // 12) * 16 + q % 12] = 1
        narrow[(q // 12) * 16 + q % 12, q] = 1
    narrow[12, 108] = 1
    ident = np.zeros((64, 256))
    for o in range(64):
        ident[o, o] = ident[o, 128 + 64 + o] = 1
    every = dict(
        place=place, shift1=shift1, order1=order1, four=four, put1=put1, shift2=shift2, swapped=swapped,
        pick2=pick2, put2=put2, pick3=pick3, put3=put3, even=even, twice=twice, spread=spread, collect=collect,
        widen=widen, narrow=narrow, ident=ident,
    )
    return every


TABLE = {}


def packed_table():
    parts, row = [], 0
    for name, value in tables().items():
        rows, lanes = value.shape
        if name == "order1":
            value = np.concatenate(np.split(value, 4), axis=1)
            rows //= 4
        wide = np.zeros((-(-rows // 16) * 16, -(-lanes // 512) * 512))
        wide[:rows, :value.shape[1]] = value
        wide = np.concatenate(np.split(wide, wide.shape[1] // 512, axis=1))
        TABLE[name] = (row, rows, lanes)
        row += wide.shape[0]
        parts.append(wide)
    return np.concatenate(parts).astype(jnp.bfloat16)


PACKED = packed_table()


class Rows:
    def __init__(self, ref, name):
        self.ref = ref
        self.row, self.rows, self.lanes = TABLE[name]

    def folded(self):
        return jnp.concatenate(
            [self.ref[self.row:self.row + self.rows, 128 * n:128 * n + 128] for n in range(4)], axis=0
        )

    def __getitem__(self, key):
        if self.lanes > 512:
            step = -(-self.rows // 16) * 16
            return jnp.concatenate(
                [self.ref[self.row + n * step:self.row + n * step + self.rows, :] for n in range(-(-self.lanes // 512))],
                axis=1,
            )
        if key is Ellipsis:
            return self.ref[self.row:self.row + self.rows, :self.lanes]
        return self.ref[self.row + key.start:self.row + key.stop, :self.lanes]


def row_to_column(row):
    n = row.shape[1]
    diagonal = lax.broadcasted_iota(jnp.int32, (n, n), 0) == lax.broadcasted_iota(jnp.int32, (n, n), 1)
    return jnp.sum(jnp.where(diagonal, jnp.broadcast_to(row, (n, n)), 0.0), axis=1, keepdims=True)


def column_to_row(column):
    n = column.shape[0]
    diagonal = lax.broadcasted_iota(jnp.int32, (n, n), 0) == lax.broadcasted_iota(jnp.int32, (n, n), 1)
    return jnp.sum(jnp.where(diagonal, jnp.broadcast_to(column, (n, n)), 0.0), axis=0, keepdims=True)


def kept(flag, value):
    return lax.select(flag, value, jnp.zeros_like(value))


def leaky(a):
    return jnp.where(a > 0, a, slope_below * a)


def slope(a):
    return jnp.where(a > 0, 1.0, slope_below)


def split3(a):
    high = a.astype(bf16)
    rest = a - high.astype(f32)
    mid = rest.astype(bf16)
    return high, mid, (rest - mid.astype(f32)).astype(bf16)


def kernel(sizes, *refs):
    GX, GY, GZ, NX = sizes
    ZL = GZ // NX
    ZH = GX // 2
    NZ = ZH * ZL
    far = refs[:7]
    refs = refs[7:]
    far_out = refs[:5]
    (
        edges, wide_in, deep_in, corner_in, col1, col1_in, xs, pre1,
        wide_t, deep_t, corner_t, pooled, packs, wide2, deep2, corner2, v2, col2, col2_in, ys,
        errs, col3, col3_in, fs, turned, perr,
        grads, core_in, red1, plane_in, z_in, total,
        one, one_core, one_plane, one_z, one_total, send_sems, recv_sems, vol, filt1, bias1, filt2, bias2, cot, packed, in_sems,
        feat, step1, off1, step2, off2, out_sems,
    ) = refs[5:]
    near = (vol, filt1, bias1, filt2, bias2, cot, packed)
    fetches = [pltpu.make_async_copy(a, b, in_sems.at[n]) for n, (a, b) in enumerate(zip(far, near))]
    for fetch in fetches:
        fetch.start()
    t = {name: Rows(packed, name) for name in TABLE}

    gx, gy, gz = lax.axis_index("gx"), lax.axis_index("gy"), lax.axis_index("gz")
    core, zh = lax.rem(gx, 2), lax.div(gx, 2)
    xc, zl = lax.rem(gz, NX), lax.div(gz, NX)
    zc = zh * ZL + zl

    def shifted(dx, dy, dz):
        return (lax.rem(gx + (dx + GX), GX), lax.rem(gy + (dy + GY), GY), lax.rem(gz + (dz + GZ), GZ))

    sibling = (gx + 1 - 2 * core, gy, gz)

    plane = xc * GY + gy
    NP = NX * GY

    def ring_gap(n, r):
        return min(r, n - r)

    plane_steps = [(rx, ry) for rx in range(NX) for ry in range(GY) if rx or ry]
    plane_steps.sort(key=lambda step: -ring_gap(NX, step[0]) - ring_gap(GY, step[1]))
    z_steps = sorted(range(1, NZ), key=lambda r: -ring_gap(NZ, r))

    def plane_peer(step):
        px, py = lax.rem(xc + step[0], NX), lax.rem(gy + step[1], GY)
        return px * GY + py, (gx, py, zl * NX + px)

    def z_peer(r):
        p = lax.rem(zc + r, NZ)
        return (2 * lax.div(p, ZL) + core, gy, lax.rem(p, ZL) * NX + xc)

    square = [(dx, dz) for dx in (-1, 1, 0) for dz in (-1, 1, 0)]
    square.sort(key=lambda step: -abs(step[0]) - abs(step[1]))
    peers = [shifted(dx, dy, dz) for dx, dz in square for dy in (-1, 1)]
    peers += [shifted(dx, 0, dz) for dx, dz in square if (dx, dz) != (0, 0)]
    peers += [plane_peer(step)[1] for step in plane_steps]
    peers += [z_peer(r) for r in z_steps]
    barrier = pltpu.get_barrier_semaphore()
    for peer in peers:
        pl.semaphore_signal(barrier, inc=1, device_id=peer, device_id_type=MESH)

    count = [0]
    started = []

    def send(src, dst, device):
        n = count[0]
        count[0] += 1
        copy = pltpu.make_async_remote_copy(
            src_ref=src, dst_ref=dst, send_sem=send_sems.at[n], recv_sem=recv_sems.at[n],
            device_id=device, device_id_type=MESH,
        )
        copy.start()
        started.append(copy)
        return copy

    def drain(keep):
        while len(started) > keep:
            started.pop(0).wait_send()

    def put_out(n):
        copy = pltpu.make_async_copy((feat, step1, off1, step2, off2)[n], far_out[n], out_sems.at[n])
        copy.start()
        return copy

    def arrive(copies):
        for copy in copies:
            copy.wait_recv()

    row = lax.broadcasted_iota(jnp.int32, (32, 256), 0)
    column = lax.broadcasted_iota(jnp.int32, (32, 256), 1)
    wanted = jnp.where(row < 16, row * 16, row * 16 - 241)
    edge = jnp.where(column == wanted, 1.0, 0.0).astype(bf16)
    fetches[0].wait()
    block = vol[...].reshape(256, 128)
    edges[...] = mm(edge, block).astype(bf16)
    pl.semaphore_wait(barrier, len(peers))

    has_left, has_right = gx > 0, gx < GX - 1
    has_front, has_back = gz > 0, gz < GZ - 1
    has_below, has_above = gy > 0, gy < GY - 1

    def send_ring(wide_src, wide_dst, deep_src, deep_dst, corner_src, corner_dst):
        copies = []
        for a in range(2):
            dx = 1 if a == 0 else -1
            copies.append(send(wide_src(a), wide_dst.at[a], shifted(dx, 0, 0)))
        for b in range(2):
            dz = 1 if b == 0 else -1
            copies.append(send(deep_src(b), deep_dst.at[b], shifted(0, 0, dz)))
        for a in range(2):
            for b in range(2):
                copies.append(
                    send(corner_src(a, b), corner_dst.at[a * 2 + b], shifted(1 if a == 0 else -1, 0, 1 if b == 0 else -1))
                )
        return copies

    def send_columns(src, dst):
        copies = []
        for dx, dz in square:
            for side in range(2):
                dy = 1 if side == 0 else -1
                copies.append(send(src, dst.at[side, 1 - dx, 1 - dz], shifted(dx, dy, dz)))
        return copies

    def columns_in(dst, dx):
        rows = []
        for side in range(2):
            for dz in (-1, 0, 1):
                flag = (has_below, has_above)[side]
                if dx:
                    flag = jnp.logical_and(flag, edge_flags[(dx + 1) // 2])
                if dz:
                    flag = jnp.logical_and(flag, deep_flags[(dz + 1) // 2])
                rows.append(kept(flag, dst[side, dx + 1, dz + 1]))
        return rows

    edge_flags = (has_left, has_right)
    deep_flags = (has_front, has_back)

    def edge_rows(b):
        return edges.at[pl.ds(16, 16)] if b == 0 else edges.at[pl.ds(0, 16)]

    copies = send_ring(
        lambda a: vol.at[:, 3] if a == 0 else vol.at[:, 0], wide_in,
        edge_rows, deep_in, lambda a, b: edge_rows(b), corner_in,
    )

    row = lax.broadcasted_iota(jnp.int32, (16, 512), 0)
    column = lax.broadcasted_iota(jnp.int32, (16, 512), 1)
    wanted = jnp.where(row < 8, lax.div(row, 2) * 128 + lax.rem(row, 2) * 127, -1)
    pick1 = jnp.where(column == wanted, 1.0, 0.0).astype(bf16)
    ends = sum(
        mm(pick1[:, 128 * ch:128 * ch + 128], vol[ch].reshape(64, 128), NT) for ch in range(4)
    )
    col1[...] = jnp.concatenate([ends, jnp.zeros((16, 64), f32)], axis=1).astype(bf16)
    copies_c = send_columns(col1, col1_in)
    for fetch in fetches[1:]:
        fetch.wait()
    first_half = filt1[...].astype(bf16)
    wide_first = mm(first_half, t["widen"][...]).astype(bf16)
    bias1_col = row_to_column(bias1[...])
    bias2_col = row_to_column(bias2[...])
    second_half = filt2[...].astype(bf16)

    copies_t = send_ring(
        lambda a: cot, wide_t, lambda b: cot.at[96:128] if b == 0 else cot.at[0:32], deep_t,
        lambda a, b: cot.at[96:128] if b == 0 else cot.at[0:32], corner_t,
    )

    turn = mm(second_half, t["ident"][...], TN).astype(bf16)
    for m in range(13):
        low = turn[64 * m:64 * m + 32, :128].astype(f32)
        high = turn[64 * m + 32:64 * m + 64, 128:].astype(f32)
        turned[:, 128 * m:128 * m + 128] = (low + high).astype(bf16)
    turned[:, 1664:1792] = turn[832:864, :128]

    arrive(copies)
    pieces = [block]
    for a in range(2):
        pieces.append(kept(edge_flags[a], wide_in[a]).reshape(64, 128))
    for b in range(2):
        pieces.append(kept(deep_flags[b], deep_in[b]))
    for a in range(2):
        for b in range(2):
            pieces.append(kept(jnp.logical_and(edge_flags[a], deep_flags[b]), corner_in[a * 2 + b]))
    rows = mm(t["place"][...], jnp.concatenate(pieces, axis=0)).astype(bf16)
    inner = mm(rows, t["shift1"][...])
    arrive(copies_c)
    columns = [columns_in(col1_in, dx) for dx in (-1, 0, 1)]
    sides = [
        jnp.concatenate([columns[a][side * 3 + b] for a in range(3) for b in range(3)], axis=1)
        for side in range(2)
    ]
    ordered = mm(jnp.concatenate(sides, axis=0), t["order1"].folded()).astype(bf16)
    ordered = mm(ordered, t["four"][...])
    row = lax.broadcasted_iota(jnp.int32, (32, 512), 0)
    column = lax.broadcasted_iota(jnp.int32, (32, 512), 1)
    same = lax.rem(lax.div(row, 2), 8) == lax.rem(column, 4)
    ordered = jnp.where(same, ordered, 0.0).astype(bf16)
    ends = mm(ordered, t["put1"][...], TN)
    full = [inner[:, :128] + ends[:, :128], inner[:, 128:256], inner[:, 256:] + ends[:, 128:]]
    third = [piece.reshape(64, 8, 128) for piece in full]
    rolled = [pltpu.roll(piece, 4, axis=1) for piece in third]
    sub = lax.broadcasted_iota(jnp.int32, (64, 8, 128), 1)
    upper = sub < 4
    ones = jnp.where(sub == 4, 1.0, 0.0)
    even_tile = jnp.concatenate(
        [jnp.where(upper, third[0], rolled[1]), jnp.where(upper, third[2], ones)], axis=1
    )
    odd_tile = jnp.concatenate(
        [jnp.where(upper, rolled[0], third[1]), jnp.where(upper, rolled[2], ones)], axis=1
    )
    xs[:, 0] = even_tile.astype(bf16)
    xs[:, 1] = odd_tile.astype(bf16)

    def cols1(w, half_d):
        def at(i, dp, parity):
            return xs[(w + i) * 9 + dp, parity]

        one = [at(i, half_d + j // 2, j % 2) for i in range(3) for j in range(3)]
        two = [at(i, half_d + (j + 1) // 2, (j + 1) % 2) for i in range(3) for j in range(3)]
        return jnp.concatenate(
            [jnp.concatenate(one, axis=0), jnp.concatenate(two, axis=0)], axis=1
        )

    def turned_half(a):
        return pltpu.roll(a.astype(f32), 64, axis=1)

    low = lax.broadcasted_iota(jnp.int32, (32, 128), 1) < 64

    def halves(a, b):
        return jnp.where(low, a.astype(f32), b.astype(f32)).astype(bf16)

    copies = []
    for dq in range(4):
        sums = [[None, None], [None, None]]
        for half in range(2):
            pd = dq + 4 * half
            for pw in range(2):
                both = None
                for w in (2 * pw, 2 * pw + 1):
                    pre = mm(wide_first, cols1(w, pd)) + bias1_col
                    pre1[w, pd] = pre
                    act = leaky(pre)
                    act = act[:, :128] + act[:, 128:]
                    both = act if both is None else both + act
                sums[pw][half] = ((both + pltpu.roll(both, 127, axis=1)) * 0.125).astype(bf16)
        lanes = [jnp.concatenate([sums[0][half], sums[1][half]], axis=0) for half in range(2)]
        value = (mm(lanes[0], t["even"][0:128]) + mm(lanes[1], t["even"][128:256])).astype(bf16)
        pooled[:, dq] = value.reshape(2, 32, 128)
        for a in range(2):
            copies.append(send(pooled.at[:, dq], wide2.at[a, :, dq], shifted(1 - 2 * a, 0, 0)))
        if dq % 2:
            b = 0 if dq == 3 else 1
            for w in range(2):
                if b == 0:
                    packs[0, w] = halves(turned_half(pooled[w, 2]), pooled[w, 3])
                else:
                    packs[1, w] = halves(pooled[w, 0], turned_half(pooled[w, 1]))
            copies.append(send(packs.at[b], deep2.at[b], shifted(0, 0, 1 - 2 * b)))
            for a in range(2):
                copies.append(send(packs.at[b], corner2.at[a * 2 + b], shifted(1 - 2 * a, 0, 1 - 2 * b)))
    pick = t["pick2"][...]
    ends = sum(
        mm(pick[:, 128 * dq:128 * dq + 128], pooled[:, dq].reshape(64, 128), NT) for dq in range(4)
    )
    col2[...] = jnp.concatenate([ends, jnp.zeros((16, 64), f32)], axis=1).astype(bf16)
    copies_c = send_columns(col2, col2_in)

    arrive(copies_t)
    spread_cot = []
    for dx in (-1, 0, 1):
        a = max(dx, 0)
        beside = edge_flags[a]
        if dx:
            rows = [kept(beside, wide_t[a])]
            rows += [kept(jnp.logical_and(beside, deep_flags[b]), corner_t[a * 2 + b]) for b in range(2)]
        else:
            rows = [cot[...]] + [kept(deep_flags[b], deep_t[b]) for b in range(2)]
        spread_cot.append(mm(jnp.concatenate(rows, axis=0), t["spread"][...], TN) * 0.125)

    arrive(copies)
    for wp in range(6):
        a, w = wp // 4, wp % 2
        if wp in (2, 3):
            near = [pooled[w, dq] for dq in range(4)]
            front, back = (kept(deep_flags[b], deep2[b, w]) for b in range(2))
        else:
            near = [kept(edge_flags[a], wide2[a, w, dq]) for dq in range(4)]
            front, back = (
                kept(jnp.logical_and(edge_flags[a], deep_flags[b]), corner2[a * 2 + b, w]) for b in range(2)
            )
        for dq in range(4):
            v2[wp * 6 + dq] = near[dq]
        v2[wp * 6 + 4] = halves(front, turned_half(near[2]))
        v2[wp * 6 + 5] = halves(turned_half(near[1]), back)
        v2[36 + wp] = halves(near[3], front)
        v2[42 + wp] = halves(back, near[0])
    inner = jnp.concatenate(
        [mm(v2[0:36].reshape(1152, 128), t["shift2"][...]), mm(v2[36:48].reshape(384, 128), t["swapped"][...])],
        axis=0,
    )
    arrive(copies_c)
    put = t["put2"][...]
    edge = [mm(jnp.concatenate(columns_in(col2_in, dx), axis=0), put, TN) for dx in (-1, 0, 1)]
    for wp in range(6):
        for dp in range(8):
            number = {0: wp * 6 + 4, 1: 36 + wp, 6: 42 + wp, 7: wp * 6 + 5}.get(dp, wp * 6 + dp - 2)
            for k in range(3):
                piece = inner[number * 32:number * 32 + 32, 128 * k:128 * k + 128]
                if k != 1:
                    lane = dp * 256 + 64 * k
                    piece = piece + edge[wp // 2][(wp % 2) * 32:(wp % 2) * 32 + 32, lane:lane + 128]
                ys[wp * 8 + dp, k * 32:k * 32 + 32, :] = piece.astype(bf16)

    def cols2(w, dq, extra):
        taps = [ys[(w + i) * 8 + dq + j] for i in range(3) for j in range(3)]
        return jnp.concatenate(taps + extra, axis=0)

    feat_sum = [None, None]
    for dq in range(6):
        kind = {0: 2, 5: 3}.get(dq, (dq - 1) // 2)
        for pair in ((1, 2), (0, 3)):
            cols = jnp.concatenate([cols2(w, dq, []) for w in pair], axis=1)
            pre = mm(second_half, cols) + bias2_col
            if pair == (1, 2) and 0 < dq < 5:
                act = leaky(pre)
                act = act[:, :128] + act[:, 128:]
                feat_sum[kind] = act if feat_sum[kind] is None else feat_sum[kind] + act
            for n, w in enumerate(pair):
                here = spread_cot[(w + 1) // 2][:, 128 * kind:128 * kind + 128]
                errs[w, dq] = (here * slope(pre[:, 128 * n:128 * n + 128])).astype(bf16)

    pick = t["pick3"][...]
    col3[...] = sum(
        mm(pick[:, 128 * dq:128 * dq + 128], errs[:, dq].reshape(256, 128), NT) for dq in range(6)
    ).astype(bf16)
    copies = [send(col3, col3_in.at[0], shifted(0, 1, 0)), send(col3, col3_in.at[1], shifted(0, -1, 0))]

    def second_half_grads():
        ends = [
            ((both + pltpu.roll(both, 127, axis=1)) * 0.125).astype(bf16) for both in feat_sum
        ]
        feat[...] = (mm(t["collect"][0:128], ends[0], NT) + mm(t["collect"][128:256], ends[1], NT)).astype(bf16)
        ones_rows = [jnp.ones((32, 128), bf16)]
        grad2 = None
        for dq in range(4):
            cols = jnp.concatenate([cols2(w, dq + 1, ones_rows) for w in (1, 2)], axis=1)
            err = jnp.concatenate([errs[w, dq + 1] for w in (1, 2)], axis=1)
            piece = mm(err, cols, NT)
            grad2 = piece if grad2 is None else grad2 + piece
        for l in range(7):
            grads[l * 64:l * 64 + 64] = grad2[:, 128 * l:128 * l + 128]
        grads[448:512] = jnp.zeros((64, 128), f32)
        return put_out(0), sum_core(send(part(grads, 1 - core, n1), core_in, sibling))

    def part(ref, index, size):
        return ref.at[pl.ds(pl.multiple_of(index * size, size), size)]

    n1, n3 = 256, 256 // NP

    def sum_core(copy):
        copy.wait_recv()
        red1[...] = part(grads, core, n1)[...] + core_in[...]
        copies = []
        for n, step in enumerate(plane_steps):
            p, device = plane_peer(step)
            copies.append(send(part(red1, p, n3), plane_in.at[n], device))
        return copies

    def sum_plane(copies):
        arrive(copies)
        acc = part(red1, plane, n3)[...]
        for r in range(1, NP):
            acc = acc + plane_in[r - 1]
        z_in[zc] = acc
        return [send(z_in.at[zc], z_in.at[zc], z_peer(r)) for r in z_steps]

    def sum_z(copies):
        arrive(copies)
        acc = z_in[0]
        for r in range(1, NZ):
            acc = acc + z_in[r]
        mine = part(total, core * NP + plane, n3)
        mine[...] = acc
        return [send(mine, mine, plane_peer(step)[1]) for step in plane_steps]

    def gather_core(copies):
        arrive(copies)
        mine = part(total, core, n1)
        return send(mine, mine, sibling)

    def everyone(value, slots, index, devices):
        slots[index] = value
        return [send(slots.at[index], slots.at[index], device) for device in devices]

    def summed_slots(copies, slots):
        arrive(copies)
        acc = slots[0]
        for n in range(1, slots.shape[0]):
            acc = acc + slots[n]
        return acc

    feat_out, copies2 = second_half_grads()
    inner = mm(errs[...].reshape(1536, 128), t["shift2"][...])
    arrive(copies)
    rows = [kept(has_below, col3_in[0]), kept(has_above, col3_in[1])]
    edge = mm(jnp.concatenate(rows, axis=0), t["put3"][...], TN)
    for wp in range(4):
        for dp in range(6):
            number = wp * 6 + dp
            for k in range(3):
                piece = inner[number * 64:number * 64 + 64, 128 * k:128 * k + 128]
                if k != 1:
                    lane = dp * 256 + 64 * k
                    piece = piece + edge[wp * 64:wp * 64 + 64, lane:lane + 128]
                fs[number, (2 - k) * 64:(2 - k) * 64 + 64, :] = piece.astype(bf16)

    for dq in range(4):
        def cols3(w):
            taps = [fs[(w + 2 - i) * 6 + dq + 2 - j] for i in range(3) for j in range(3)]
            return jnp.concatenate(taps + [jnp.zeros((64, 128), bf16)], axis=0)

        cols = jnp.concatenate([cols3(0), cols3(1)], axis=1)
        pe = mm(turned[...], cols).astype(bf16)
        both = mm(jnp.concatenate([pe[:, :128], pe[:, 128:]], axis=0), t["twice"][...]) * 0.125
        for w in range(2):
            perr[w, dq] = both[32 * w:32 * w + 32, :128]
            perr[w, dq + 4] = both[32 * w:32 * w + 32, 128:]

    grad1 = None
    for pd in range(8):
        for w in range(4):
            here = perr[w // 2, pd]
            err = (jnp.concatenate([here, here], axis=1) * slope(pre1[w, pd])).astype(bf16)
            piece = mm(err, cols1(w, pd), NT)
            grad1 = piece if grad1 is None else grad1 + piece
    one[...] = sum(mm(piece, t["narrow"][...]) for piece in split3(grad1))
    copies1 = send(part(one, 1 - core, 16), one_core, sibling)
    copies2 = sum_plane(copies2)
    drain(NP + NZ)
    copies1.wait_recv()
    copies1 = everyone(
        part(one, core, 16)[...] + one_core[...], one_plane, plane, [plane_peer(step)[1] for step in plane_steps]
    )
    drain(NP)
    copies2 = sum_z(copies2)
    copies1 = everyone(summed_slots(copies1, one_plane), one_z, zc, [z_peer(r) for r in z_steps])
    copy2 = gather_core(copies2)
    drain(1)
    mine = part(one_total, core, 16)
    mine[...] = summed_slots(copies1, one_z)
    copy1 = send(mine, mine, sibling)
    copy2.wait_recv()
    sums2 = jnp.concatenate([total[l * 64:l * 64 + 64] for l in range(7)], axis=1)
    step2[...] = filt2[...] - learn_rate * sums2[:, :864]
    off2[...] = bias2[...] - learn_rate * column_to_row(sums2[:, 864:865])
    outs = [put_out(3), put_out(4)]
    copy1.wait_recv()
    sums1 = one_total[...]
    step1[...] = filt1[...] - learn_rate * sums1[:, :108]
    off1[...] = bias1[...] - learn_rate * column_to_row(sums1[:, 108:109])
    outs += [put_out(1), put_out(2)]

    drain(0)
    feat_out.wait()
    for out in outs:
        out.wait()


def hand_on(*refs):
    ins, outs, spots, in_sems, out_sems = refs[:5], refs[5:10], refs[10:15], refs[15], refs[16]
    reads = [pltpu.make_async_copy(ins[n], spots[n], in_sems.at[n]) for n in range(5)]
    writes = [pltpu.make_async_copy(spots[n], outs[n], out_sems.at[n]) for n in range(5)]
    for copy in reads:
        copy.start()
    for n in (3, 0, 1, 2, 4):
        reads[n].wait()
        writes[n].start()
    for copy in writes:
        copy.wait()


def shards(volume, first_filters, first_bias, second_filters, second_bias, cotangent):
    GX, GY, GZ = lax.axis_size("gx"), lax.axis_size("gy"), lax.axis_size("gz")
    NX = 4 if GZ >= 8 else 2
    NZ = (GX // 2) * (GZ // NX)
    NP = NX * GY
    n3 = 256 // NP
    operands = [
        volume, first_filters, first_bias.reshape(1, 32), second_filters, second_bias.reshape(1, 64),
        cotangent.transpose(1, 2, 3, 0).reshape(128, 64), jnp.asarray(PACKED),
    ]
    sems = 68 + 4 + 3 * (NP - 1) + 2 * (NZ - 1)
    V = pltpu.VMEM
    results = (
        jax.ShapeDtypeStruct((128, 64), bf16),
        jax.ShapeDtypeStruct((32, 108), f32),
        jax.ShapeDtypeStruct((1, 32), f32),
        jax.ShapeDtypeStruct((64, 864), f32),
        jax.ShapeDtypeStruct((1, 64), f32),
    )
    out = pl.pallas_call(
        functools.partial(kernel, (GX, GY, GZ, NX)),
        out_shape=results,
        in_specs=[pl.BlockSpec(memory_space=pltpu.HBM)] * len(operands),
        out_specs=[pl.BlockSpec(memory_space=pltpu.HBM)] * 5,
        scratch_shapes=[
            V((32, 128), bf16), V((2, 4, 16, 128), bf16), V((2, 16, 128), bf16), V((4, 16, 128), bf16),
            V((16, 128), bf16), V((2, 3, 3, 16, 128), bf16), V((64, 2, 16, 128), bf16), V((4, 8, 32, 256), f32),
            V((2, 128, 64), bf16), V((2, 32, 64), bf16), V((4, 32, 64), bf16),
            V((2, 4, 32, 128), bf16), V((2, 2, 32, 128), bf16), V((2, 2, 4, 32, 128), bf16),
            V((2, 2, 32, 128), bf16), V((4, 2, 32, 128), bf16), V((48, 32, 128), bf16),
            V((16, 128), bf16), V((2, 3, 3, 16, 128), bf16), V((48, 96, 128), bf16),
            V((4, 6, 64, 128), bf16), V((32, 256), bf16), V((2, 32, 256), bf16), V((24, 192, 128), bf16),
            V((32, 1792), bf16), V((2, 8, 32, 128), f32),
            V((512, 128), f32), V((256, 128), f32), V((256, 128), f32), V((NP - 1, n3, 128), f32),
            V((NZ, n3, 128), f32),
            V((512, 128), f32),
            V((32, 128), f32), V((16, 128), f32), V((NP, 16, 128), f32),
            V((NZ, 16, 128), f32), V((32, 128), f32),
            pltpu.SemaphoreType.DMA((sems,)), pltpu.SemaphoreType.DMA((sems,)),
        ] + [V(a.shape, a.dtype) for a in operands] + [
            pltpu.SemaphoreType.DMA((len(operands),)),
        ] + [V(a.shape, a.dtype) for a in results] + [
            pltpu.SemaphoreType.DMA((5,)),
        ],
        compiler_params=pltpu.CompilerParams(
            collective_id=0, has_side_effects=True, vmem_limit_bytes=62 * 2**20
        ),
    )(*operands)
    out = pl.pallas_call(
        hand_on,
        out_shape=results,
        in_specs=[pl.BlockSpec(memory_space=pltpu.HBM)] * 5,
        out_specs=[pl.BlockSpec(memory_space=pltpu.HBM)] * 5,
        scratch_shapes=[V(a.shape, a.dtype) for a in results]
        + [pltpu.SemaphoreType.DMA((5,)), pltpu.SemaphoreType.DMA((5,))],
        compiler_params=pltpu.CompilerParams(vmem_limit_bytes=62 * 2**20),
    )(*out)
    features, stepped_first, offset_first, stepped_second, offset_second = out
    return (
        features.reshape(1, 4, 32, 64).transpose(3, 0, 1, 2), stepped_first, offset_first.reshape(32), stepped_second,
        offset_second.reshape(64),
    )


def solution(mesh):
    return jax.shard_map(
        shards,
        mesh=mesh,
        in_specs=(P(None, "gx", "gz", "gy"), P(), P(), P(), P(), P(None, "gx", "gz", "gy")),
        out_specs=(P(None, "gx", "gz", "gy"), P(), P(), P(), P()),
        check_vma=False,
    )
```

```python
import functools

import jax
import jax.numpy as jnp
import numpy as np
from jax import lax
from jax.experimental import pallas as pl
from jax.experimental.pallas import tpu as pltpu
from jax.sharding import PartitionSpec as P

slope_below = 0.3
learn_rate = 0.001
f32 = jnp.float32
bf16 = jnp.bfloat16
MESH = pl.DeviceIdType.MESH
NN = (((1,), (0,)), ((), ()))
NT = (((1,), (1,)), ((), ()))
TN = (((0,), (0,)), ((), ()))


def mm(a, b, dims=NN):
    return lax.dot_general(a, b, dims, preferred_element_type=f32)


def tables():
    place = np.zeros((512, 480))
    for wp in range(6):
        for dp in range(18):
            for ch in range(4):
                w, d = wp - 1, dp - 1
                inner_w, inner_d = 0 <= w < 4, 0 <= d < 16
                if inner_w and inner_d:
                    src = (ch * 4 + w) * 16 + d
                elif inner_d:
                    src = 256 + (64 if w > 0 else 0) + ch * 16 + d
                elif inner_w:
                    src = 384 + (16 if d > 0 else 0) + ch * 4 + w
                else:
                    a, b = int(w > 0), int(d > 0)
                    src = 416 + (a * 2 + b) * 16 + ch * 4 + (0 if a else 3)
                place[(wp * 18 + dp) * 4 + ch, src] = 1
    shift1 = np.zeros((128, 384))
    for l in range(128):
        if l:
            shift1[l - 1, l] = 1
        shift1[l, 128 + l] = 1
        if l < 127:
            shift1[l + 1, 256 + l] = 1
    order1 = np.zeros((1152, 128))
    for wp in range(6):
        for dp in range(18):
            a, b = (wp > 0) + (wp > 4), (dp > 0) + (dp > 16)
            w, d = (3, wp - 1, 0)[a], (15, dp - 1, 0)[b]
            order1[(a * 3 + b) * 128 + w * 16 + d, wp * 18 + dp] = 1
    four = np.zeros((128, 512))
    for q in range(512):
        four[q // 4, q] = 1
    put1 = np.zeros((32, 256))
    for ch in range(4):
        put1[ch * 2 + 1, 0] = put1[16 + ch * 2, 255] = 1
    shift2 = np.zeros((128, 384))
    swapped = np.zeros((128, 384))
    for l in range(128):
        for k in range(3):
            s = l % 64 + k - 1
            if 0 <= s < 64:
                s += l - l % 64
                shift2[s, k * 128 + l] = 1
                swapped[(s + 64) % 128, k * 128 + l] = 1
    ends = (0, 63, 64, 127)
    pick2 = np.zeros((16, 512))
    for dq in range(4):
        for n, l in enumerate(ends):
            pick2[dq * 4 + n, dq * 128 + l] = 1
    put2 = np.zeros((96, 2048))
    for dq in range(-2, 6):
        for half in range(2):
            d = dq + 4 * half
            dz = (d >= 0) + (d > 7)
            there, row = (d % 8) // 4, (d % 4) * 4
            put2[dz * 16 + row + 2 * there + 1, (dq + 2) * 256 + 64 * half] = 1
            put2[48 + dz * 16 + row + 2 * there, (dq + 2) * 256 + 128 + 64 * half + 63] = 1
    pick3 = np.zeros((32, 768))
    put3 = np.zeros((64, 1536))
    for dq in range(6):
        for n, l in enumerate(ends):
            pick3[dq * 4 + n, dq * 128 + l] = 1
        for half in range(2):
            put3[dq * 4 + 2 * half + 1, dq * 256 + 64 * half] = 1
            put3[32 + dq * 4 + 2 * half, dq * 256 + 128 + 64 * half + 63] = 1
    even = np.zeros((256, 128))
    for half in range(2):
        for h in range(64):
            even[half * 128 + 2 * h, half * 64 + h] = 1
    twice = np.zeros((128, 256))
    for half in range(2):
        for h in range(128):
            twice[half * 64 + h // 2, half * 128 + h] = 1
    spread = np.zeros((192, 512))
    for dc in range(-1, 5):
        for hc in range(32):
            row = (128 if dc < 0 else 160 if dc > 3 else dc * 32) + hc
            for t in range(2):
                for half in range(2):
                    kind = {0: 0, 1: 1, -1: 2, 2: 3}.get(dc - 2 * half)
                    if kind is not None:
                        spread[row, kind * 128 + half * 64 + 2 * hc + t] = 1
    collect = np.zeros((256, 128))
    for dc in range(4):
        for hc in range(32):
            collect[(dc % 2) * 128 + dc * 32 + hc, (dc // 2) * 64 + 2 * hc] = 1
    widen = np.zeros((108, 1536))
    narrow = np.zeros((144, 128))
    for q in range(108):
        for w in range(4):
            widen[q, w * 384 + w * 48 + (q // 12) * 16 + q % 12] = 1
        narrow[(q // 12) * 16 + q % 12, q] = 1
    narrow[12, 108] = 1
    ident = np.zeros((64, 256))
    for o in range(64):
        ident[o, o] = ident[o, 128 + 64 + o] = 1
    every = dict(
        place=place, shift1=shift1, order1=order1, four=four, put1=put1, shift2=shift2, swapped=swapped,
        pick2=pick2, put2=put2, pick3=pick3, put3=put3, even=even, twice=twice, spread=spread, collect=collect,
        widen=widen, narrow=narrow, ident=ident,
    )
    return every


TABLE = {}


def packed_table():
    parts, row = [], 0
    for name, value in tables().items():
        rows, lanes = value.shape
        if name == "order1":
            value = np.concatenate(np.split(value, 4), axis=1)
            rows //= 4
        wide = np.zeros((-(-rows // 16) * 16, -(-lanes // 512) * 512))
        wide[:rows, :value.shape[1]] = value
        wide = np.concatenate(np.split(wide, wide.shape[1] // 512, axis=1))
        TABLE[name] = (row, rows, lanes)
        row += wide.shape[0]
        parts.append(wide)
    return np.concatenate(parts).astype(jnp.bfloat16)


PACKED = packed_table()


class Rows:
    def __init__(self, ref, name):
        self.ref = ref
        self.row, self.rows, self.lanes = TABLE[name]

    def folded(self):
        return jnp.concatenate(
            [self.ref[self.row:self.row + self.rows, 128 * n:128 * n + 128] for n in range(4)], axis=0
        )

    def __getitem__(self, key):
        if self.lanes > 512:
            step = -(-self.rows // 16) * 16
            return jnp.concatenate(
                [self.ref[self.row + n * step:self.row + n * step + self.rows, :] for n in range(-(-self.lanes // 512))],
                axis=1,
            )
        if key is Ellipsis:
            return self.ref[self.row:self.row + self.rows, :self.lanes]
        return self.ref[self.row + key.start:self.row + key.stop, :self.lanes]


def row_to_column(row):
    n = row.shape[1]
    diagonal = lax.broadcasted_iota(jnp.int32, (n, n), 0) == lax.broadcasted_iota(jnp.int32, (n, n), 1)
    return jnp.sum(jnp.where(diagonal, jnp.broadcast_to(row, (n, n)), 0.0), axis=1, keepdims=True)


def column_to_row(column):
    n = column.shape[0]
    diagonal = lax.broadcasted_iota(jnp.int32, (n, n), 0) == lax.broadcasted_iota(jnp.int32, (n, n), 1)
    return jnp.sum(jnp.where(diagonal, jnp.broadcast_to(column, (n, n)), 0.0), axis=0, keepdims=True)


def kept(flag, value):
    return lax.select(flag, value, jnp.zeros_like(value))


def leaky(a):
    return jnp.where(a > 0, a, slope_below * a)


def slope(a):
    return jnp.where(a > 0, 1.0, slope_below)


def split3(a):
    high = a.astype(bf16)
    rest = a - high.astype(f32)
    mid = rest.astype(bf16)
    return high, mid, (rest - mid.astype(f32)).astype(bf16)


def kernel(sizes, *refs):
    GX, GY, GZ, NX = sizes
    ZL = GZ // NX
    ZH = GX // 2
    NZ = ZH * ZL
    far = refs[:7]
    refs = refs[7:]
    feat_out, one_out, total_out = refs[:3]
    (
        edges, wide_in, deep_in, corner_in, col1, col1_in, xs, pre1,
        wide_t, deep_t, corner_t, pooled, packs, wide2, deep2, corner2, v2, col2, col2_in, ys,
        errs, col3, col3_in, fs, turned, perr,
        grads, core_in, red1, plane_in, z_in, total,
        one, one_core, one_plane, one_z, one_half, send_sems, recv_sems, vol, filt1, bias1, filt2, bias2, cot, packed, in_sems,
        feat, base1, base2, out_sems,
    ) = refs[3:]
    near = (vol, filt1, bias1, filt2, bias2, cot, packed)
    fetches = [pltpu.make_async_copy(a, b, in_sems.at[n]) for n, (a, b) in enumerate(zip(far, near))]
    for fetch in fetches:
        fetch.start()
    t = {name: Rows(packed, name) for name in TABLE}

    gx, gy, gz = lax.axis_index("gx"), lax.axis_index("gy"), lax.axis_index("gz")
    core, zh = lax.rem(gx, 2), lax.div(gx, 2)
    xc, zl = lax.rem(gz, NX), lax.div(gz, NX)
    zc = zh * ZL + zl

    def shifted(dx, dy, dz):
        return (lax.rem(gx + (dx + GX), GX), lax.rem(gy + (dy + GY), GY), lax.rem(gz + (dz + GZ), GZ))

    sibling = (gx + 1 - 2 * core, gy, gz)

    plane = xc * GY + gy
    NP = NX * GY

    def ring_gap(n, r):
        return min(r, n - r)

    plane_steps = [(rx, ry) for rx in range(NX) for ry in range(GY) if rx or ry]
    plane_steps.sort(key=lambda step: -ring_gap(NX, step[0]) - ring_gap(GY, step[1]))
    z_steps = sorted(range(1, NZ), key=lambda r: -ring_gap(NZ, r))

    def plane_peer(step):
        px, py = lax.rem(xc + step[0], NX), lax.rem(gy + step[1], GY)
        return px * GY + py, (gx, py, zl * NX + px)

    def z_peer(r):
        p = lax.rem(zc + r, NZ)
        return (2 * lax.div(p, ZL) + core, gy, lax.rem(p, ZL) * NX + xc)

    square = [(dx, dz) for dx in (-1, 1, 0) for dz in (-1, 1, 0)]
    square.sort(key=lambda step: -abs(step[0]) - abs(step[1]))
    peers = [shifted(dx, dy, dz) for dx, dz in square for dy in (-1, 1)]
    peers += [shifted(dx, 0, dz) for dx, dz in square if (dx, dz) != (0, 0)]
    peers += [plane_peer(step)[1] for step in plane_steps]
    peers += [z_peer(r) for r in z_steps]
    barrier = pltpu.get_barrier_semaphore()
    for peer in peers:
        pl.semaphore_signal(barrier, inc=1, device_id=peer, device_id_type=MESH)

    count = [0]
    started = []

    def send(src, dst, device):
        n = count[0]
        count[0] += 1
        copy = pltpu.make_async_remote_copy(
            src_ref=src, dst_ref=dst, send_sem=send_sems.at[n], recv_sem=recv_sems.at[n],
            device_id=device, device_id_type=MESH,
        )
        copy.start()
        started.append(copy)
        return copy

    def drain(keep):
        while len(started) > keep:
            started.pop(0).wait_send()

    outs = []

    def put_out(src, dst):
        copy = pltpu.make_async_copy(src, dst, out_sems.at[len(outs)])
        copy.start()
        outs.append(copy)

    def arrive(copies):
        for copy in copies:
            copy.wait_recv()

    row = lax.broadcasted_iota(jnp.int32, (32, 256), 0)
    column = lax.broadcasted_iota(jnp.int32, (32, 256), 1)
    wanted = jnp.where(row < 16, row * 16, row * 16 - 241)
    edge = jnp.where(column == wanted, 1.0, 0.0).astype(bf16)
    fetches[0].wait()
    block = vol[...].reshape(256, 128)
    edges[...] = mm(edge, block).astype(bf16)
    pl.semaphore_wait(barrier, len(peers))

    has_left, has_right = gx > 0, gx < GX - 1
    has_front, has_back = gz > 0, gz < GZ - 1
    has_below, has_above = gy > 0, gy < GY - 1

    def send_ring(wide_src, wide_dst, deep_src, deep_dst, corner_src, corner_dst):
        copies = []
        for a in range(2):
            dx = 1 if a == 0 else -1
            copies.append(send(wide_src(a), wide_dst.at[a], shifted(dx, 0, 0)))
        for b in range(2):
            dz = 1 if b == 0 else -1
            copies.append(send(deep_src(b), deep_dst.at[b], shifted(0, 0, dz)))
        for a in range(2):
            for b in range(2):
                copies.append(
                    send(corner_src(a, b), corner_dst.at[a * 2 + b], shifted(1 if a == 0 else -1, 0, 1 if b == 0 else -1))
                )
        return copies

    def send_columns(src, dst):
        copies = []
        for dx, dz in square:
            for side in range(2):
                dy = 1 if side == 0 else -1
                copies.append(send(src, dst.at[side, 1 - dx, 1 - dz], shifted(dx, dy, dz)))
        return copies

    def columns_in(dst, dx):
        rows = []
        for side in range(2):
            for dz in (-1, 0, 1):
                flag = (has_below, has_above)[side]
                if dx:
                    flag = jnp.logical_and(flag, edge_flags[(dx + 1) // 2])
                if dz:
                    flag = jnp.logical_and(flag, deep_flags[(dz + 1) // 2])
                rows.append(kept(flag, dst[side, dx + 1, dz + 1]))
        return rows

    edge_flags = (has_left, has_right)
    deep_flags = (has_front, has_back)

    def edge_rows(b):
        return edges.at[pl.ds(16, 16)] if b == 0 else edges.at[pl.ds(0, 16)]

    copies = send_ring(
        lambda a: vol.at[:, 3] if a == 0 else vol.at[:, 0], wide_in,
        edge_rows, deep_in, lambda a, b: edge_rows(b), corner_in,
    )

    row = lax.broadcasted_iota(jnp.int32, (16, 512), 0)
    column = lax.broadcasted_iota(jnp.int32, (16, 512), 1)
    wanted = jnp.where(row < 8, lax.div(row, 2) * 128 + lax.rem(row, 2) * 127, -1)
    pick1 = jnp.where(column == wanted, 1.0, 0.0).astype(bf16)
    ends = sum(
        mm(pick1[:, 128 * ch:128 * ch + 128], vol[ch].reshape(64, 128), NT) for ch in range(4)
    )
    col1[...] = jnp.concatenate([ends, jnp.zeros((16, 64), f32)], axis=1).astype(bf16)
    copies_c = send_columns(col1, col1_in)
    for fetch in fetches[1:]:
        fetch.wait()
    first_half = filt1[...].astype(bf16)
    base1[...] = jnp.concatenate([filt1[...], row_to_column(bias1[...]), jnp.zeros((32, 19), f32)], axis=1)
    for l in range(6):
        base2[64 * l:64 * l + 64] = filt2[:, 128 * l:128 * l + 128]
    base2[384:448] = jnp.concatenate(
        [filt2[:, 768:864], jnp.broadcast_to(row_to_column(bias2[...]), (64, 32))], axis=1
    )
    base2[448:512] = jnp.zeros((64, 128), f32)
    wide_first = mm(first_half, t["widen"][...]).astype(bf16)
    wide_first = jnp.concatenate([wide_first[:, 384 * w:384 * w + 288] for w in range(4)], axis=0)
    bias1_col = row_to_column(bias1[...])
    bias1_col = jnp.concatenate([bias1_col] * 4, axis=0)
    bias2_col = row_to_column(bias2[...])
    second_half = filt2[...].astype(bf16)

    copies_t = send_ring(
        lambda a: cot, wide_t, lambda b: cot.at[96:128] if b == 0 else cot.at[0:32], deep_t,
        lambda a, b: cot.at[96:128] if b == 0 else cot.at[0:32], corner_t,
    )

    turn = mm(second_half, t["ident"][...], TN).astype(bf16)
    for w in range(2):
        for m in range(18):
            pair = []
            for high in range(2):
                wp, rest = divmod(2 * m + high, 9)
                i = w + 2 - wp
                if 0 <= i <= 2:
                    tap = 9 * i + rest
                    pair.append(turn[32 * tap:32 * tap + 32, 128 * high:128 * high + 128].astype(f32))
            value = sum(pair) if pair else jnp.zeros((32, 128), f32)
            turned[32 * w:32 * w + 32, 128 * m:128 * m + 128] = value.astype(bf16)

    arrive(copies)
    pieces = [block]
    for a in range(2):
        pieces.append(kept(edge_flags[a], wide_in[a]).reshape(64, 128))
    for b in range(2):
        pieces.append(kept(deep_flags[b], deep_in[b]))
    for a in range(2):
        for b in range(2):
            pieces.append(kept(jnp.logical_and(edge_flags[a], deep_flags[b]), corner_in[a * 2 + b]))
    rows = mm(t["place"][...], jnp.concatenate(pieces, axis=0)).astype(bf16)
    inner = mm(rows, t["shift1"][...])
    arrive(copies_c)
    columns = [columns_in(col1_in, dx) for dx in (-1, 0, 1)]
    sides = [
        jnp.concatenate([columns[a][side * 3 + b] for a in range(3) for b in range(3)], axis=1)
        for side in range(2)
    ]
    ordered = mm(jnp.concatenate(sides, axis=0), t["order1"].folded()).astype(bf16)
    ordered = mm(ordered, t["four"][...])
    row = lax.broadcasted_iota(jnp.int32, (32, 512), 0)
    column = lax.broadcasted_iota(jnp.int32, (32, 512), 1)
    same = lax.rem(lax.div(row, 2), 8) == lax.rem(column, 4)
    ordered = jnp.where(same, ordered, 0.0).astype(bf16)
    ends = mm(ordered, t["put1"][...], TN)
    full = [inner[:, :128] + ends[:, :128], inner[:, 128:256], inner[:, 256:] + ends[:, 128:]]
    third = [piece.reshape(64, 8, 128) for piece in full]
    rolled = [pltpu.roll(piece, 4, axis=1) for piece in third]
    sub = lax.broadcasted_iota(jnp.int32, (64, 8, 128), 1)
    upper = sub < 4
    ones = jnp.where(sub == 4, 1.0, 0.0)
    even_tile = jnp.concatenate(
        [jnp.where(upper, third[0], rolled[1]), jnp.where(upper, third[2], ones)], axis=1
    )
    odd_tile = jnp.concatenate(
        [jnp.where(upper, rolled[0], third[1]), jnp.where(upper, rolled[2], ones)], axis=1
    )
    xs[:, 0] = even_tile.astype(bf16)
    xs[:, 1] = odd_tile.astype(bf16)

    def cols1(half_d):
        sides = []
        for e in range(2):
            tiles = [xs[wp * 9 + half_d + (j + e) // 2, (j + e) % 2] for wp in range(6) for j in range(3)]
            sides.append(jnp.concatenate(tiles, axis=0))
        return jnp.concatenate(sides, axis=1)

    def turned_half(a):
        return pltpu.roll(a.astype(f32), 64, axis=1)

    low = lax.broadcasted_iota(jnp.int32, (32, 128), 1) < 64

    def halves(a, b):
        return jnp.where(low, a.astype(f32), b.astype(f32)).astype(bf16)

    copies = []
    for dq in range(4):
        sums = [[None, None], [None, None]]
        for half in range(2):
            pd = dq + 4 * half
            pre = mm(wide_first, cols1(pd)) + bias1_col
            pre1[pd] = pre
            act = leaky(pre)
            act = act[:, :128] + act[:, 128:]
            for pw in range(2):
                both = act[64 * pw:64 * pw + 32] + act[64 * pw + 32:64 * pw + 64]
                sums[pw][half] = ((both + pltpu.roll(both, 127, axis=1)) * 0.125).astype(bf16)
        lanes = [jnp.concatenate([sums[0][half], sums[1][half]], axis=0) for half in range(2)]
        value = (mm(lanes[0], t["even"][0:128]) + mm(lanes[1], t["even"][128:256])).astype(bf16)
        pooled[:, dq] = value.reshape(2, 32, 128)
        for a in range(2):
            copies.append(send(pooled.at[:, dq], wide2.at[a, :, dq], shifted(1 - 2 * a, 0, 0)))
        if dq % 2:
            b = 0 if dq == 3 else 1
            for w in range(2):
                if b == 0:
                    packs[0, w] = halves(turned_half(pooled[w, 2]), pooled[w, 3])
                else:
                    packs[1, w] = halves(pooled[w, 0], turned_half(pooled[w, 1]))
            copies.append(send(packs.at[b], deep2.at[b], shifted(0, 0, 1 - 2 * b)))
            for a in range(2):
                copies.append(send(packs.at[b], corner2.at[a * 2 + b], shifted(1 - 2 * a, 0, 1 - 2 * b)))
    pick = t["pick2"][...]
    ends = sum(
        mm(pick[:, 128 * dq:128 * dq + 128], pooled[:, dq].reshape(64, 128), NT) for dq in range(4)
    )
    col2[...] = jnp.concatenate([ends, jnp.zeros((16, 64), f32)], axis=1).astype(bf16)
    copies_c = send_columns(col2, col2_in)

    arrive(copies_t)
    spread_cot = []
    for dx in (-1, 0, 1):
        a = max(dx, 0)
        beside = edge_flags[a]
        if dx:
            rows = [kept(beside, wide_t[a])]
            rows += [kept(jnp.logical_and(beside, deep_flags[b]), corner_t[a * 2 + b]) for b in range(2)]
        else:
            rows = [cot[...]] + [kept(deep_flags[b], deep_t[b]) for b in range(2)]
        spread_cot.append(mm(jnp.concatenate(rows, axis=0), t["spread"][...], TN) * 0.125)

    arrive(copies)
    for wp in range(6):
        a, w = wp // 4, wp % 2
        if wp in (2, 3):
            near = [pooled[w, dq] for dq in range(4)]
            front, back = (kept(deep_flags[b], deep2[b, w]) for b in range(2))
        else:
            near = [kept(edge_flags[a], wide2[a, w, dq]) for dq in range(4)]
            front, back = (
                kept(jnp.logical_and(edge_flags[a], deep_flags[b]), corner2[a * 2 + b, w]) for b in range(2)
            )
        for dq in range(4):
            v2[wp * 6 + dq] = near[dq]
        v2[wp * 6 + 4] = halves(front, turned_half(near[2]))
        v2[wp * 6 + 5] = halves(turned_half(near[1]), back)
        v2[36 + wp] = halves(near[3], front)
        v2[42 + wp] = halves(back, near[0])
    inner = jnp.concatenate(
        [mm(v2[0:36].reshape(1152, 128), t["shift2"][...]), mm(v2[36:48].reshape(384, 128), t["swapped"][...])],
        axis=0,
    )
    arrive(copies_c)
    put = t["put2"][...]
    edge = [mm(jnp.concatenate(columns_in(col2_in, dx), axis=0), put, TN) for dx in (-1, 0, 1)]
    for wp in range(6):
        for dp in range(8):
            number = {0: wp * 6 + 4, 1: 36 + wp, 6: 42 + wp, 7: wp * 6 + 5}.get(dp, wp * 6 + dp - 2)
            for k in range(3):
                piece = inner[number * 32:number * 32 + 32, 128 * k:128 * k + 128]
                if k != 1:
                    lane = dp * 256 + 64 * k
                    piece = piece + edge[wp // 2][(wp % 2) * 32:(wp % 2) * 32 + 32, lane:lane + 128]
                ys[wp * 8 + dp, k * 32:k * 32 + 32, :] = piece.astype(bf16)

    def cols2(w, dq, extra):
        taps = [ys[(w + i) * 8 + dq + j] for i in range(3) for j in range(3)]
        return jnp.concatenate(taps + extra, axis=0)

    feat_sum = [None, None]

    def errors(dqs, pairs):
        for dq in dqs:
            kind = {0: 2, 5: 3}.get(dq, (dq - 1) // 2)
            for pair in pairs:
                errors_of(dq, kind, pair)

    def errors_of(dq, kind, pair):
        cols = jnp.concatenate([cols2(w, dq, []) for w in pair], axis=1)
        pre = mm(second_half, cols) + bias2_col
        if pair == (1, 2) and 0 < dq < 5:
            act = leaky(pre)
            act = act[:, :128] + act[:, 128:]
            feat_sum[kind] = act if feat_sum[kind] is None else feat_sum[kind] + act
        for n, w in enumerate(pair):
            here = spread_cot[(w + 1) // 2][:, 128 * kind:128 * kind + 128]
            errs[w, dq] = (here * slope(pre[:, 128 * n:128 * n + 128])).astype(bf16)

    def second_half_grads():
        ends = [
            ((both + pltpu.roll(both, 127, axis=1)) * 0.125).astype(bf16) for both in feat_sum
        ]
        feat[...] = (mm(t["collect"][0:128], ends[0], NT) + mm(t["collect"][128:256], ends[1], NT)).astype(bf16)
        ones_rows = [jnp.ones((32, 128), bf16)]
        grad2 = None
        for dq in range(4):
            cols = jnp.concatenate([cols2(w, dq + 1, ones_rows) for w in (1, 2)], axis=1)
            err = jnp.concatenate([errs[w, dq + 1] for w in (1, 2)], axis=1)
            piece = mm(err, cols, NT)
            grad2 = piece if grad2 is None else grad2 + piece
        for l in range(7):
            grads[l * 64:l * 64 + 64] = grad2[:, 128 * l:128 * l + 128]
        grads[448:512] = jnp.zeros((64, 128), f32)
        put_out(feat, feat_out)
        return send(part(grads, 1 - core, n1), core_in, sibling)

    def part(ref, index, size):
        return ref.at[pl.ds(pl.multiple_of(index * size, size), size)]

    n1, n3 = 256, 256 // NP

    def sum_core(copy):
        copy.wait_recv()
        red1[...] = part(grads, core, n1)[...] + core_in[...]
        copies = []
        for n, step in enumerate(plane_steps):
            p, device = plane_peer(step)
            copies.append(send(part(red1, p, n3), plane_in.at[n], device))
        return copies

    def sum_plane(copies):
        arrive(copies)
        acc = part(red1, plane, n3)[...]
        for r in range(1, NP):
            acc = acc + plane_in[r - 1]
        z_in[zc] = acc
        return [send(z_in.at[zc], z_in.at[zc], z_peer(r)) for r in z_steps]

    def sum_z(copies):
        arrive(copies)
        acc = z_in[0]
        for r in range(1, NZ):
            acc = acc + z_in[r]
        mine = part(total, core * NP + plane, n3)
        mine[...] = part(base2, core * NP + plane, n3)[...] - learn_rate * acc
        return [send(mine, mine, plane_peer(step)[1]) for step in plane_steps]

    def gather_core(copies):
        arrive(copies)
        mine, far = part(total, core, n1), part(total_out, core, n1)
        copy = send(mine, far, sibling)
        put_out(mine, far)
        return copy

    def everyone(value, slots, index, devices):
        slots[index] = value
        return [send(slots.at[index], slots.at[index], device) for device in devices]

    def summed_slots(copies, slots):
        arrive(copies)
        acc = slots[0]
        for n in range(1, slots.shape[0]):
            acc = acc + slots[n]
        return acc

    errors(range(0, 6), [(1, 2), (0, 3)])
    pick = t["pick3"][...]
    col3[...] = sum(
        mm(pick[:, 128 * dq:128 * dq + 128], errs[:, dq].reshape(256, 128), NT) for dq in range(6)
    ).astype(bf16)
    copies = [send(col3, col3_in.at[0], shifted(0, 1, 0)), send(col3, col3_in.at[1], shifted(0, -1, 0))]

    copies2 = sum_core(second_half_grads())
    inner = mm(errs[...].reshape(1536, 128), t["shift2"][...])
    arrive(copies)
    rows = [kept(has_below, col3_in[0]), kept(has_above, col3_in[1])]
    edge = mm(jnp.concatenate(rows, axis=0), t["put3"][...], TN)
    for wp in range(4):
        for dp in range(6):
            number = wp * 6 + dp
            for k in range(3):
                piece = inner[number * 64:number * 64 + 64, 128 * k:128 * k + 128]
                if k != 1:
                    lane = dp * 256 + 64 * k
                    piece = piece + edge[wp * 64:wp * 64 + 64, lane:lane + 128]
                fs[number, (2 - k) * 64:(2 - k) * 64 + 64, :] = piece.astype(bf16)

    def cols3(dq):
        return jnp.concatenate([fs[wp * 6 + dq + 2 - j] for wp in range(4) for j in range(3)], axis=0)

    for dq in (0, 2):
        pe = mm(turned[...], jnp.concatenate([cols3(dq), cols3(dq + 1)], axis=1)).astype(bf16)
        both = mm(jnp.concatenate([pe[:, :128], pe[:, 128:]], axis=0), t["twice"][...]) * 0.125
        for n in range(2):
            for w in range(2):
                rows = both[64 * n + 32 * w:64 * n + 32 * w + 32]
                perr[w, dq + n] = rows[:, :128]
                perr[w, dq + n + 4] = rows[:, 128:]

    grad1 = None
    for pd in range(8):
        here = jnp.concatenate([perr[w // 2, pd] for w in range(4)], axis=0)
        err = (jnp.concatenate([here, here], axis=1) * slope(pre1[pd])).astype(bf16)
        piece = mm(err, cols1(pd), NT)
        grad1 = piece if grad1 is None else grad1 + piece
    grad1 = sum(grad1[32 * w:32 * w + 32, 48 * w:48 * w + 144] for w in range(4))
    one[...] = sum(mm(piece, t["narrow"][...]) for piece in split3(grad1))
    copies1 = send(part(one, 1 - core, 16), one_core, sibling)
    copies2 = sum_plane(copies2)
    drain(NP + NZ)
    copies1.wait_recv()
    copies1 = everyone(
        part(one, core, 16)[...] + one_core[...], one_plane, plane, [plane_peer(step)[1] for step in plane_steps]
    )
    drain(NP)
    copies2 = sum_z(copies2)
    copies1 = everyone(summed_slots(copies1, one_plane), one_z, zc, [z_peer(r) for r in z_steps])
    copy2 = gather_core(copies2)
    drain(1)
    one_half[...] = part(base1, core, 16)[...] - learn_rate * summed_slots(copies1, one_z)
    far = part(one_out, core, 16)
    copy1 = send(one_half, far, sibling)
    put_out(one_half, far)
    copy2.wait_recv()
    copy1.wait_recv()

    drain(0)
    for out in outs:
        out.wait()


def hand_on(*refs):
    ins, outs, spots, results, in_sems, out_sems = refs[:3], refs[3:8], refs[8:11], refs[11:15], refs[15], refs[16]
    reads = [pltpu.make_async_copy(ins[n], spots[n], in_sems.at[n]) for n in range(3)]
    feat, one, total = spots
    step1, off1, step2, off2 = results
    writes = [pltpu.make_async_copy(a, b, out_sems.at[n]) for n, (a, b) in enumerate(zip((feat,) + results, outs))]
    for n in (2, 1, 0):
        reads[n].start()
    reads[2].wait()
    for l in range(6):
        step2[:, 128 * l:128 * l + 128] = total[64 * l:64 * l + 64]
    step2[:, 768:864] = total[384:448, 0:96]
    writes[3].start()
    reads[1].wait()
    step1[...] = one[:, 0:108]
    writes[1].start()
    reads[0].wait()
    writes[0].start()
    off1[...] = column_to_row(one[:, 108:109])
    off2[...] = column_to_row(total[384:448, 96:97])
    writes[2].start()
    writes[4].start()
    for copy in writes:
        copy.wait()


def shards(volume, first_filters, first_bias, second_filters, second_bias, cotangent):
    GX, GY, GZ = lax.axis_size("gx"), lax.axis_size("gy"), lax.axis_size("gz")
    NX = 4 if GZ >= 8 else 2
    NZ = (GX // 2) * (GZ // NX)
    NP = NX * GY
    n3 = 256 // NP
    operands = [
        volume, first_filters, first_bias.reshape(1, 32), second_filters, second_bias.reshape(1, 64),
        cotangent.transpose(1, 2, 3, 0).reshape(128, 64), jnp.asarray(PACKED),
    ]
    sems = 68 + 4 + 3 * (NP - 1) + 2 * (NZ - 1)
    V = pltpu.VMEM
    results = (
        jax.ShapeDtypeStruct((128, 64), bf16),
        jax.ShapeDtypeStruct((32, 108), f32),
        jax.ShapeDtypeStruct((1, 32), f32),
        jax.ShapeDtypeStruct((64, 864), f32),
        jax.ShapeDtypeStruct((1, 64), f32),
    )
    sums = (
        results[0],
        jax.ShapeDtypeStruct((32, 128), f32),
        jax.ShapeDtypeStruct((512, 128), f32),
    )
    out = pl.pallas_call(
        functools.partial(kernel, (GX, GY, GZ, NX)),
        out_shape=sums,
        in_specs=[pl.BlockSpec(memory_space=pltpu.HBM)] * len(operands),
        out_specs=[pl.BlockSpec(memory_space=pltpu.HBM)] * 3,
        scratch_shapes=[
            V((32, 128), bf16), V((2, 4, 16, 128), bf16), V((2, 16, 128), bf16), V((4, 16, 128), bf16),
            V((16, 128), bf16), V((2, 3, 3, 16, 128), bf16), V((64, 2, 16, 128), bf16), V((8, 128, 256), f32),
            V((2, 128, 64), bf16), V((2, 32, 64), bf16), V((4, 32, 64), bf16),
            V((2, 4, 32, 128), bf16), V((2, 2, 32, 128), bf16), V((2, 2, 4, 32, 128), bf16),
            V((2, 2, 32, 128), bf16), V((4, 2, 32, 128), bf16), V((48, 32, 128), bf16),
            V((16, 128), bf16), V((2, 3, 3, 16, 128), bf16), V((48, 96, 128), bf16),
            V((4, 6, 64, 128), bf16), V((32, 256), bf16), V((2, 32, 256), bf16), V((24, 192, 128), bf16),
            V((64, 2304), bf16), V((2, 8, 32, 128), f32),
            V((512, 128), f32), V((256, 128), f32), V((256, 128), f32), V((NP - 1, n3, 128), f32),
            V((NZ, n3, 128), f32),
            V((512, 128), f32),
            V((32, 128), f32), V((16, 128), f32), V((NP, 16, 128), f32),
            V((NZ, 16, 128), f32), V((16, 128), f32),
            pltpu.SemaphoreType.DMA((sems,)), pltpu.SemaphoreType.DMA((sems,)),
        ] + [V(a.shape, a.dtype) for a in operands] + [
            pltpu.SemaphoreType.DMA((len(operands),)),
            V((128, 64), bf16), V((32, 128), f32), V((512, 128), f32), pltpu.SemaphoreType.DMA((3,)),
        ],
        compiler_params=pltpu.CompilerParams(
            collective_id=0, has_side_effects=True, vmem_limit_bytes=62 * 2**20
        ),
    )(*operands)
    out = pl.pallas_call(
        hand_on,
        out_shape=results,
        in_specs=[pl.BlockSpec(memory_space=pltpu.HBM)] * 3,
        out_specs=[pl.BlockSpec(memory_space=pltpu.HBM)] * 5,
        scratch_shapes=[V(a.shape, a.dtype) for a in sums + results[1:]]
        + [pltpu.SemaphoreType.DMA((3,)), pltpu.SemaphoreType.DMA((5,))],
        compiler_params=pltpu.CompilerParams(vmem_limit_bytes=62 * 2**20),
    )(*out)
    features, stepped_first, offset_first, stepped_second, offset_second = out
    return (
        features.reshape(1, 4, 32, 64).transpose(3, 0, 1, 2), stepped_first, offset_first.reshape(32), stepped_second,
        offset_second.reshape(64),
    )


def solution(mesh):
    return jax.shard_map(
        shards,
        mesh=mesh,
        in_specs=(P(None, "gx", "gz", "gy"), P(), P(), P(), P(), P(None, "gx", "gz", "gy")),
        out_specs=(P(None, "gx", "gz", "gy"), P(), P(), P(), P()),
        check_vma=False,
    )
```

```python
import functools

import jax
import jax.numpy as jnp
import numpy as np
from jax import lax
from jax.experimental import pallas as pl
from jax.experimental.pallas import tpu as pltpu
from jax.sharding import PartitionSpec as P

slope_below = 0.3
learn_rate = 0.001
f32 = jnp.float32
bf16 = jnp.bfloat16
MESH = pl.DeviceIdType.MESH
NN = (((1,), (0,)), ((), ()))
NT = (((1,), (1,)), ((), ()))
TN = (((0,), (0,)), ((), ()))


def mm(a, b, dims=NN):
    return lax.dot_general(a, b, dims, preferred_element_type=f32)


def tables():
    place = np.zeros((512, 480))
    for wp in range(6):
        for dp in range(18):
            for ch in range(4):
                w, d = wp - 1, dp - 1
                inner_w, inner_d = 0 <= w < 4, 0 <= d < 16
                if inner_w and inner_d:
                    src = (ch * 4 + w) * 16 + d
                elif inner_d:
                    src = 256 + (64 if w > 0 else 0) + ch * 16 + d
                elif inner_w:
                    src = 384 + (16 if d > 0 else 0) + ch * 4 + w
                else:
                    a, b = int(w > 0), int(d > 0)
                    src = 416 + (a * 2 + b) * 16 + ch * 4 + (0 if a else 3)
                place[(wp * 18 + dp) * 4 + ch, src] = 1
    shift1 = np.zeros((128, 384))
    for l in range(128):
        if l:
            shift1[l - 1, l] = 1
        shift1[l, 128 + l] = 1
        if l < 127:
            shift1[l + 1, 256 + l] = 1
    order1 = np.zeros((1152, 128))
    for wp in range(6):
        for dp in range(18):
            a, b = (wp > 0) + (wp > 4), (dp > 0) + (dp > 16)
            w, d = (3, wp - 1, 0)[a], (15, dp - 1, 0)[b]
            order1[(a * 3 + b) * 128 + w * 16 + d, wp * 18 + dp] = 1
    four = np.zeros((128, 512))
    for q in range(512):
        four[q // 4, q] = 1
    put1 = np.zeros((32, 256))
    for ch in range(4):
        put1[ch * 2 + 1, 0] = put1[16 + ch * 2, 255] = 1
    shift2 = np.zeros((128, 384))
    swapped = np.zeros((128, 384))
    for l in range(128):
        for k in range(3):
            s = l % 64 + k - 1
            if 0 <= s < 64:
                s += l - l % 64
                shift2[s, k * 128 + l] = 1
                swapped[(s + 64) % 128, k * 128 + l] = 1
    ends = (0, 63, 64, 127)
    pick2 = np.zeros((16, 512))
    for dq in range(4):
        for n, l in enumerate(ends):
            pick2[dq * 4 + n, dq * 128 + l] = 1
    put2 = np.zeros((96, 2048))
    for dq in range(-2, 6):
        for half in range(2):
            d = dq + 4 * half
            dz = (d >= 0) + (d > 7)
            there, row = (d % 8) // 4, (d % 4) * 4
            put2[dz * 16 + row + 2 * there + 1, (dq + 2) * 256 + 64 * half] = 1
            put2[48 + dz * 16 + row + 2 * there, (dq + 2) * 256 + 128 + 64 * half + 63] = 1
    pick3 = np.zeros((32, 768))
    put3 = np.zeros((64, 1536))
    for dq in range(6):
        for n, l in enumerate(ends):
            pick3[dq * 4 + n, dq * 128 + l] = 1
        for half in range(2):
            put3[dq * 4 + 2 * half + 1, dq * 256 + 64 * half] = 1
            put3[32 + dq * 4 + 2 * half, dq * 256 + 128 + 64 * half + 63] = 1
    even = np.zeros((256, 128))
    for half in range(2):
        for h in range(64):
            even[half * 128 + 2 * h, half * 64 + h] = 1
    twice = np.zeros((128, 256))
    for half in range(2):
        for h in range(128):
            twice[half * 64 + h // 2, half * 128 + h] = 1
    spread = np.zeros((192, 512))
    for dc in range(-1, 5):
        for hc in range(32):
            row = (128 if dc < 0 else 160 if dc > 3 else dc * 32) + hc
            for t in range(2):
                for half in range(2):
                    kind = {0: 0, 1: 1, -1: 2, 2: 3}.get(dc - 2 * half)
                    if kind is not None:
                        spread[row, kind * 128 + half * 64 + 2 * hc + t] = 1
    collect = np.zeros((256, 128))
    for dc in range(4):
        for hc in range(32):
            collect[(dc % 2) * 128 + dc * 32 + hc, (dc // 2) * 64 + 2 * hc] = 1
    widen = np.zeros((108, 1536))
    narrow = np.zeros((144, 128))
    for q in range(108):
        for w in range(4):
            widen[q, w * 384 + w * 48 + (q // 12) * 16 + q % 12] = 1
        narrow[(q // 12) * 16 + q % 12, q] = 1
    narrow[12, 108] = 1
    ident = np.zeros((64, 256))
    for o in range(64):
        ident[o, o] = ident[o, 128 + 64 + o] = 1
    every = dict(
        place=place, shift1=shift1, order1=order1, four=four, put1=put1, shift2=shift2, swapped=swapped,
        pick2=pick2, put2=put2, pick3=pick3, put3=put3, even=even, twice=twice, spread=spread, collect=collect,
        widen=widen, narrow=narrow, ident=ident,
    )
    return every


TABLE = {}


def packed_table():
    parts, row = [], 0
    for name, value in tables().items():
        rows, lanes = value.shape
        if name == "order1":
            value = np.concatenate(np.split(value, 4), axis=1)
            rows //= 4
        wide = np.zeros((-(-rows // 16) * 16, -(-lanes // 512) * 512))
        wide[:rows, :value.shape[1]] = value
        wide = np.concatenate(np.split(wide, wide.shape[1] // 512, axis=1))
        TABLE[name] = (row, rows, lanes)
        row += wide.shape[0]
        parts.append(wide)
    return np.concatenate(parts).astype(jnp.bfloat16)


PACKED = packed_table()


class Rows:
    def __init__(self, ref, name):
        self.ref = ref
        self.row, self.rows, self.lanes = TABLE[name]

    def folded(self):
        return jnp.concatenate(
            [self.ref[self.row:self.row + self.rows, 128 * n:128 * n + 128] for n in range(4)], axis=0
        )

    def __getitem__(self, key):
        if self.lanes > 512:
            step = -(-self.rows // 16) * 16
            return jnp.concatenate(
                [self.ref[self.row + n * step:self.row + n * step + self.rows, :] for n in range(-(-self.lanes // 512))],
                axis=1,
            )
        if key is Ellipsis:
            return self.ref[self.row:self.row + self.rows, :self.lanes]
        return self.ref[self.row + key.start:self.row + key.stop, :self.lanes]


def row_to_column(row):
    n = row.shape[1]
    diagonal = lax.broadcasted_iota(jnp.int32, (n, n), 0) == lax.broadcasted_iota(jnp.int32, (n, n), 1)
    return jnp.sum(jnp.where(diagonal, jnp.broadcast_to(row, (n, n)), 0.0), axis=1, keepdims=True)


def column_to_row(column):
    n = column.shape[0]
    diagonal = lax.broadcasted_iota(jnp.int32, (n, n), 0) == lax.broadcasted_iota(jnp.int32, (n, n), 1)
    return jnp.sum(jnp.where(diagonal, jnp.broadcast_to(column, (n, n)), 0.0), axis=0, keepdims=True)


def kept(flag, value):
    return lax.select(flag, value, jnp.zeros_like(value))


def leaky(a):
    return jnp.where(a > 0, a, slope_below * a)


def slope(a):
    return jnp.where(a > 0, 1.0, slope_below)


def split3(a):
    high = a.astype(bf16)
    rest = a - high.astype(f32)
    mid = rest.astype(bf16)
    return high, mid, (rest - mid.astype(f32)).astype(bf16)


def kernel(sizes, *refs):
    GX, GY, GZ, NX = sizes
    ZL = GZ // NX
    ZH = GX // 2
    NZ = ZH * ZL
    far = refs[:7]
    refs = refs[7:]
    feat_out, one_out, total_out = refs[:3]
    (
        edges, wide_in, deep_in, corner_in, col1, col1_in, xs, pre1,
        wide_t, deep_t, corner_t, pooled, packs, wide2, deep2, corner2, v2, col2, col2_in, ys,
        errs, col3, col3_in, fs, turned, perr,
        grads, core_in, red1, plane_in, z_in, total,
        one, one_core, one_plane, one_z, one_half, send_sems, recv_sems, vol, filt1, bias1, filt2, bias2, cot, packed, in_sems,
        feat, base1, base2, out_sems,
    ) = refs[3:]
    near = (vol, filt1, bias1, filt2, bias2, cot, packed)
    fetches = [pltpu.make_async_copy(a, b, in_sems.at[n]) for n, (a, b) in enumerate(zip(far, near))]
    fetches[0].start()
    t = {name: Rows(packed, name) for name in TABLE}

    gx, gy, gz = lax.axis_index("gx"), lax.axis_index("gy"), lax.axis_index("gz")
    core, zh = lax.rem(gx, 2), lax.div(gx, 2)
    xc, zl = lax.rem(gz, NX), lax.div(gz, NX)
    zc = zh * ZL + zl

    def shifted(dx, dy, dz):
        return (lax.rem(gx + (dx + GX), GX), lax.rem(gy + (dy + GY), GY), lax.rem(gz + (dz + GZ), GZ))

    sibling = (gx + 1 - 2 * core, gy, gz)

    plane = xc * GY + gy
    NP = NX * GY

    def ring_gap(n, r):
        return min(r, n - r)

    plane_steps = [(rx, ry) for rx in range(NX) for ry in range(GY) if rx or ry]
    plane_steps.sort(key=lambda step: -ring_gap(NX, step[0]) - ring_gap(GY, step[1]))
    z_steps = sorted(range(1, NZ), key=lambda r: -ring_gap(NZ, r))

    def plane_peer(step):
        px, py = lax.rem(xc + step[0], NX), lax.rem(gy + step[1], GY)
        return px * GY + py, (gx, py, zl * NX + px)

    def z_peer(r):
        p = lax.rem(zc + r, NZ)
        return (2 * lax.div(p, ZL) + core, gy, lax.rem(p, ZL) * NX + xc)

    square = [(dx, dz) for dx in (-1, 1, 0) for dz in (-1, 1, 0)]
    square.sort(key=lambda step: -abs(step[0]) - abs(step[1]))
    peers = [shifted(dx, dy, dz) for dx, dz in square for dy in (-1, 1)]
    peers += [shifted(dx, 0, dz) for dx, dz in square if (dx, dz) != (0, 0)]
    peers += [plane_peer(step)[1] for step in plane_steps]
    peers += [z_peer(r) for r in z_steps]
    barrier = pltpu.get_barrier_semaphore()
    for peer in peers:
        pl.semaphore_signal(barrier, inc=1, device_id=peer, device_id_type=MESH)

    count = [0]
    started = []

    def send(src, dst, device):
        n = count[0]
        count[0] += 1
        copy = pltpu.make_async_remote_copy(
            src_ref=src, dst_ref=dst, send_sem=send_sems.at[n], recv_sem=recv_sems.at[n],
            device_id=device, device_id_type=MESH,
        )
        copy.start()
        started.append(copy)
        return copy

    def drain(keep):
        while len(started) > keep:
            started.pop(0).wait_send()

    outs = []

    def put_out(src, dst):
        copy = pltpu.make_async_copy(src, dst, out_sems.at[len(outs)])
        copy.start()
        outs.append(copy)

    def arrive(copies):
        for copy in copies:
            copy.wait_recv()

    row = lax.broadcasted_iota(jnp.int32, (32, 256), 0)
    column = lax.broadcasted_iota(jnp.int32, (32, 256), 1)
    wanted = jnp.where(row < 16, row * 16, row * 16 - 241)
    edge = jnp.where(column == wanted, 1.0, 0.0).astype(bf16)
    fetches[0].wait()
    for fetch in fetches[1:]:
        fetch.start()
    block = vol[...].reshape(256, 128)
    edges[...] = mm(edge, block).astype(bf16)
    pl.semaphore_wait(barrier, len(peers))

    has_left, has_right = gx > 0, gx < GX - 1
    has_front, has_back = gz > 0, gz < GZ - 1
    has_below, has_above = gy > 0, gy < GY - 1

    def send_ring(wide_src, wide_dst, deep_src, deep_dst, corner_src, corner_dst):
        copies = []
        for a in range(2):
            dx = 1 if a == 0 else -1
            copies.append(send(wide_src(a), wide_dst.at[a], shifted(dx, 0, 0)))
        for b in range(2):
            dz = 1 if b == 0 else -1
            copies.append(send(deep_src(b), deep_dst.at[b], shifted(0, 0, dz)))
        for a in range(2):
            for b in range(2):
                copies.append(
                    send(corner_src(a, b), corner_dst.at[a * 2 + b], shifted(1 if a == 0 else -1, 0, 1 if b == 0 else -1))
                )
        return copies

    def send_columns(src, dst):
        copies = []
        for dx, dz in square:
            for side in range(2):
                dy = 1 if side == 0 else -1
                copies.append(send(src, dst.at[side, 1 - dx, 1 - dz], shifted(dx, dy, dz)))
        return copies

    def columns_in(dst, dx):
        rows = []
        for side in range(2):
            for dz in (-1, 0, 1):
                flag = (has_below, has_above)[side]
                if dx:
                    flag = jnp.logical_and(flag, edge_flags[(dx + 1) // 2])
                if dz:
                    flag = jnp.logical_and(flag, deep_flags[(dz + 1) // 2])
                rows.append(kept(flag, dst[side, dx + 1, dz + 1]))
        return rows

    edge_flags = (has_left, has_right)
    deep_flags = (has_front, has_back)

    def edge_rows(b):
        return edges.at[pl.ds(16, 16)] if b == 0 else edges.at[pl.ds(0, 16)]

    copies = send_ring(
        lambda a: vol.at[:, 3] if a == 0 else vol.at[:, 0], wide_in,
        edge_rows, deep_in, lambda a, b: edge_rows(b), corner_in,
    )

    row = lax.broadcasted_iota(jnp.int32, (16, 512), 0)
    column = lax.broadcasted_iota(jnp.int32, (16, 512), 1)
    wanted = jnp.where(row < 8, lax.div(row, 2) * 128 + lax.rem(row, 2) * 127, -1)
    pick1 = jnp.where(column == wanted, 1.0, 0.0).astype(bf16)
    ends = sum(
        mm(pick1[:, 128 * ch:128 * ch + 128], vol[ch].reshape(64, 128), NT) for ch in range(4)
    )
    col1[...] = jnp.concatenate([ends, jnp.zeros((16, 64), f32)], axis=1).astype(bf16)
    copies_c = send_columns(col1, col1_in)
    for fetch in fetches[1:]:
        fetch.wait()
    first_half = filt1[...].astype(bf16)
    base1[...] = jnp.concatenate([filt1[...], row_to_column(bias1[...]), jnp.zeros((32, 19), f32)], axis=1)
    for l in range(6):
        base2[64 * l:64 * l + 64] = filt2[:, 128 * l:128 * l + 128]
    base2[384:448] = jnp.concatenate(
        [filt2[:, 768:864], jnp.broadcast_to(row_to_column(bias2[...]), (64, 32))], axis=1
    )
    base2[448:512] = jnp.zeros((64, 128), f32)
    wide_first = mm(first_half, t["widen"][...]).astype(bf16)
    wide_first = jnp.concatenate([wide_first[:, 384 * w:384 * w + 288] for w in range(4)], axis=0)
    bias1_col = row_to_column(bias1[...])
    bias1_col = jnp.concatenate([bias1_col] * 4, axis=0)
    bias2_col = row_to_column(bias2[...])
    second_half = filt2[...].astype(bf16)

    copies_t = send_ring(
        lambda a: cot, wide_t, lambda b: cot.at[96:128] if b == 0 else cot.at[0:32], deep_t,
        lambda a, b: cot.at[96:128] if b == 0 else cot.at[0:32], corner_t,
    )

    turn = mm(second_half, t["ident"][...], TN).astype(bf16)
    for w in range(2):
        for m in range(18):
            pair = []
            for high in range(2):
                wp, rest = divmod(2 * m + high, 9)
                i = w + 2 - wp
                if 0 <= i <= 2:
                    tap = 9 * i + rest
                    pair.append(turn[32 * tap:32 * tap + 32, 128 * high:128 * high + 128].astype(f32))
            value = sum(pair) if pair else jnp.zeros((32, 128), f32)
            turned[32 * w:32 * w + 32, 128 * m:128 * m + 128] = value.astype(bf16)

    arrive(copies)
    pieces = [block]
    for a in range(2):
        pieces.append(kept(edge_flags[a], wide_in[a]).reshape(64, 128))
    for b in range(2):
        pieces.append(kept(deep_flags[b], deep_in[b]))
    for a in range(2):
        for b in range(2):
            pieces.append(kept(jnp.logical_and(edge_flags[a], deep_flags[b]), corner_in[a * 2 + b]))
    rows = mm(t["place"][...], jnp.concatenate(pieces, axis=0)).astype(bf16)
    inner = mm(rows, t["shift1"][...])
    arrive(copies_c)
    columns = [columns_in(col1_in, dx) for dx in (-1, 0, 1)]
    sides = [
        jnp.concatenate([columns[a][side * 3 + b] for a in range(3) for b in range(3)], axis=1)
        for side in range(2)
    ]
    ordered = mm(jnp.concatenate(sides, axis=0), t["order1"].folded()).astype(bf16)
    ordered = mm(ordered, t["four"][...])
    row = lax.broadcasted_iota(jnp.int32, (32, 512), 0)
    column = lax.broadcasted_iota(jnp.int32, (32, 512), 1)
    same = lax.rem(lax.div(row, 2), 8) == lax.rem(column, 4)
    ordered = jnp.where(same, ordered, 0.0).astype(bf16)
    ends = mm(ordered, t["put1"][...], TN)
    full = [inner[:, :128] + ends[:, :128], inner[:, 128:256], inner[:, 256:] + ends[:, 128:]]
    third = [piece.reshape(64, 8, 128) for piece in full]
    rolled = [pltpu.roll(piece, 4, axis=1) for piece in third]
    sub = lax.broadcasted_iota(jnp.int32, (64, 8, 128), 1)
    upper = sub < 4
    ones = jnp.where(sub == 4, 1.0, 0.0)
    even_tile = jnp.concatenate(
        [jnp.where(upper, third[0], rolled[1]), jnp.where(upper, third[2], ones)], axis=1
    )
    odd_tile = jnp.concatenate(
        [jnp.where(upper, rolled[0], third[1]), jnp.where(upper, rolled[2], ones)], axis=1
    )
    xs[:, 0] = even_tile.astype(bf16)
    xs[:, 1] = odd_tile.astype(bf16)

    def cols1(half_d):
        sides = []
        for e in range(2):
            tiles = [xs[wp * 9 + half_d + (j + e) // 2, (j + e) % 2] for wp in range(6) for j in range(3)]
            sides.append(jnp.concatenate(tiles, axis=0))
        return jnp.concatenate(sides, axis=1)

    def turned_half(a):
        return pltpu.roll(a.astype(f32), 64, axis=1)

    low = lax.broadcasted_iota(jnp.int32, (32, 128), 1) < 64

    def halves(a, b):
        return jnp.where(low, a.astype(f32), b.astype(f32)).astype(bf16)

    copies = []
    for dq in range(4):
        sums = [[None, None], [None, None]]
        for half in range(2):
            pd = dq + 4 * half
            pre = mm(wide_first, cols1(pd)) + bias1_col
            pre1[pd] = pre
            act = leaky(pre)
            act = act[:, :128] + act[:, 128:]
            for pw in range(2):
                both = act[64 * pw:64 * pw + 32] + act[64 * pw + 32:64 * pw + 64]
                sums[pw][half] = ((both + pltpu.roll(both, 127, axis=1)) * 0.125).astype(bf16)
        lanes = [jnp.concatenate([sums[0][half], sums[1][half]], axis=0) for half in range(2)]
        value = (mm(lanes[0], t["even"][0:128]) + mm(lanes[1], t["even"][128:256])).astype(bf16)
        pooled[:, dq] = value.reshape(2, 32, 128)
        for a in range(2):
            copies.append(send(pooled.at[:, dq], wide2.at[a, :, dq], shifted(1 - 2 * a, 0, 0)))
        if dq % 2:
            b = 0 if dq == 3 else 1
            for w in range(2):
                if b == 0:
                    packs[0, w] = halves(turned_half(pooled[w, 2]), pooled[w, 3])
                else:
                    packs[1, w] = halves(pooled[w, 0], turned_half(pooled[w, 1]))
            copies.append(send(packs.at[b], deep2.at[b], shifted(0, 0, 1 - 2 * b)))
            for a in range(2):
                copies.append(send(packs.at[b], corner2.at[a * 2 + b], shifted(1 - 2 * a, 0, 1 - 2 * b)))
    pick = t["pick2"][...]
    ends = mm(pick, jnp.concatenate([pooled[:, dq].reshape(64, 128) for dq in range(4)], axis=1), NT)
    col2[...] = jnp.concatenate([ends, jnp.zeros((16, 64), f32)], axis=1).astype(bf16)
    copies_c = send_columns(col2, col2_in)

    arrive(copies_t)
    spread_cot = []
    for dx in (-1, 0, 1):
        a = max(dx, 0)
        beside = edge_flags[a]
        if dx:
            rows = [kept(beside, wide_t[a])]
            rows += [kept(jnp.logical_and(beside, deep_flags[b]), corner_t[a * 2 + b]) for b in range(2)]
        else:
            rows = [cot[...]] + [kept(deep_flags[b], deep_t[b]) for b in range(2)]
        spread_cot.append(mm(jnp.concatenate(rows, axis=0), t["spread"][...], TN) * 0.125)

    arrive(copies)
    for wp in range(6):
        a, w = wp // 4, wp % 2
        if wp in (2, 3):
            near = [pooled[w, dq] for dq in range(4)]
            front, back = (kept(deep_flags[b], deep2[b, w]) for b in range(2))
        else:
            near = [kept(edge_flags[a], wide2[a, w, dq]) for dq in range(4)]
            front, back = (
                kept(jnp.logical_and(edge_flags[a], deep_flags[b]), corner2[a * 2 + b, w]) for b in range(2)
            )
        for dq in range(4):
            v2[wp * 6 + dq] = near[dq]
        v2[wp * 6 + 4] = halves(front, turned_half(near[2]))
        v2[wp * 6 + 5] = halves(turned_half(near[1]), back)
        v2[36 + wp] = halves(near[3], front)
        v2[42 + wp] = halves(back, near[0])
    inner = jnp.concatenate(
        [mm(v2[0:36].reshape(1152, 128), t["shift2"][...]), mm(v2[36:48].reshape(384, 128), t["swapped"][...])],
        axis=0,
    )
    arrive(copies_c)
    put = t["put2"][...]
    edge = [mm(jnp.concatenate(columns_in(col2_in, dx), axis=0), put, TN) for dx in (-1, 0, 1)]
    for wp in range(6):
        for dp in range(8):
            number = {0: wp * 6 + 4, 1: 36 + wp, 6: 42 + wp, 7: wp * 6 + 5}.get(dp, wp * 6 + dp - 2)
            for k in range(3):
                piece = inner[number * 32:number * 32 + 32, 128 * k:128 * k + 128]
                if k != 1:
                    lane = dp * 256 + 64 * k
                    piece = piece + edge[wp // 2][(wp % 2) * 32:(wp % 2) * 32 + 32, lane:lane + 128]
                ys[wp * 8 + dp, k * 32:k * 32 + 32, :] = piece.astype(bf16)

    def cols2(w, dq, extra):
        taps = [ys[(w + i) * 8 + dq + j] for i in range(3) for j in range(3)]
        return jnp.concatenate(taps + extra, axis=0)

    feat_sum = [None, None]

    def errors(dqs, pairs):
        for dq in dqs:
            kind = {0: 2, 5: 3}.get(dq, (dq - 1) // 2)
            for pair in pairs:
                errors_of(dq, kind, pair)

    def errors_of(dq, kind, pair):
        cols = jnp.concatenate([cols2(w, dq, []) for w in pair], axis=1)
        pre = mm(second_half, cols) + bias2_col
        if pair == (1, 2) and 0 < dq < 5:
            act = leaky(pre)
            act = act[:, :128] + act[:, 128:]
            feat_sum[kind] = act if feat_sum[kind] is None else feat_sum[kind] + act
        for n, w in enumerate(pair):
            here = spread_cot[(w + 1) // 2][:, 128 * kind:128 * kind + 128]
            errs[w, dq] = (here * slope(pre[:, 128 * n:128 * n + 128])).astype(bf16)

    def second_half_grads():
        ends = [
            ((both + pltpu.roll(both, 127, axis=1)) * 0.125).astype(bf16) for both in feat_sum
        ]
        feat[...] = (mm(t["collect"][0:128], ends[0], NT) + mm(t["collect"][128:256], ends[1], NT)).astype(bf16)
        ones_rows = [jnp.ones((32, 128), bf16)]
        cols = jnp.concatenate([cols2(w, dq, ones_rows) for dq in range(1, 5) for w in (1, 2)], axis=1)
        err = jnp.concatenate([errs[w, dq] for dq in range(1, 5) for w in (1, 2)], axis=1)
        grad2 = mm(err, cols, NT)
        for l in range(7):
            grads[l * 64:l * 64 + 64] = grad2[:, 128 * l:128 * l + 128]
        grads[448:512] = jnp.zeros((64, 128), f32)
        put_out(feat, feat_out)
        return send(part(grads, 1 - core, n1), core_in, sibling)

    def part(ref, index, size):
        return ref.at[pl.ds(pl.multiple_of(index * size, size), size)]

    n1, n3 = 256, 256 // NP

    def sum_core(copy):
        copy.wait_recv()
        red1[...] = part(grads, core, n1)[...] + core_in[...]
        copies = []
        for n, step in enumerate(plane_steps):
            p, device = plane_peer(step)
            copies.append(send(part(red1, p, n3), plane_in.at[n], device))
        return copies

    def sum_plane(copies):
        arrive(copies)
        acc = part(red1, plane, n3)[...]
        for r in range(1, NP):
            acc = acc + plane_in[r - 1]
        z_in[zc] = acc
        return [send(z_in.at[zc], z_in.at[zc], z_peer(r)) for r in z_steps]

    def sum_z(copies):
        arrive(copies)
        acc = z_in[0]
        for r in range(1, NZ):
            acc = acc + z_in[r]
        mine = part(total, core * NP + plane, n3)
        mine[...] = part(base2, core * NP + plane, n3)[...] - learn_rate * acc
        return [send(mine, mine, plane_peer(step)[1]) for step in plane_steps]

    def gather_core(copies):
        arrive(copies)
        mine, far = part(total, core, n1), part(total_out, core, n1)
        copy = send(mine, far, sibling)
        put_out(mine, far)
        return copy

    def everyone(value, slots, index, devices):
        slots[index] = value
        return [send(slots.at[index], slots.at[index], device) for device in devices]

    def summed_slots(copies, slots):
        arrive(copies)
        acc = slots[0]
        for n in range(1, slots.shape[0]):
            acc = acc + slots[n]
        return acc

    errors(range(1, 5), [(1, 2)])
    copies2 = second_half_grads()
    errors((0, 5), [(1, 2), (0, 3)])
    errors(range(1, 5), [(0, 3)])
    pick = t["pick3"][...]
    every = jnp.concatenate([errs[:, dq].reshape(256, 128) for dq in range(6)], axis=1)
    col3[...] = mm(pick[:, :768], every, NT).astype(bf16)
    copies = [send(col3, col3_in.at[0], shifted(0, 1, 0)), send(col3, col3_in.at[1], shifted(0, -1, 0))]

    copies2 = sum_core(copies2)
    inner = mm(errs[...].reshape(1536, 128), t["shift2"][...])
    arrive(copies)
    rows = [kept(has_below, col3_in[0]), kept(has_above, col3_in[1])]
    edge = mm(jnp.concatenate(rows, axis=0), t["put3"][...], TN)
    for wp in range(4):
        for dp in range(6):
            number = wp * 6 + dp
            for k in range(3):
                piece = inner[number * 64:number * 64 + 64, 128 * k:128 * k + 128]
                if k != 1:
                    lane = dp * 256 + 64 * k
                    piece = piece + edge[wp * 64:wp * 64 + 64, lane:lane + 128]
                fs[number, (2 - k) * 64:(2 - k) * 64 + 64, :] = piece.astype(bf16)

    def cols3(dq):
        return jnp.concatenate([fs[wp * 6 + dq + 2 - j] for wp in range(4) for j in range(3)], axis=0)

    for dq in (0, 2):
        pe = mm(turned[...], jnp.concatenate([cols3(dq), cols3(dq + 1)], axis=1)).astype(bf16)
        both = mm(jnp.concatenate([pe[:, :128], pe[:, 128:]], axis=0), t["twice"][...]) * 0.125
        for n in range(2):
            for w in range(2):
                rows = both[64 * n + 32 * w:64 * n + 32 * w + 32]
                perr[w, dq + n] = rows[:, :128]
                perr[w, dq + n + 4] = rows[:, 128:]

    grad1 = None
    for pd in range(8):
        here = jnp.concatenate([perr[w // 2, pd] for w in range(4)], axis=0)
        err = (jnp.concatenate([here, here], axis=1) * slope(pre1[pd])).astype(bf16)
        piece = mm(err, cols1(pd), NT)
        grad1 = piece if grad1 is None else grad1 + piece
    grad1 = sum(grad1[32 * w:32 * w + 32, 48 * w:48 * w + 144] for w in range(4))
    one[...] = sum(mm(piece, t["narrow"][...]) for piece in split3(grad1))
    copies1 = send(part(one, 1 - core, 16), one_core, sibling)
    drain(NP + 1)
    copies1.wait_recv()
    copies1 = everyone(
        part(one, core, 16)[...] + one_core[...], one_plane, plane, [plane_peer(step)[1] for step in plane_steps]
    )
    copies2 = sum_plane(copies2)
    drain(NP + NZ)
    copies1 = everyone(summed_slots(copies1, one_plane), one_z, zc, [z_peer(r) for r in z_steps])
    copies2 = sum_z(copies2)
    drain(NP)
    copy2 = gather_core(copies2)
    drain(1)
    one_half[...] = part(base1, core, 16)[...] - learn_rate * summed_slots(copies1, one_z)
    far = part(one_out, core, 16)
    copy1 = send(one_half, far, sibling)
    put_out(one_half, far)
    copy2.wait_recv()
    copy1.wait_recv()

    drain(0)
    for out in outs:
        out.wait()


def hand_on(*refs):
    ins, outs, spots, results, in_sems, out_sems = refs[:3], refs[3:8], refs[8:11], refs[11:15], refs[15], refs[16]
    reads = [pltpu.make_async_copy(ins[n], spots[n], in_sems.at[n]) for n in range(3)]
    feat, one, total = spots
    step1, off1, step2, off2 = results
    writes = [pltpu.make_async_copy(a, b, out_sems.at[n]) for n, (a, b) in enumerate(zip((feat,) + results, outs))]
    for n in (2, 1, 0):
        reads[n].start()
    reads[2].wait()
    for l in range(6):
        step2[:, 128 * l:128 * l + 128] = total[64 * l:64 * l + 64]
    step2[:, 768:864] = total[384:448, 0:96]
    writes[3].start()
    reads[1].wait()
    step1[...] = one[:, 0:108]
    writes[1].start()
    reads[0].wait()
    writes[0].start()
    off1[...] = column_to_row(one[:, 108:109])
    off2[...] = column_to_row(total[384:448, 96:97])
    writes[2].start()
    writes[4].start()
    for copy in writes:
        copy.wait()


def shards(volume, first_filters, first_bias, second_filters, second_bias, cotangent):
    GX, GY, GZ = lax.axis_size("gx"), lax.axis_size("gy"), lax.axis_size("gz")
    NX = 4 if GZ >= 8 else 2
    NZ = (GX // 2) * (GZ // NX)
    NP = NX * GY
    n3 = 256 // NP
    operands = [
        volume, first_filters, first_bias.reshape(1, 32), second_filters, second_bias.reshape(1, 64),
        cotangent.transpose(1, 2, 3, 0).reshape(128, 64), jnp.asarray(PACKED),
    ]
    sems = 68 + 4 + 3 * (NP - 1) + 2 * (NZ - 1)
    V = pltpu.VMEM
    results = (
        jax.ShapeDtypeStruct((128, 64), bf16),
        jax.ShapeDtypeStruct((32, 108), f32),
        jax.ShapeDtypeStruct((1, 32), f32),
        jax.ShapeDtypeStruct((64, 864), f32),
        jax.ShapeDtypeStruct((1, 64), f32),
    )
    sums = (
        results[0],
        jax.ShapeDtypeStruct((32, 128), f32),
        jax.ShapeDtypeStruct((512, 128), f32),
    )
    out = pl.pallas_call(
        functools.partial(kernel, (GX, GY, GZ, NX)),
        out_shape=sums,
        in_specs=[pl.BlockSpec(memory_space=pltpu.HBM)] * len(operands),
        out_specs=[pl.BlockSpec(memory_space=pltpu.HBM)] * 3,
        scratch_shapes=[
            V((32, 128), bf16), V((2, 4, 16, 128), bf16), V((2, 16, 128), bf16), V((4, 16, 128), bf16),
            V((16, 128), bf16), V((2, 3, 3, 16, 128), bf16), V((64, 2, 16, 128), bf16), V((8, 128, 256), f32),
            V((2, 128, 64), bf16), V((2, 32, 64), bf16), V((4, 32, 64), bf16),
            V((2, 4, 32, 128), bf16), V((2, 2, 32, 128), bf16), V((2, 2, 4, 32, 128), bf16),
            V((2, 2, 32, 128), bf16), V((4, 2, 32, 128), bf16), V((48, 32, 128), bf16),
            V((16, 128), bf16), V((2, 3, 3, 16, 128), bf16), V((48, 96, 128), bf16),
            V((4, 6, 64, 128), bf16), V((32, 256), bf16), V((2, 32, 256), bf16), V((24, 192, 128), bf16),
            V((64, 2304), bf16), V((2, 8, 32, 128), f32),
            V((512, 128), f32), V((256, 128), f32), V((256, 128), f32), V((NP - 1, n3, 128), f32),
            V((NZ, n3, 128), f32),
            V((512, 128), f32),
            V((32, 128), f32), V((16, 128), f32), V((NP, 16, 128), f32),
            V((NZ, 16, 128), f32), V((16, 128), f32),
            pltpu.SemaphoreType.DMA((sems,)), pltpu.SemaphoreType.DMA((sems,)),
        ] + [V(a.shape, a.dtype) for a in operands] + [
            pltpu.SemaphoreType.DMA((len(operands),)),
            V((128, 64), bf16), V((32, 128), f32), V((512, 128), f32), pltpu.SemaphoreType.DMA((3,)),
        ],
        compiler_params=pltpu.CompilerParams(
            collective_id=0, has_side_effects=True, vmem_limit_bytes=62 * 2**20
        ),
    )(*operands)
    out = pl.pallas_call(
        hand_on,
        out_shape=results,
        in_specs=[pl.BlockSpec(memory_space=pltpu.HBM)] * 3,
        out_specs=[pl.BlockSpec(memory_space=pltpu.HBM)] * 5,
        scratch_shapes=[V(a.shape, a.dtype) for a in sums + results[1:]]
        + [pltpu.SemaphoreType.DMA((3,)), pltpu.SemaphoreType.DMA((5,))],
        compiler_params=pltpu.CompilerParams(vmem_limit_bytes=62 * 2**20),
    )(*out)
    features, stepped_first, offset_first, stepped_second, offset_second = out
    return (
        features.reshape(1, 4, 32, 64).transpose(3, 0, 1, 2), stepped_first, offset_first.reshape(32), stepped_second,
        offset_second.reshape(64),
    )


def solution(mesh):
    return jax.shard_map(
        shards,
        mesh=mesh,
        in_specs=(P(None, "gx", "gz", "gy"), P(), P(), P(), P(), P(None, "gx", "gz", "gy")),
        out_specs=(P(None, "gx", "gz", "gy"), P(), P(), P(), P()),
        check_vma=False,
    )
```

```python
import functools

import jax
import jax.numpy as jnp
import numpy as np
from jax import lax
from jax.experimental import pallas as pl
from jax.experimental.pallas import tpu as pltpu
from jax.sharding import PartitionSpec as P

slope_below = 0.3
learn_rate = 0.001
f32 = jnp.float32
bf16 = jnp.bfloat16
MESH = pl.DeviceIdType.MESH
NN = (((1,), (0,)), ((), ()))
NT = (((1,), (1,)), ((), ()))
TN = (((0,), (0,)), ((), ()))


def mm(a, b, dims=NN):
    return lax.dot_general(a, b, dims, preferred_element_type=f32)


def tables():
    place = np.zeros((512, 480))
    for wp in range(6):
        for dp in range(18):
            for ch in range(4):
                w, d = wp - 1, dp - 1
                inner_w, inner_d = 0 <= w < 4, 0 <= d < 16
                if inner_w and inner_d:
                    src = (ch * 4 + w) * 16 + d
                elif inner_d:
                    src = 256 + (64 if w > 0 else 0) + ch * 16 + d
                elif inner_w:
                    src = 384 + (16 if d > 0 else 0) + ch * 4 + w
                else:
                    a, b = int(w > 0), int(d > 0)
                    src = 416 + (a * 2 + b) * 16 + ch * 4 + (0 if a else 3)
                place[(wp * 18 + dp) * 4 + ch, src] = 1
    shift1 = np.zeros((128, 384))
    for l in range(128):
        if l:
            shift1[l - 1, l] = 1
        shift1[l, 128 + l] = 1
        if l < 127:
            shift1[l + 1, 256 + l] = 1
    order1 = np.zeros((1152, 128))
    for wp in range(6):
        for dp in range(18):
            a, b = (wp > 0) + (wp > 4), (dp > 0) + (dp > 16)
            w, d = (3, wp - 1, 0)[a], (15, dp - 1, 0)[b]
            order1[(a * 3 + b) * 128 + w * 16 + d, wp * 18 + dp] = 1
    four = np.zeros((128, 512))
    for q in range(512):
        four[q // 4, q] = 1
    put1 = np.zeros((32, 256))
    for ch in range(4):
        put1[ch * 2 + 1, 0] = put1[16 + ch * 2, 255] = 1
    shift2 = np.zeros((128, 384))
    swapped = np.zeros((128, 384))
    for l in range(128):
        for k in range(3):
            s = l % 64 + k - 1
            if 0 <= s < 64:
                s += l - l % 64
                shift2[s, k * 128 + l] = 1
                swapped[(s + 64) % 128, k * 128 + l] = 1
    ends = (0, 63, 64, 127)
    pick2 = np.zeros((16, 512))
    for dq in range(4):
        for n, l in enumerate(ends):
            pick2[dq * 4 + n, dq * 128 + l] = 1
    put2 = np.zeros((96, 2048))
    for dq in range(-2, 6):
        for half in range(2):
            d = dq + 4 * half
            dz = (d >= 0) + (d > 7)
            there, row = (d % 8) // 4, (d % 4) * 4
            put2[dz * 16 + row + 2 * there + 1, (dq + 2) * 256 + 64 * half] = 1
            put2[48 + dz * 16 + row + 2 * there, (dq + 2) * 256 + 128 + 64 * half + 63] = 1
    pick3 = np.zeros((32, 768))
    put3 = np.zeros((64, 1536))
    for dq in range(6):
        for n, l in enumerate(ends):
            pick3[dq * 4 + n, dq * 128 + l] = 1
        for half in range(2):
            put3[dq * 4 + 2 * half + 1, dq * 256 + 64 * half] = 1
            put3[32 + dq * 4 + 2 * half, dq * 256 + 128 + 64 * half + 63] = 1
    even = np.zeros((256, 128))
    for half in range(2):
        for h in range(64):
            even[half * 128 + 2 * h, half * 64 + h] = 1
    twice = np.zeros((128, 256))
    for half in range(2):
        for h in range(128):
            twice[half * 64 + h // 2, half * 128 + h] = 1
    spread = np.zeros((192, 512))
    for dc in range(-1, 5):
        for hc in range(32):
            row = (128 if dc < 0 else 160 if dc > 3 else dc * 32) + hc
            for t in range(2):
                for half in range(2):
                    kind = {0: 0, 1: 1, -1: 2, 2: 3}.get(dc - 2 * half)
                    if kind is not None:
                        spread[row, kind * 128 + half * 64 + 2 * hc + t] = 1
    collect = np.zeros((256, 128))
    for dc in range(4):
        for hc in range(32):
            collect[(dc % 2) * 128 + dc * 32 + hc, (dc // 2) * 64 + 2 * hc] = 1
    widen = np.zeros((108, 1536))
    narrow = np.zeros((144, 128))
    for q in range(108):
        for w in range(4):
            widen[q, w * 384 + w * 48 + (q // 12) * 16 + q % 12] = 1
        narrow[(q // 12) * 16 + q % 12, q] = 1
    narrow[12, 108] = 1
    ident = np.zeros((64, 256))
    for o in range(64):
        ident[o, o] = ident[o, 128 + 64 + o] = 1
    every = dict(
        place=place, shift1=shift1, order1=order1, four=four, put1=put1, shift2=shift2, swapped=swapped,
        pick2=pick2, put2=put2, pick3=pick3, put3=put3, even=even, twice=twice, spread=spread, collect=collect,
        widen=widen, narrow=narrow, ident=ident,
    )
    return every


TABLE = {}


def packed_table():
    parts, row = [], 0
    for name, value in tables().items():
        rows, lanes = value.shape
        if name == "order1":
            value = np.concatenate(np.split(value, 4), axis=1)
            rows //= 4
        wide = np.zeros((-(-rows // 16) * 16, -(-lanes // 512) * 512))
        wide[:rows, :value.shape[1]] = value
        wide = np.concatenate(np.split(wide, wide.shape[1] // 512, axis=1))
        TABLE[name] = (row, rows, lanes)
        row += wide.shape[0]
        parts.append(wide)
    return np.concatenate(parts).astype(jnp.bfloat16)


PACKED = packed_table()


class Rows:
    def __init__(self, ref, name):
        self.ref = ref
        self.row, self.rows, self.lanes = TABLE[name]

    def folded(self):
        return jnp.concatenate(
            [self.ref[self.row:self.row + self.rows, 128 * n:128 * n + 128] for n in range(4)], axis=0
        )

    def __getitem__(self, key):
        if self.lanes > 512:
            step = -(-self.rows // 16) * 16
            return jnp.concatenate(
                [self.ref[self.row + n * step:self.row + n * step + self.rows, :] for n in range(-(-self.lanes // 512))],
                axis=1,
            )
        if key is Ellipsis:
            return self.ref[self.row:self.row + self.rows, :self.lanes]
        return self.ref[self.row + key.start:self.row + key.stop, :self.lanes]


def row_to_column(row):
    n = row.shape[1]
    diagonal = lax.broadcasted_iota(jnp.int32, (n, n), 0) == lax.broadcasted_iota(jnp.int32, (n, n), 1)
    return jnp.sum(jnp.where(diagonal, jnp.broadcast_to(row, (n, n)), 0.0), axis=1, keepdims=True)


def column_to_row(column):
    n = column.shape[0]
    diagonal = lax.broadcasted_iota(jnp.int32, (n, n), 0) == lax.broadcasted_iota(jnp.int32, (n, n), 1)
    return jnp.sum(jnp.where(diagonal, jnp.broadcast_to(column, (n, n)), 0.0), axis=0, keepdims=True)


def kept(flag, value):
    return lax.select(flag, value, jnp.zeros_like(value))


def leaky(a):
    return jnp.where(a > 0, a, slope_below * a)


def slope(a):
    return jnp.where(a > 0, 1.0, slope_below)


def split3(a):
    high = a.astype(bf16)
    rest = a - high.astype(f32)
    mid = rest.astype(bf16)
    return high, mid, (rest - mid.astype(f32)).astype(bf16)


def kernel(sizes, *refs):
    GX, GY, GZ, NX = sizes
    ZL = GZ // NX
    ZH = GX // 2
    NZ = ZH * ZL
    far = refs[:7]
    refs = refs[7:]
    feat_out, one_out, total_out = refs[:3]
    (
        edges, wide_in, deep_in, corner_in, col1, col1_in, xs, pre1,
        wide_t, deep_t, corner_t, pooled, packs, wide2, deep2, corner2, v2, col2, col2_in, ys,
        errs, col3, col3_in, fs, turned, perr,
        grads, core_in, red1, plane_in, z_in, total,
        one, one_core, one_plane, one_z, one_half, send_sems, recv_sems, vol, filt1, bias1, filt2, bias2, cot, packed, in_sems,
        feat, base1, base2, out_sems,
    ) = refs[3:]
    near = (vol, filt1, bias1, filt2, bias2, cot, packed)
    fetches = [pltpu.make_async_copy(a, b, in_sems.at[n]) for n, (a, b) in enumerate(zip(far, near))]
    for fetch in fetches:
        fetch.start()
    t = {name: Rows(packed, name) for name in TABLE}

    gx, gy, gz = lax.axis_index("gx"), lax.axis_index("gy"), lax.axis_index("gz")
    core, zh = lax.rem(gx, 2), lax.div(gx, 2)
    xc, zl = lax.rem(gz, NX), lax.div(gz, NX)
    zc = zh * ZL + zl

    def shifted(dx, dy, dz):
        return (lax.rem(gx + (dx + GX), GX), lax.rem(gy + (dy + GY), GY), lax.rem(gz + (dz + GZ), GZ))

    sibling = (gx + 1 - 2 * core, gy, gz)

    plane = xc * GY + gy
    NP = NX * GY

    def ring_gap(n, r):
        return min(r, n - r)

    plane_steps = [(rx, ry) for rx in range(NX) for ry in range(GY) if rx or ry]
    plane_steps.sort(key=lambda step: -ring_gap(NX, step[0]) - ring_gap(GY, step[1]))
    z_steps = sorted(range(1, NZ), key=lambda r: -ring_gap(NZ, r))

    def plane_peer(step):
        px, py = lax.rem(xc + step[0], NX), lax.rem(gy + step[1], GY)
        return px * GY + py, (gx, py, zl * NX + px)

    def z_peer(r):
        p = lax.rem(zc + r, NZ)
        return (2 * lax.div(p, ZL) + core, gy, lax.rem(p, ZL) * NX + xc)

    square = [(dx, dz) for dx in (-1, 1, 0) for dz in (-1, 1, 0)]
    square.sort(key=lambda step: -abs(step[0]) - abs(step[1]))
    peers = [shifted(dx, dy, dz) for dx, dz in square for dy in (-1, 1)]
    peers += [shifted(dx, 0, dz) for dx, dz in square if (dx, dz) != (0, 0)]
    peers += [plane_peer(step)[1] for step in plane_steps]
    peers += [z_peer(r) for r in z_steps]
    barrier = pltpu.get_barrier_semaphore()
    for peer in peers:
        pl.semaphore_signal(barrier, inc=1, device_id=peer, device_id_type=MESH)

    count = [0]
    started = []

    def send(src, dst, device):
        n = count[0]
        count[0] += 1
        copy = pltpu.make_async_remote_copy(
            src_ref=src, dst_ref=dst, send_sem=send_sems.at[n], recv_sem=recv_sems.at[n],
            device_id=device, device_id_type=MESH,
        )
        copy.start()
        started.append(copy)
        return copy

    def drain(keep):
        while len(started) > keep:
            started.pop(0).wait_send()

    outs = []

    def put_out(src, dst):
        copy = pltpu.make_async_copy(src, dst, out_sems.at[len(outs)])
        copy.start()
        outs.append(copy)

    def arrive(copies):
        for copy in copies:
            copy.wait_recv()

    row = lax.broadcasted_iota(jnp.int32, (32, 256), 0)
    column = lax.broadcasted_iota(jnp.int32, (32, 256), 1)
    wanted = jnp.where(row < 16, row * 16, row * 16 - 241)
    edge = jnp.where(column == wanted, 1.0, 0.0).astype(bf16)
    fetches[0].wait()
    block = vol[...].reshape(256, 128)
    edges[...] = mm(edge, block).astype(bf16)
    pl.semaphore_wait(barrier, len(peers))

    has_left, has_right = gx > 0, gx < GX - 1
    has_front, has_back = gz > 0, gz < GZ - 1
    has_below, has_above = gy > 0, gy < GY - 1

    def send_ring(wide_src, wide_dst, deep_src, deep_dst, corner_src, corner_dst):
        copies = []
        for a in range(2):
            dx = 1 if a == 0 else -1
            copies.append(send(wide_src(a), wide_dst.at[a], shifted(dx, 0, 0)))
        for b in range(2):
            dz = 1 if b == 0 else -1
            copies.append(send(deep_src(b), deep_dst.at[b], shifted(0, 0, dz)))
        for a in range(2):
            for b in range(2):
                copies.append(
                    send(corner_src(a, b), corner_dst.at[a * 2 + b], shifted(1 if a == 0 else -1, 0, 1 if b == 0 else -1))
                )
        return copies

    def send_columns(src, dst):
        copies = []
        for dx, dz in square:
            for side in range(2):
                dy = 1 if side == 0 else -1
                copies.append(send(src, dst.at[side, 1 - dx, 1 - dz], shifted(dx, dy, dz)))
        return copies

    def columns_in(dst, dx):
        rows = []
        for side in range(2):
            for dz in (-1, 0, 1):
                flag = (has_below, has_above)[side]
                if dx:
                    flag = jnp.logical_and(flag, edge_flags[(dx + 1) // 2])
                if dz:
                    flag = jnp.logical_and(flag, deep_flags[(dz + 1) // 2])
                rows.append(kept(flag, dst[side, dx + 1, dz + 1]))
        return rows

    edge_flags = (has_left, has_right)
    deep_flags = (has_front, has_back)

    def edge_rows(b):
        return edges.at[pl.ds(16, 16)] if b == 0 else edges.at[pl.ds(0, 16)]

    copies = send_ring(
        lambda a: vol.at[:, 3] if a == 0 else vol.at[:, 0], wide_in,
        edge_rows, deep_in, lambda a, b: edge_rows(b), corner_in,
    )

    row = lax.broadcasted_iota(jnp.int32, (16, 512), 0)
    column = lax.broadcasted_iota(jnp.int32, (16, 512), 1)
    wanted = jnp.where(row < 8, lax.div(row, 2) * 128 + lax.rem(row, 2) * 127, -1)
    pick1 = jnp.where(column == wanted, 1.0, 0.0).astype(bf16)
    ends = sum(
        mm(pick1[:, 128 * ch:128 * ch + 128], vol[ch].reshape(64, 128), NT) for ch in range(4)
    )
    col1[...] = jnp.concatenate([ends, jnp.zeros((16, 64), f32)], axis=1).astype(bf16)
    copies_c = send_columns(col1, col1_in)
    for fetch in fetches[1:]:
        fetch.wait()
    first_half = filt1[...].astype(bf16)
    base1[...] = jnp.concatenate([filt1[...], row_to_column(bias1[...]), jnp.zeros((32, 19), f32)], axis=1)
    for l in range(6):
        base2[64 * l:64 * l + 64] = filt2[:, 128 * l:128 * l + 128]
    base2[384:448] = jnp.concatenate(
        [filt2[:, 768:864], jnp.broadcast_to(row_to_column(bias2[...]), (64, 32))], axis=1
    )
    base2[448:512] = jnp.zeros((64, 128), f32)
    wide_first = mm(first_half, t["widen"][...]).astype(bf16)
    wide_first = jnp.concatenate([wide_first[:, 384 * w:384 * w + 288] for w in range(4)], axis=0)
    bias1_col = row_to_column(bias1[...])
    bias1_col = jnp.concatenate([bias1_col] * 4, axis=0)
    bias2_col = row_to_column(bias2[...])
    second_half = filt2[...].astype(bf16)

    copies_t = send_ring(
        lambda a: cot, wide_t, lambda b: cot.at[96:128] if b == 0 else cot.at[0:32], deep_t,
        lambda a, b: cot.at[96:128] if b == 0 else cot.at[0:32], corner_t,
    )

    turn = mm(second_half, t["ident"][...], TN).astype(bf16)
    for w in range(2):
        for m in range(18):
            pair = []
            for high in range(2):
                wp, rest = divmod(2 * m + high, 9)
                i = w + 2 - wp
                if 0 <= i <= 2:
                    tap = 9 * i + rest
                    pair.append(turn[32 * tap:32 * tap + 32, 128 * high:128 * high + 128].astype(f32))
            value = sum(pair) if pair else jnp.zeros((32, 128), f32)
            turned[32 * w:32 * w + 32, 128 * m:128 * m + 128] = value.astype(bf16)

    arrive(copies)
    pieces = [block]
    for a in range(2):
        pieces.append(kept(edge_flags[a], wide_in[a]).reshape(64, 128))
    for b in range(2):
        pieces.append(kept(deep_flags[b], deep_in[b]))
    for a in range(2):
        for b in range(2):
            pieces.append(kept(jnp.logical_and(edge_flags[a], deep_flags[b]), corner_in[a * 2 + b]))
    rows = mm(t["place"][...], jnp.concatenate(pieces, axis=0)).astype(bf16)
    inner = mm(rows, t["shift1"][...])
    arrive(copies_c)
    columns = [columns_in(col1_in, dx) for dx in (-1, 0, 1)]
    sides = [
        jnp.concatenate([columns[a][side * 3 + b] for a in range(3) for b in range(3)], axis=1)
        for side in range(2)
    ]
    ordered = mm(jnp.concatenate(sides, axis=0), t["order1"].folded()).astype(bf16)
    ordered = mm(ordered, t["four"][...])
    row = lax.broadcasted_iota(jnp.int32, (32, 512), 0)
    column = lax.broadcasted_iota(jnp.int32, (32, 512), 1)
    same = lax.rem(lax.div(row, 2), 8) == lax.rem(column, 4)
    ordered = jnp.where(same, ordered, 0.0).astype(bf16)
    ends = mm(ordered, t["put1"][...], TN)
    full = [inner[:, :128] + ends[:, :128], inner[:, 128:256], inner[:, 256:] + ends[:, 128:]]
    third = [piece.reshape(64, 8, 128) for piece in full]
    rolled = [pltpu.roll(piece, 4, axis=1) for piece in third]
    sub = lax.broadcasted_iota(jnp.int32, (64, 8, 128), 1)
    upper = sub < 4
    ones = jnp.where(sub == 4, 1.0, 0.0)
    even_tile = jnp.concatenate(
        [jnp.where(upper, third[0], rolled[1]), jnp.where(upper, third[2], ones)], axis=1
    )
    odd_tile = jnp.concatenate(
        [jnp.where(upper, rolled[0], third[1]), jnp.where(upper, rolled[2], ones)], axis=1
    )
    xs[:, 0] = even_tile.astype(bf16)
    xs[:, 1] = odd_tile.astype(bf16)

    def cols1(half_d):
        sides = []
        for e in range(2):
            tiles = [xs[wp * 9 + half_d + (j + e) // 2, (j + e) % 2] for wp in range(6) for j in range(3)]
            sides.append(jnp.concatenate(tiles, axis=0))
        return jnp.concatenate(sides, axis=1)

    def turned_half(a):
        return pltpu.roll(a.astype(f32), 64, axis=1)

    low = lax.broadcasted_iota(jnp.int32, (32, 128), 1) < 64

    def halves(a, b):
        return jnp.where(low, a.astype(f32), b.astype(f32)).astype(bf16)

    copies = []
    for dq in range(4):
        sums = [[None, None], [None, None]]
        for half in range(2):
            pd = dq + 4 * half
            pre = mm(wide_first, cols1(pd)) + bias1_col
            pre1[pd] = pre
            act = leaky(pre)
            act = act[:, :128] + act[:, 128:]
            for pw in range(2):
                both = act[64 * pw:64 * pw + 32] + act[64 * pw + 32:64 * pw + 64]
                sums[pw][half] = ((both + pltpu.roll(both, 127, axis=1)) * 0.125).astype(bf16)
        lanes = [jnp.concatenate([sums[0][half], sums[1][half]], axis=0) for half in range(2)]
        value = (mm(lanes[0], t["even"][0:128]) + mm(lanes[1], t["even"][128:256])).astype(bf16)
        pooled[:, dq] = value.reshape(2, 32, 128)
        for a in range(2):
            copies.append(send(pooled.at[:, dq], wide2.at[a, :, dq], shifted(1 - 2 * a, 0, 0)))
        if dq % 2:
            b = 0 if dq == 3 else 1
            for w in range(2):
                if b == 0:
                    packs[0, w] = halves(turned_half(pooled[w, 2]), pooled[w, 3])
                else:
                    packs[1, w] = halves(pooled[w, 0], turned_half(pooled[w, 1]))
            copies.append(send(packs.at[b], deep2.at[b], shifted(0, 0, 1 - 2 * b)))
            for a in range(2):
                copies.append(send(packs.at[b], corner2.at[a * 2 + b], shifted(1 - 2 * a, 0, 1 - 2 * b)))
    pick = t["pick2"][...]
    ends = sum(
        mm(pick[:, 128 * dq:128 * dq + 128], pooled[:, dq].reshape(64, 128), NT) for dq in range(4)
    )
    col2[...] = jnp.concatenate([ends, jnp.zeros((16, 64), f32)], axis=1).astype(bf16)
    copies_c = send_columns(col2, col2_in)

    arrive(copies_t)
    spread_cot = []
    for dx in (-1, 0, 1):
        a = max(dx, 0)
        beside = edge_flags[a]
        if dx:
            rows = [kept(beside, wide_t[a])]
            rows += [kept(jnp.logical_and(beside, deep_flags[b]), corner_t[a * 2 + b]) for b in range(2)]
        else:
            rows = [cot[...]] + [kept(deep_flags[b], deep_t[b]) for b in range(2)]
        spread_cot.append(mm(jnp.concatenate(rows, axis=0), t["spread"][...], TN) * 0.125)

    arrive(copies)
    for wp in range(6):
        a, w = wp // 4, wp % 2
        if wp in (2, 3):
            near = [pooled[w, dq] for dq in range(4)]
            front, back = (kept(deep_flags[b], deep2[b, w]) for b in range(2))
        else:
            near = [kept(edge_flags[a], wide2[a, w, dq]) for dq in range(4)]
            front, back = (
                kept(jnp.logical_and(edge_flags[a], deep_flags[b]), corner2[a * 2 + b, w]) for b in range(2)
            )
        for dq in range(4):
            v2[wp * 6 + dq] = near[dq]
        v2[wp * 6 + 4] = halves(front, turned_half(near[2]))
        v2[wp * 6 + 5] = halves(turned_half(near[1]), back)
        v2[36 + wp] = halves(near[3], front)
        v2[42 + wp] = halves(back, near[0])
    inner = jnp.concatenate(
        [mm(v2[0:36].reshape(1152, 128), t["shift2"][...]), mm(v2[36:48].reshape(384, 128), t["swapped"][...])],
        axis=0,
    )
    arrive(copies_c)
    put = t["put2"][...]
    edge = [mm(jnp.concatenate(columns_in(col2_in, dx), axis=0), put, TN) for dx in (-1, 0, 1)]
    for wp in range(6):
        for dp in range(8):
            number = {0: wp * 6 + 4, 1: 36 + wp, 6: 42 + wp, 7: wp * 6 + 5}.get(dp, wp * 6 + dp - 2)
            for k in range(3):
                piece = inner[number * 32:number * 32 + 32, 128 * k:128 * k + 128]
                if k != 1:
                    lane = dp * 256 + 64 * k
                    piece = piece + edge[wp // 2][(wp % 2) * 32:(wp % 2) * 32 + 32, lane:lane + 128]
                ys[wp * 8 + dp, k * 32:k * 32 + 32, :] = piece.astype(bf16)

    def cols2(w, dq, extra):
        taps = [ys[(w + i) * 8 + dq + j] for i in range(3) for j in range(3)]
        return jnp.concatenate(taps + extra, axis=0)

    feat_sum = [None, None]

    def errors(dqs, pairs):
        for dq in dqs:
            kind = {0: 2, 5: 3}.get(dq, (dq - 1) // 2)
            for pair in pairs:
                errors_of(dq, kind, pair)

    def errors_of(dq, kind, pair):
        cols = jnp.concatenate([cols2(w, dq, []) for w in pair], axis=1)
        pre = mm(second_half, cols) + bias2_col
        if pair == (1, 2) and 0 < dq < 5:
            act = leaky(pre)
            act = act[:, :128] + act[:, 128:]
            feat_sum[kind] = act if feat_sum[kind] is None else feat_sum[kind] + act
        for n, w in enumerate(pair):
            here = spread_cot[(w + 1) // 2][:, 128 * kind:128 * kind + 128]
            errs[w, dq] = (here * slope(pre[:, 128 * n:128 * n + 128])).astype(bf16)

    def second_half_grads():
        ends = [
            ((both + pltpu.roll(both, 127, axis=1)) * 0.125).astype(bf16) for both in feat_sum
        ]
        feat[...] = (mm(t["collect"][0:128], ends[0], NT) + mm(t["collect"][128:256], ends[1], NT)).astype(bf16)
        ones_rows = [jnp.ones((32, 128), bf16)]
        grad2 = None
        for dq in range(4):
            cols = jnp.concatenate([cols2(w, dq + 1, ones_rows) for w in (1, 2)], axis=1)
            err = jnp.concatenate([errs[w, dq + 1] for w in (1, 2)], axis=1)
            piece = mm(err, cols, NT)
            grad2 = piece if grad2 is None else grad2 + piece
        for l in range(7):
            grads[l * 64:l * 64 + 64] = grad2[:, 128 * l:128 * l + 128]
        grads[448:512] = jnp.zeros((64, 128), f32)
        put_out(feat, feat_out)
        return send(part(grads, 1 - core, n1), core_in, sibling)

    def part(ref, index, size):
        return ref.at[pl.ds(pl.multiple_of(index * size, size), size)]

    n1, n3 = 256, 256 // NP

    def sum_core(copy):
        copy.wait_recv()
        red1[...] = part(grads, core, n1)[...] + core_in[...]
        copies = []
        for n, step in enumerate(plane_steps):
            p, device = plane_peer(step)
            copies.append(send(part(red1, p, n3), plane_in.at[n], device))
        return copies

    def sum_plane(copies):
        arrive(copies)
        acc = part(red1, plane, n3)[...]
        for r in range(1, NP):
            acc = acc + plane_in[r - 1]
        z_in[zc] = acc
        return [send(z_in.at[zc], z_in.at[zc], z_peer(r)) for r in z_steps]

    def sum_z(copies):
        arrive(copies)
        acc = z_in[0]
        for r in range(1, NZ):
            acc = acc + z_in[r]
        mine = part(total, core * NP + plane, n3)
        mine[...] = part(base2, core * NP + plane, n3)[...] - learn_rate * acc
        return [send(mine, mine, plane_peer(step)[1]) for step in plane_steps]

    def forward(p):
        row = core * NP + p
        return send(part(total, row, n3), part(total_out, row, n3), sibling)

    def gather_core(copies):
        copies_on = [forward(plane)]
        for copy, step in reversed(list(zip(copies, plane_steps))):
            copy.wait_recv()
            px, py = lax.rem(xc + NX - step[0], NX), lax.rem(gy + GY - step[1], GY)
            copies_on.append(forward(px * GY + py))
        put_out(part(total, core, n1), part(total_out, core, n1))
        return copies_on

    def everyone(value, slots, index, devices):
        slots[index] = value
        return [send(slots.at[index], slots.at[index], device) for device in devices]

    def summed_slots(copies, slots):
        arrive(copies)
        acc = slots[0]
        for n in range(1, slots.shape[0]):
            acc = acc + slots[n]
        return acc

    errors(range(0, 6), [(1, 2), (0, 3)])
    pick = t["pick3"][...]
    col3[...] = sum(
        mm(pick[:, 128 * dq:128 * dq + 128], errs[:, dq].reshape(256, 128), NT) for dq in range(6)
    ).astype(bf16)
    copies = [send(col3, col3_in.at[0], shifted(0, 1, 0)), send(col3, col3_in.at[1], shifted(0, -1, 0))]

    copies2 = sum_core(second_half_grads())
    inner = mm(errs[...].reshape(1536, 128), t["shift2"][...])
    arrive(copies)
    rows = [kept(has_below, col3_in[0]), kept(has_above, col3_in[1])]
    edge = mm(jnp.concatenate(rows, axis=0), t["put3"][...], TN)
    for wp in range(4):
        for dp in range(6):
            number = wp * 6 + dp
            for k in range(3):
                piece = inner[number * 64:number * 64 + 64, 128 * k:128 * k + 128]
                if k != 1:
                    lane = dp * 256 + 64 * k
                    piece = piece + edge[wp * 64:wp * 64 + 64, lane:lane + 128]
                fs[number, (2 - k) * 64:(2 - k) * 64 + 64, :] = piece.astype(bf16)

    def cols3(dq):
        return jnp.concatenate([fs[wp * 6 + dq + 2 - j] for wp in range(4) for j in range(3)], axis=0)

    for dq in (0, 2):
        pe = mm(turned[...], jnp.concatenate([cols3(dq), cols3(dq + 1)], axis=1)).astype(bf16)
        both = mm(jnp.concatenate([pe[:, :128], pe[:, 128:]], axis=0), t["twice"][...]) * 0.125
        for n in range(2):
            for w in range(2):
                rows = both[64 * n + 32 * w:64 * n + 32 * w + 32]
                perr[w, dq + n] = rows[:, :128]
                perr[w, dq + n + 4] = rows[:, 128:]

    grad1 = None
    for pd in range(8):
        here = jnp.concatenate([perr[w // 2, pd] for w in range(4)], axis=0)
        err = (jnp.concatenate([here, here], axis=1) * slope(pre1[pd])).astype(bf16)
        piece = mm(err, cols1(pd), NT)
        grad1 = piece if grad1 is None else grad1 + piece
    grad1 = sum(grad1[32 * w:32 * w + 32, 48 * w:48 * w + 144] for w in range(4))
    one[...] = sum(mm(piece, t["narrow"][...]) for piece in split3(grad1))
    copies1 = send(part(one, 1 - core, 16), one_core, sibling)
    copies2 = sum_plane(copies2)
    drain(NP + NZ)
    copies1.wait_recv()
    copies1 = everyone(
        part(one, core, 16)[...] + one_core[...], one_plane, plane, [plane_peer(step)[1] for step in plane_steps]
    )
    drain(NP)
    copies2 = sum_z(copies2)
    copies1 = everyone(summed_slots(copies1, one_plane), one_z, zc, [z_peer(r) for r in z_steps])
    copies2 = gather_core(copies2)
    drain(NP)
    one_half[...] = part(base1, core, 16)[...] - learn_rate * summed_slots(copies1, one_z)
    far = part(one_out, core, 16)
    copy1 = send(one_half, far, sibling)
    put_out(one_half, far)
    arrive(copies2)
    copy1.wait_recv()

    drain(0)
    for out in outs:
        out.wait()


def hand_on(*refs):
    ins, outs, spots, results, in_sems, out_sems = refs[:3], refs[3:8], refs[8:11], refs[11:15], refs[15], refs[16]
    reads = [pltpu.make_async_copy(ins[n], spots[n], in_sems.at[n]) for n in range(3)]
    feat, one, total = spots
    step1, off1, step2, off2 = results
    writes = [pltpu.make_async_copy(a, b, out_sems.at[n]) for n, (a, b) in enumerate(zip((feat,) + results, outs))]
    for n in (2, 1, 0):
        reads[n].start()
    reads[2].wait()
    for l in range(6):
        step2[:, 128 * l:128 * l + 128] = total[64 * l:64 * l + 64]
    step2[:, 768:864] = total[384:448, 0:96]
    writes[3].start()
    reads[1].wait()
    step1[...] = one[:, 0:108]
    writes[1].start()
    reads[0].wait()
    writes[0].start()
    off1[...] = column_to_row(one[:, 108:109])
    off2[...] = column_to_row(total[384:448, 96:97])
    writes[2].start()
    writes[4].start()
    for copy in writes:
        copy.wait()


def shards(volume, first_filters, first_bias, second_filters, second_bias, cotangent):
    GX, GY, GZ = lax.axis_size("gx"), lax.axis_size("gy"), lax.axis_size("gz")
    NX = 4 if GZ >= 8 else 2
    NZ = (GX // 2) * (GZ // NX)
    NP = NX * GY
    n3 = 256 // NP
    operands = [
        volume, first_filters, first_bias.reshape(1, 32), second_filters, second_bias.reshape(1, 64),
        cotangent.transpose(1, 2, 3, 0).reshape(128, 64), jnp.asarray(PACKED),
    ]
    sems = 68 + 4 + 4 * (NP - 1) + 2 * (NZ - 1)
    V = pltpu.VMEM
    results = (
        jax.ShapeDtypeStruct((128, 64), bf16),
        jax.ShapeDtypeStruct((32, 108), f32),
        jax.ShapeDtypeStruct((1, 32), f32),
        jax.ShapeDtypeStruct((64, 864), f32),
        jax.ShapeDtypeStruct((1, 64), f32),
    )
    sums = (
        results[0],
        jax.ShapeDtypeStruct((32, 128), f32),
        jax.ShapeDtypeStruct((512, 128), f32),
    )
    out = pl.pallas_call(
        functools.partial(kernel, (GX, GY, GZ, NX)),
        out_shape=sums,
        in_specs=[pl.BlockSpec(memory_space=pltpu.HBM)] * len(operands),
        out_specs=[pl.BlockSpec(memory_space=pltpu.HBM)] * 3,
        scratch_shapes=[
            V((32, 128), bf16), V((2, 4, 16, 128), bf16), V((2, 16, 128), bf16), V((4, 16, 128), bf16),
            V((16, 128), bf16), V((2, 3, 3, 16, 128), bf16), V((64, 2, 16, 128), bf16), V((8, 128, 256), f32),
            V((2, 128, 64), bf16), V((2, 32, 64), bf16), V((4, 32, 64), bf16),
            V((2, 4, 32, 128), bf16), V((2, 2, 32, 128), bf16), V((2, 2, 4, 32, 128), bf16),
            V((2, 2, 32, 128), bf16), V((4, 2, 32, 128), bf16), V((48, 32, 128), bf16),
            V((16, 128), bf16), V((2, 3, 3, 16, 128), bf16), V((48, 96, 128), bf16),
            V((4, 6, 64, 128), bf16), V((32, 256), bf16), V((2, 32, 256), bf16), V((24, 192, 128), bf16),
            V((64, 2304), bf16), V((2, 8, 32, 128), f32),
            V((512, 128), f32), V((256, 128), f32), V((256, 128), f32), V((NP - 1, n3, 128), f32),
            V((NZ, n3, 128), f32),
            V((512, 128), f32),
            V((32, 128), f32), V((16, 128), f32), V((NP, 16, 128), f32),
            V((NZ, 16, 128), f32), V((16, 128), f32),
            pltpu.SemaphoreType.DMA((sems,)), pltpu.SemaphoreType.DMA((sems,)),
        ] + [V(a.shape, a.dtype) for a in operands] + [
            pltpu.SemaphoreType.DMA((len(operands),)),
            V((128, 64), bf16), V((32, 128), f32), V((512, 128), f32), pltpu.SemaphoreType.DMA((3,)),
        ],
        compiler_params=pltpu.CompilerParams(
            collective_id=0, has_side_effects=True, vmem_limit_bytes=62 * 2**20
        ),
    )(*operands)
    out = pl.pallas_call(
        hand_on,
        out_shape=results,
        in_specs=[pl.BlockSpec(memory_space=pltpu.HBM)] * 3,
        out_specs=[pl.BlockSpec(memory_space=pltpu.HBM)] * 5,
        scratch_shapes=[V(a.shape, a.dtype) for a in sums + results[1:]]
        + [pltpu.SemaphoreType.DMA((3,)), pltpu.SemaphoreType.DMA((5,))],
        compiler_params=pltpu.CompilerParams(vmem_limit_bytes=62 * 2**20),
    )(*out)
    features, stepped_first, offset_first, stepped_second, offset_second = out
    return (
        features.reshape(1, 4, 32, 64).transpose(3, 0, 1, 2), stepped_first, offset_first.reshape(32), stepped_second,
        offset_second.reshape(64),
    )


def solution(mesh):
    return jax.shard_map(
        shards,
        mesh=mesh,
        in_specs=(P(None, "gx", "gz", "gy"), P(), P(), P(), P(), P(None, "gx", "gz", "gy")),
        out_specs=(P(None, "gx", "gz", "gy"), P(), P(), P(), P()),
        check_vma=False,
    )
```
